32 devices in a mesh: cfg: 2 (over x), seq: 8 (over z, y), clip: 2 (over core).
Axes of the slice: x: 2, y: 2, z: 4, core: 2. Of those that a mesh axis runs over, the one named last changes fastest.
Arguments:
- clean: bfloat16 [128, 256, 1152], P(('clip', 'seq')), parts along dimension 0, may hold values from -6 to 6
- noise: bfloat16 [128, 256, 1152], P(('clip', 'seq')), parts along dimension 0, may hold values from -6 to 6
- timestep: float32 [2], P('clip'), parts along dimension 0, may hold values from 0.1 to 0.9
- guidance: float32 [2], P('clip'), parts along dimension 0, may hold values from 2 to 6
- condition_vector: bfloat16 [2304], P('clip'), parts along dimension 0, may hold values from -6 to 6
- empty_prompt_vector: bfloat16 [1152], replicated, may hold values from -6 to 6
- timestep_direction: bfloat16 [1152], replicated, may hold values from -6 to 6
- spatial_query_key_value: bfloat16 [3, 1152, 1152], P(None, None, ('cfg', 'seq')), may hold values from -1 to 1
- spatial_output_weight: bfloat16 [1152, 1152], P(('cfg', 'seq')), may hold values from -0.1875 to 0.1875
- temporal_query_key_value: bfloat16 [3, 1152, 1152], P(None, None, ('cfg', 'seq')), may hold values from -1 to 1
- temporal_output_weight: bfloat16 [1152, 1152], P(('cfg', 'seq')), may hold values from -0.1875 to 0.1875
- adapter_down_maps: bfloat16 [2, 1152, 64], replicated, may hold values from -0.1875 to 0.1875
- adapter_up_maps: bfloat16 [2, 64, 1152], replicated, may hold values from -0.75 to 0.75
Outputs:
- student_out: bfloat16 [128, 256, 1152], P(('clip', 'seq'), 'cfg'), parts along dimension 0
- student_tangent: bfloat16 [128, 256, 1152], P(('clip', 'seq'), 'cfg'), parts along dimension 0
The draws below stay inside these ranges and needn't reach their ends.
There are 2 independent parts, one for each index of `clip`. The reference program is written for one: setup_inputs(seed, part) draws one part's arguments, and reference() takes and returns one part's arrays. A program takes and returns all parts, laid end to end along the dimension named above; an argument that names none is the same for every part. Nothing has to cross between parts.
All inputs are finite; a program needn't handle non-finite values.
Results may differ from the reference program's by a relative error of at most 0.028.
Values may be sent and summed in bfloat16 or wider, within the bound.
No kernel may reach another device: no remote copies, remote signals or barrier semaphores. Data moves between devices by JAX's collectives and lax.ppermute only.
A program may use at most 128 MiB of HBM per device.

```python
import math
import jax
import jax.numpy as jnp
from jax import lax

MODEL_WIDTH = 1152
HEAD_DIM = 72
FRAMES = 64
POSITIONS = 256
ADAPTER_RANK = 64


def projection_draw(seed_key, salt):
    folded = jax.random.fold_in(seed_key, salt)
    first_key = jax.random.fold_in(folded, 0)
    gaussian = jax.random.normal(first_key, (3, MODEL_WIDTH, MODEL_WIDTH), jnp.float32) / math.sqrt(MODEL_WIDTH)
    return jnp.clip(gaussian, -1.0, 1.0).astype(jnp.bfloat16)


def draw_spatial_query_key_value(key, part):
    return projection_draw(key, 101)


def draw_temporal_query_key_value(key, part):
    return projection_draw(key, 202)


def shard_levels(key, dims, shards, smallest, largest):
    def one(dim, blocks):
        heights = jax.random.uniform(jax.random.fold_in(jax.random.fold_in(key, 6), dim), (blocks,), jnp.float32, smallest / len(shards), largest / len(shards))
        return jnp.repeat(jnp.exp(heights), dims[dim] // blocks).reshape((-1,) + (1,) * (len(dims) - dim - 1))

    level = one(*shards[0])
    for cut in shards[1:]:
        level = level * one(*cut)
    return level


def bell_draw(key, extent, width, bound, cuts=(), dtype=jnp.bfloat16):
    gain = shard_levels(key, extent, cuts, -0.22, 0.18) if cuts else 1.0
    values = jax.random.normal(key, extent, jnp.float32) * width * gain
    return jnp.minimum(jnp.maximum(values, -bound), bound).astype(dtype)


def setup_inputs(seed: int = 0, part: int = 0) -> dict:
    splits = jax.random.split(jax.random.key(seed), 14)
    own_keys = jax.random.split(jax.random.fold_in(splits[13], part), 14)
    clean = bell_draw(own_keys[0], (FRAMES, POSITIONS, MODEL_WIDTH), 1.0, 6.0, ((0, 8),))
    noise = bell_draw(own_keys[1], (FRAMES, POSITIONS, MODEL_WIDTH), 1.0, 6.0, ((0, 8),))
    timestep = jnp.clip(jax.random.uniform(own_keys[2], (1,), jnp.float32, 0.1, 0.9), 0.1, 0.9)
    guidance = jnp.clip(jax.random.uniform(own_keys[3], (1,), jnp.float32, 2.0, 6.0), 2.0, 6.0)
    condition_vector = bell_draw(own_keys[4], (MODEL_WIDTH,), 1.0, 6.0)
    empty_prompt_vector = bell_draw(splits[5], (MODEL_WIDTH,), 1.0, 6.0)
    timestep_direction = bell_draw(splits[6], (MODEL_WIDTH,), 1.0, 6.0)
    spatial_query_key_value = draw_spatial_query_key_value(jax.random.fold_in(splits[13], 71), part)
    spatial_output_weight = bell_draw(splits[8], (MODEL_WIDTH, MODEL_WIDTH), MODEL_WIDTH ** -0.5, 0.1875, ((0, 16),))
    temporal_query_key_value = draw_temporal_query_key_value(jax.random.fold_in(splits[13], 71), part)
    temporal_output_weight = bell_draw(splits[10], (MODEL_WIDTH, MODEL_WIDTH), MODEL_WIDTH ** -0.5, 0.1875, ((0, 16),))
    adapter_down_maps = bell_draw(splits[11], (2, MODEL_WIDTH, ADAPTER_RANK), MODEL_WIDTH ** -0.5, 0.1875)
    adapter_up_maps = bell_draw(splits[12], (2, ADAPTER_RANK, MODEL_WIDTH), ADAPTER_RANK ** -0.5, 0.75)
    return {"clean": clean, "noise": noise, "timestep": timestep, "guidance": guidance, "condition_vector": condition_vector, "empty_prompt_vector": empty_prompt_vector, "timestep_direction": timestep_direction, "spatial_query_key_value": spatial_query_key_value, "spatial_output_weight": spatial_output_weight, "temporal_query_key_value": temporal_query_key_value, "temporal_output_weight": temporal_output_weight, "adapter_down_maps": adapter_down_maps, "adapter_up_maps": adapter_up_maps}


epsilon = 1e-06

def rms_scale(features):
    return features * lax.rsqrt(lax.optimization_barrier(jnp.mean(features * features, axis=-1, keepdims=True)) + epsilon)

def project(rows_in, matrix):
    return jnp.einsum('...d,dk->...k', rows_in.astype(jnp.float32), matrix.astype(jnp.float32))

def space_attend(queries, key_rows, value_rows):
    head_count = queries.shape[-1] // HEAD_DIM
    split_dims = queries.shape[:-1] + (head_count, HEAD_DIM)
    scores = jnp.einsum('...qhd,...khd->...hqk', queries.reshape(split_dims).astype(jnp.float32), key_rows.reshape(split_dims).astype(jnp.float32)) * HEAD_DIM ** (-0.5)
    scores = scores - lax.optimization_barrier(jnp.max(scores, axis=-1, keepdims=True))
    exponent = jnp.exp(scores)
    soft_weights = (exponent / lax.optimization_barrier(jnp.sum(exponent, axis=-1, keepdims=True))).astype(jnp.bfloat16)
    result = jnp.einsum('...hqk,...khd->...qhd', soft_weights.astype(jnp.float32), value_rows.reshape(split_dims).astype(jnp.float32))
    return result.astype(jnp.bfloat16).reshape(queries.shape)

def time_attend(queries, key_rows, value_rows):
    head_count = queries.shape[-1] // HEAD_DIM
    split_dims = queries.shape[:-1] + (head_count, HEAD_DIM)
    scores = jnp.einsum('...fxhd,...gxhd->...xhfg', queries.reshape(split_dims).astype(jnp.float32), key_rows.reshape(split_dims).astype(jnp.float32)) * HEAD_DIM ** (-0.5)
    scores = scores - lax.optimization_barrier(jnp.max(scores, axis=-1, keepdims=True))
    exponent = jnp.exp(scores)
    soft_weights = (exponent / lax.optimization_barrier(jnp.sum(exponent, axis=-1, keepdims=True))).astype(jnp.bfloat16)
    result = jnp.einsum('...xhfg,...gxhd->...fxhd', soft_weights.astype(jnp.float32), value_rows.reshape(split_dims).astype(jnp.float32))
    return result.astype(jnp.bfloat16).reshape(queries.shape)

def time_core(embedding_rows, query_weight, key_weight, value_weight, out_weight):
    normed = rms_scale(embedding_rows).astype(jnp.bfloat16)
    queries = project(normed, query_weight).astype(jnp.bfloat16)
    key_rows = project(normed, key_weight).astype(jnp.bfloat16)
    value_rows = project(normed, value_weight).astype(jnp.bfloat16)
    return project(time_attend(queries, key_rows, value_rows), out_weight)

def student_network(embedding_rows, query_weight, key_weight, value_weight, out_weight, down_query, query_up_map, down_value, value_up_map):
    normed = rms_scale(embedding_rows).astype(jnp.bfloat16)
    low_query = project(normed, down_query).astype(jnp.bfloat16)
    low_value = project(normed, down_value).astype(jnp.bfloat16)
    queries = (project(normed, query_weight) + project(low_query, query_up_map)).astype(jnp.bfloat16)
    key_rows = project(normed, key_weight).astype(jnp.bfloat16)
    value_rows = (project(normed, value_weight) + project(low_value, value_up_map)).astype(jnp.bfloat16)
    return project(time_attend(queries, key_rows, value_rows), out_weight)

def reference(clean, noise, timestep, guidance, condition_vector, empty_prompt_vector, timestep_direction, spatial_query_key_value, spatial_output_weight, temporal_query_key_value, temporal_output_weight, adapter_down_maps, adapter_up_maps):
    moment = timestep[0]
    strength = guidance[0]
    noisy_rows = ((1.0 - moment) * clean.astype(jnp.float32) + moment * noise.astype(jnp.float32)).astype(jnp.bfloat16)
    shifted = noisy_rows.astype(jnp.float32) + moment * timestep_direction.astype(jnp.float32)
    velocities = []
    for embedding_rows in (condition_vector, empty_prompt_vector):
        entries = shifted + embedding_rows.astype(jnp.float32)
        normed = rms_scale(entries).astype(jnp.bfloat16)
        queries = project(normed, spatial_query_key_value[0]).astype(jnp.bfloat16)
        key_rows = project(normed, spatial_query_key_value[1]).astype(jnp.bfloat16)
        value_rows = project(normed, spatial_query_key_value[2]).astype(jnp.bfloat16)
        attended = lax.map(lambda trio: space_attend(trio[0], trio[1], trio[2]), (queries, key_rows, value_rows))
        layer_one = (entries + project(attended, spatial_output_weight)).astype(jnp.bfloat16)
        partial_value = time_core(layer_one.astype(jnp.float32), temporal_query_key_value[0], temporal_query_key_value[1], temporal_query_key_value[2], temporal_output_weight)
        velocities.append((layer_one.astype(jnp.float32) + partial_value).astype(jnp.bfloat16))
    cond_velocity = velocities[0].astype(jnp.float32)
    uncond_velocity = velocities[1].astype(jnp.float32)
    guided = (uncond_velocity + strength * (cond_velocity - uncond_velocity)).astype(jnp.bfloat16)
    student_in = shifted + condition_vector.astype(jnp.float32)

    def student_map(embedding_rows):
        return student_network(embedding_rows, temporal_query_key_value[0], temporal_query_key_value[1], temporal_query_key_value[2], temporal_output_weight, adapter_down_maps[0], adapter_up_maps[0], adapter_down_maps[1], adapter_up_maps[1])
    partial_value, tangent_part = jax.jvp(student_map, (student_in,), (guided.astype(jnp.float32),))
    student_out = (student_in + partial_value).astype(jnp.bfloat16)
    student_tangent = (guided.astype(jnp.float32) + tangent_part).astype(jnp.bfloat16)
    return (student_out, student_tangent)
```

```python
import functools
import math

import jax
import jax.numpy as jnp
from jax import lax
from jax.experimental import pallas as pl
from jax.experimental.pallas import tpu as pltpu
from jax.sharding import PartitionSpec as P

HEAD_DIM = 72
LANES = 128
ROW_TILE = 16
BLOCK = 8
TANGENT_BLOCK = 4
PAIR = 2
EXPONENT_SCALE = HEAD_DIM ** (-0.5) * math.log2(math.e)
VMEM_LIMIT = 40 * 1024 * 1024

epsilon = 1e-06


def partner(value, axis, bit):
    mask = 2**bit
    pairs = [(source, source ^ mask) for source in range(lax.axis_size(axis))]
    return lax.ppermute(value, axis, pairs)


def rms_scale(features):
    return features * lax.rsqrt(jnp.mean(features * features, axis=-1, keepdims=True) + epsilon)


def project(rows_in, matrix):
    return jnp.einsum("...d,dk->...k", rows_in, matrix, preferred_element_type=jnp.float32)


def space_attend(queries, key_rows, value_rows):
    head_count = queries.shape[-1] // HEAD_DIM
    split_dims = queries.shape[:-1] + (head_count, HEAD_DIM)
    scores = jnp.einsum(
        "...qhd,...khd->...hqk",
        queries.reshape(split_dims),
        key_rows.reshape(split_dims),
        preferred_element_type=jnp.float32,
    ) * HEAD_DIM ** (-0.5)
    scores = scores - jnp.max(scores, axis=-1, keepdims=True)
    exponent = jnp.exp(scores)
    soft_weights = (exponent / jnp.sum(exponent, axis=-1, keepdims=True)).astype(jnp.bfloat16)
    result = jnp.einsum(
        "...hqk,...khd->...qhd",
        soft_weights,
        value_rows.reshape(split_dims),
        preferred_element_type=jnp.float32,
    )
    return result.astype(jnp.bfloat16).reshape(queries.shape)


def time_attend(queries, key_rows, value_rows):
    head_count = queries.shape[-1] // HEAD_DIM
    split_dims = queries.shape[:-1] + (head_count, HEAD_DIM)
    scores = jnp.einsum(
        "...fxhd,...gxhd->...xhfg",
        queries.reshape(split_dims),
        key_rows.reshape(split_dims),
        preferred_element_type=jnp.float32,
    ) * HEAD_DIM ** (-0.5)
    scores = scores - jnp.max(scores, axis=-1, keepdims=True)
    exponent = jnp.exp(scores)
    soft_weights = (exponent / jnp.sum(exponent, axis=-1, keepdims=True)).astype(jnp.bfloat16)
    result = jnp.einsum(
        "...xhfg,...gxhd->...fxhd",
        soft_weights,
        value_rows.reshape(split_dims),
        preferred_element_type=jnp.float32,
    )
    return result.astype(jnp.bfloat16).reshape(queries.shape)


def time_core(embedding_rows, query_weight, key_weight, value_weight, out_weight):
    normed = rms_scale(embedding_rows).astype(jnp.bfloat16)
    queries = project(normed, query_weight).astype(jnp.bfloat16)
    key_rows = project(normed, key_weight).astype(jnp.bfloat16)
    value_rows = project(normed, value_weight).astype(jnp.bfloat16)
    return project(time_attend(queries, key_rows, value_rows), out_weight)


def student_network(
    embedding_rows,
    query_weight,
    key_weight,
    value_weight,
    out_weight,
    down_query,
    query_up_map,
    down_value,
    value_up_map,
):
    normed = rms_scale(embedding_rows).astype(jnp.bfloat16)
    low_query = project(normed, down_query).astype(jnp.bfloat16)
    low_value = project(normed, down_value).astype(jnp.bfloat16)
    queries = (project(normed, query_weight) + project(low_query, query_up_map)).astype(
        jnp.bfloat16
    )
    key_rows = project(normed, key_weight).astype(jnp.bfloat16)
    value_rows = (project(normed, value_weight) + project(low_value, value_up_map)).astype(
        jnp.bfloat16
    )
    return project(time_attend(queries, key_rows, value_rows), out_weight)


def plain_on_device(
    clean,
    noise,
    timestep,
    guidance,
    condition_vector,
    empty_prompt_vector,
    timestep_direction,
    spatial_query_key_value,
    spatial_output_weight,
    temporal_query_key_value,
    temporal_output_weight,
    adapter_down_maps,
    adapter_up_maps,
):
    moment = timestep[0]
    strength = guidance[0]
    pair_side = lax.axis_index("cfg")
    noisy_rows = (
        (1.0 - moment) * clean.astype(jnp.float32) + moment * noise.astype(jnp.float32)
    ).astype(jnp.bfloat16)
    shifted = noisy_rows.astype(jnp.float32) + moment * timestep_direction.astype(jnp.float32)
    embeds = jnp.where(pair_side == 0, condition_vector, empty_prompt_vector)[None]
    branch_count = embeds.shape[0]
    entries = shifted[None] + embeds.astype(jnp.float32)[:, None, None, :]
    normed = rms_scale(entries).astype(jnp.bfloat16)
    triple = jnp.einsum(
        "bfpd,jdk->jbfpk",
        normed,
        lax.all_gather(spatial_query_key_value, ("cfg", "seq"), axis=2, tiled=True),
        preferred_element_type=jnp.float32,
    ).astype(jnp.bfloat16)
    attended = space_attend(triple[0], triple[1], triple[2])
    partial_value = jnp.einsum(
        "bfpk,kd->bfpd",
        attended,
        lax.all_gather(spatial_output_weight, ("cfg", "seq"), axis=0, tiled=True),
        preferred_element_type=jnp.float32,
    )
    layer_one = (entries + partial_value).astype(jnp.bfloat16)
    frame_count = layer_one.shape[1]
    position_count = layer_one.shape[2]
    width = layer_one.shape[3]
    stacked = jnp.concatenate([layer_one, noisy_rows[None]], axis=0).reshape(
        branch_count + 1, frame_count, 2, position_count // 2, width
    )
    regrouped = lax.all_to_all(stacked, "seq", split_axis=3, concat_axis=1, tiled=True)
    frames = regrouped.shape[1]
    local_rows = regrouped.shape[3]
    teacher_in = regrouped[:branch_count].reshape(branch_count, frames, 2 * local_rows, width)
    noisy_local = regrouped[branch_count]
    time_qkv, time_out = (
        lax.all_gather(temporal_query_key_value, ("cfg", "seq"), axis=2, tiled=True),
        lax.all_gather(temporal_output_weight, ("cfg", "seq"), axis=0, tiled=True),
    )
    teacher_part = time_core(
        teacher_in.astype(jnp.float32), time_qkv[0], time_qkv[1], time_qkv[2], time_out
    )
    velocity = (
        (teacher_in.astype(jnp.float32) + teacher_part)
        .astype(jnp.bfloat16)
        .reshape(branch_count, frames, 2, local_rows, width)
    )
    own_velocity = velocity[0]
    own_half = lax.dynamic_index_in_dim(own_velocity, pair_side, 1, keepdims=False)
    outgoing = lax.dynamic_index_in_dim(own_velocity, 1 - pair_side, 1, keepdims=False)
    other_half = partner(outgoing, "cfg", 0)
    is_first = pair_side == 0
    cond_velocity = jnp.where(is_first, own_half, other_half)
    uncond_velocity = jnp.where(is_first, other_half, own_half)
    student_noisy = lax.dynamic_index_in_dim(noisy_local, pair_side, 1, keepdims=False)
    query_up_map = adapter_up_maps[0]
    value_up_map = adapter_up_maps[1]
    uncond_float = uncond_velocity.astype(jnp.float32)
    guided = (uncond_float + strength * (cond_velocity.astype(jnp.float32) - uncond_float)).astype(
        jnp.bfloat16
    )
    student_in = (
        student_noisy.astype(jnp.float32)
        + moment * timestep_direction.astype(jnp.float32)
        + condition_vector.astype(jnp.float32)
    )

    def student_map(embedding_rows):
        return student_network(
            embedding_rows,
            time_qkv[0],
            time_qkv[1],
            time_qkv[2],
            time_out,
            adapter_down_maps[0],
            query_up_map,
            adapter_down_maps[1],
            value_up_map,
        )

    partial_value, tangent_part = jax.jvp(student_map, (student_in,), (guided.astype(jnp.float32),))
    primal = (student_in + partial_value).astype(jnp.bfloat16)
    tangent = (guided.astype(jnp.float32) + tangent_part).astype(jnp.bfloat16)
    returned = lax.all_to_all(
        jnp.stack([primal, tangent]), "seq", split_axis=1, concat_axis=2, tiled=True
    )
    return (returned[0], returned[1])


def dot(left, right):
    return lax.dot_general(
        left, right, (((1,), (0,)), ((), ())), preferred_element_type=jnp.float32
    )


def dot_t(left, right):
    return lax.dot_general(
        left, right, (((1,), (1,)), ((), ())), preferred_element_type=jnp.float32
    )


def lane_range(shape, start, low, high):
    lane = lax.broadcasted_iota(jnp.int32, shape, len(shape) - 1) + start
    return (lane >= low) & (lane < high)


def only(value, keep):
    return jnp.where(keep, value, jnp.zeros_like(value))


def window_of(low, high):
    start = low // LANES * LANES
    return start, -(-high // LANES) * LANES - start


def inverse_rms(features):
    return lax.rsqrt(jnp.mean(features * features, axis=-1, keepdims=True) + epsilon)


def weight_copies(seat, layout, pieces, weights_ref, sems):
    side, place, core = seat[0], seat[1], seat[2]
    across, along = place // 4, lax.rem(place, 2)
    copies = []
    for array, part, sibling, (x, z, y) in layout:
        piece = pieces[array] if part is None else pieces[array].at[part]
        count, rows = piece.shape[:2]
        block = ((side ^ x) * 2 + (across ^ z)) * 2 + (along ^ y)
        start = pl.multiple_of(block * rows, ROW_TILE)
        copies.append(
            pltpu.make_async_copy(
                piece,
                weights_ref.at[pl.ds((core ^ sibling) * count, count), pl.ds(start, rows), :],
                sems.at[len(copies)],
            )
        )
    return copies


def noisy_kernel(seat_ref, moment_ref, clean_ref, noise_ref, *rest):
    line_refs, rows_ref = rest[:-1], rest[-1]
    moment = moment_ref[0]
    rows_ref[...] = (
        (1.0 - moment) * clean_ref[0].astype(jnp.float32)
        + moment * noise_ref[0].astype(jnp.float32)
    ).astype(jnp.bfloat16)
    for index in range(2 * len(line_refs)):
        start = pl.multiple_of((seat_ref[1] ^ index) * ROW_TILE, ROW_TILE)
        line_refs[index // 2][index % 2, 0] = rows_ref[pl.ds(start, ROW_TILE), :]


def noisy_pieces(seat, moment, clean, noise, seats):
    frames, positions, width = clean.shape
    rows = seats * ROW_TILE
    block = pl.BlockSpec((1, rows, width), lambda f, seat: (f, seat[0], 0))
    half = seats // 2
    piece = jax.ShapeDtypeStruct((2, frames, ROW_TILE, width), jnp.bfloat16)
    out_block = pl.BlockSpec((2, 1, ROW_TILE, width), lambda f, seat: (0, f, 0, 0))
    return pl.pallas_call(
        noisy_kernel,
        out_shape=[piece] * half,
        grid_spec=pltpu.PrefetchScalarGridSpec(
            num_scalar_prefetch=1,
            grid=(frames,),
            in_specs=[pl.BlockSpec(memory_space=pltpu.SMEM), block, block],
            out_specs=[out_block] * half,
            scratch_shapes=[pltpu.VMEM((rows, width), jnp.bfloat16)],
        ),
        compiler_params=pltpu.CompilerParams(vmem_limit_bytes=VMEM_LIMIT),
    )(seat, moment, clean, noise)


def space_kernel(layout, pieces, targets, seat_ref, moment_ref, clean_ref, noise_ref, shift_ref, *rest):
    weight_pieces, sent_refs = rest[:pieces], rest[pieces : pieces + targets]
    weights_ref, noisy_ref, query_ref, key_ref, value_ref, mixed_ref, sems = rest[pieces + targets :]
    moment = moment_ref[0]
    pair, positions, width = clean_ref.shape

    @pl.when(pl.program_id(0) == 0)
    def _():
        wait_all(start_all(weight_copies(seat_ref, layout, weight_pieces, weights_ref, sems)))

    noisy = (
        (1.0 - moment) * clean_ref[...].reshape(pair * positions, width).astype(jnp.float32)
        + moment * noise_ref[...].reshape(pair * positions, width).astype(jnp.float32)
    ).astype(jnp.bfloat16)
    noisy_ref[...] = noisy
    entry = noisy.astype(jnp.float32) + shift_ref[...]
    normed = (entry * inverse_rms(entry)).astype(jnp.bfloat16)
    query_ref[...] = dot_t(normed, weights_ref[0]).astype(jnp.bfloat16)
    key_ref[...] = dot_t(normed, weights_ref[1]).astype(jnp.bfloat16)
    value_ref[...] = dot_t(normed, weights_ref[2]).astype(jnp.bfloat16)

    @pl.loop(0, pair)
    def _(frame):
        here = pl.ds(pl.multiple_of(frame * positions, positions), positions)
        space_mix(query_ref.at[here], key_ref.at[here], value_ref.at[here], mixed_ref.at[here])

    entry = noisy_ref[...].astype(jnp.float32) + shift_ref[...]
    query_ref[...] = (entry + dot(mixed_ref[...], weights_ref[3])).astype(jnp.bfloat16)
    lines = sent_refs[0].shape[0]
    for index, ref in enumerate(sent_refs):
        for line in range(lines):
            seat = (seat_ref[0] ^ (index // 2)) * lines * 2 + (
                seat_ref[1] ^ (line * 2 + index % 2)
            )
            for frame in range(pair):
                start = pl.multiple_of(frame * positions + seat * ROW_TILE, ROW_TILE)
                ref[line, frame] = query_ref[pl.ds(start, ROW_TILE), :]


def space_mix(query_ref, key_ref, value_ref, mixed_ref):
    positions, width = query_ref.shape
    weights = []
    for head in range(width // HEAD_DIM):
        low, high = head * HEAD_DIM, (head + 1) * HEAD_DIM
        start, extent = window_of(low, high)
        keep = lane_range((positions, extent), start, low, high)
        queries = only(query_ref[:, pl.ds(start, extent)], keep)
        scores = dot_t(queries, key_ref[:, pl.ds(start, extent)])
        top = jnp.max(scores, axis=-1, keepdims=True)
        exponent = jnp.exp2((scores - top) * EXPONENT_SCALE)
        total = jnp.sum(exponent, axis=-1, keepdims=True)
        weights.append((exponent * (1.0 / total)).astype(jnp.bfloat16))
        tile = high // (2 * LANES)
        done = [low // (2 * LANES)] if tile > low // (2 * LANES) else []
        if head == width // HEAD_DIM - 1:
            done = [(width - 1) // (2 * LANES)]
        for full in done:
            left_edge = full * 2 * LANES
            edge = min(width, left_edge + 2 * LANES)
            heads = range(left_edge // HEAD_DIM, -(-edge // HEAD_DIM))
            values = value_ref[:, pl.ds(left_edge, edge - left_edge)]
            parts = [
                only(
                    values,
                    lane_range(values.shape, left_edge, h * HEAD_DIM, (h + 1) * HEAD_DIM),
                )
                for h in heads
            ]
            mixed = dot(
                jnp.concatenate([weights[h] for h in heads], axis=1),
                jnp.concatenate(parts, axis=0),
            )
            mixed_ref[:, pl.ds(left_edge, edge - left_edge)] = mixed.astype(jnp.bfloat16)


def spatial_layer(seat, moment, clean, noise, shift, weights, frames, seats):
    pieces, layout = weights
    positions, width = clean.shape[1:]
    frame_block = pl.BlockSpec(
        (PAIR, positions, width), lambda f, seat: (seat[0] * (frames // PAIR) + f, 0, 0)
    )
    lines = seats // 2
    piece = jax.ShapeDtypeStruct((lines, frames, ROW_TILE, width), jnp.bfloat16)
    vmem = lambda *shape: pltpu.VMEM(shape, jnp.bfloat16)
    rows = frames * positions
    return pl.pallas_call(
        functools.partial(space_kernel, layout, len(pieces), 4),
        out_shape=[piece] * 4,
        grid_spec=pltpu.PrefetchScalarGridSpec(
            num_scalar_prefetch=1,
            grid=(frames // PAIR,),
            in_specs=[
                pl.BlockSpec(memory_space=pltpu.SMEM),
                frame_block,
                frame_block,
                pl.BlockSpec(shift.shape, lambda f, seat: (0, 0)),
            ]
            + [pl.BlockSpec(memory_space=pl.ANY)] * len(pieces),
            out_specs=[
                pl.BlockSpec((lines, PAIR, ROW_TILE, width), lambda f, seat: (0, f, 0, 0))
            ]
            * 4,
            scratch_shapes=[vmem(4, width, width)]
            + [vmem(PAIR * positions, width)] * 5
            + [pltpu.SemaphoreType.DMA((len(layout),))],
        ),
        compiler_params=pltpu.CompilerParams(vmem_limit_bytes=VMEM_LIMIT),
        cost_estimate=pl.CostEstimate(
            flops=14 * rows * width * width,
            bytes_accessed=8 * width * width + 6 * rows * width,
            transcendentals=rows * positions * width // HEAD_DIM,
        ),
    )(seat, moment, clean, noise, shift, *pieces)


def swap_matrix(rows, columns):
    count = rows * columns
    target = lax.broadcasted_iota(jnp.int32, (count, count), 0)
    source = lax.broadcasted_iota(jnp.int32, (count, count), 1)
    moved = lax.rem(target, rows) * columns + lax.div(target, rows)
    return jnp.where(source == moved, 1.0, 0.0).astype(jnp.bfloat16)


def halves(value, frames, reduce):
    first = lane_range(value.shape, 0, 0, frames)
    if reduce == "max":
        low = jnp.max(jnp.where(first, value, -jnp.inf), axis=-1, keepdims=True)
        high = jnp.max(jnp.where(first, -jnp.inf, value), axis=-1, keepdims=True)
    else:
        low = jnp.sum(jnp.where(first, value, 0.0), axis=-1, keepdims=True)
        high = jnp.sum(jnp.where(first, 0.0, value), axis=-1, keepdims=True)
    return first, low, high


def time_mix(frames, refs, tangents=None):
    query_ref, key_ref, value_ref, mixed_ref = refs
    rows, width = query_ref.shape
    scale = HEAD_DIM ** (-0.5)
    tiles = [[] for _ in range(width // LANES)]
    tangent_tiles = [[] for _ in range(width // LANES)]
    pairs = width // (2 * HEAD_DIM)
    blocks = [pl.ds(i * frames, frames) for i in range(rows // frames)]

    def stack(value, start, low):
        shape = value.shape
        return jnp.concatenate(
            [
                only(value, lane_range(shape, start, low, low + HEAD_DIM)),
                only(value, lane_range(shape, start, low + HEAD_DIM, low + 2 * HEAD_DIM)),
            ],
            axis=0,
        )

    for pair in range(pairs):
        low = pair * 2 * HEAD_DIM
        start, extent = window_of(low, low + 2 * HEAD_DIM)
        columns = pl.ds(start, extent)
        keys = [stack(key_ref[b, columns], start, low) for b in blocks]
        values = [stack(value_ref[b, columns], start, low) for b in blocks]
        scores = jnp.concatenate(
            [dot_t(query_ref[b, columns], k) for b, k in zip(blocks, keys)], axis=0
        )
        first, top_low, top_high = halves(scores, frames, "max")
        exponent = jnp.exp2((scores - jnp.where(first, top_low, top_high)) * EXPONENT_SCALE)
        _, sum_low, sum_high = halves(exponent, frames, "sum")
        weights = exponent * jnp.where(first, 1.0 / sum_low, 1.0 / sum_high)
        rounded = weights.astype(jnp.bfloat16)
        mixed = jnp.concatenate(
            [
                dot(rounded[i * frames : (i + 1) * frames], v)
                for i, v in enumerate(values)
            ],
            axis=0,
        )
        for tile in range(extent // LANES):
            tiles[start // LANES + tile].append(mixed[:, tile * LANES : (tile + 1) * LANES])
        if tangents is not None:
            query_dot, key_dot, value_dot, _ = tangents
            score_dots = jnp.concatenate(
                [
                    dot_t(query_dot[b, columns], k)
                    + dot_t(query_ref[b, columns], stack(key_dot[b, columns], start, low))
                    for b, k in zip(blocks, keys)
                ],
                axis=0,
            ) * scale
            _, mean_low, mean_high = halves(weights * score_dots, frames, "sum")
            weight_dots = (
                weights * (score_dots - jnp.where(first, mean_low, mean_high))
            ).astype(jnp.bfloat16)
            mixed_dots = jnp.concatenate(
                [
                    dot(
                        jnp.concatenate(
                            [
                                weight_dots[i * frames : (i + 1) * frames],
                                rounded[i * frames : (i + 1) * frames],
                            ],
                            axis=1,
                        ),
                        jnp.concatenate(
                            [v, stack(value_dot[b, columns], start, low)], axis=0
                        ),
                    )
                    for i, (b, v) in enumerate(zip(blocks, values))
                ],
                axis=0,
            )
            for tile in range(extent // LANES):
                tangent_tiles[start // LANES + tile].append(
                    mixed_dots[:, tile * LANES : (tile + 1) * LANES]
                )
    for tile in range(width // LANES):
        columns = pl.ds(tile * LANES, LANES)
        mixed_ref[:, columns] = functools.reduce(jnp.add, tiles[tile]).astype(jnp.bfloat16)
        if tangents is not None:
            tangents[3][:, columns] = functools.reduce(jnp.add, tangent_tiles[tile]).astype(
                jnp.bfloat16
            )


def arrivals(seat, pieces, came_ref, sems):
    copies = []
    for line, piece in enumerate(pieces):
        neighbours, frames = piece.shape[:2]
        for index in range(neighbours):
            first = (seat[1] ^ (line * 2 + index % 2)) * frames * (neighbours // 2)
            if neighbours > 2:
                first = first + (seat[0] ^ (index // 2)) * frames
            copies.append(
                pltpu.make_async_copy(
                    piece.at[index], came_ref.at[pl.ds(first, frames)], sems.at[len(copies)]
                )
            )
    return copies


def departures(seat, going_ref, pieces, sems):
    rows = pieces[0].shape[0]
    return [
        pltpu.make_async_copy(
            going_ref.at[pl.ds(pl.multiple_of((seat[1] ^ index) * rows, ROW_TILE), rows)],
            piece,
            sems.at[index],
        )
        for index, piece in enumerate(pieces)
    ]


def by_position(came_ref, rows_ref):
    frames, positions, width = came_ref.shape
    turn = swap_matrix(ROW_TILE, positions)
    for part in range(frames // ROW_TILE):
        first = part * ROW_TILE
        piece = came_ref[first : first + ROW_TILE].reshape(ROW_TILE * positions, width)
        turned = dot(turn, piece).astype(jnp.bfloat16)
        for position in range(positions):
            rows_ref[pl.ds(position * frames + first, ROW_TILE), :] = turned[
                position * ROW_TILE : (position + 1) * ROW_TILE
            ]


def by_frame(rows_ref, going_ref, frames):
    positions = rows_ref.shape[0] // frames
    group = min(frames, 2 * LANES // positions)
    turn = swap_matrix(positions, group)
    for part in range(frames // group):
        piece = jnp.concatenate(
            [rows_ref[pl.ds(p * frames + part * group, group), :] for p in range(positions)],
            axis=0,
        )
        here = pl.ds(part * group * positions, group * positions)
        going_ref[here, :] = dot(turn, piece).astype(jnp.bfloat16)


def wait_all(copies):
    for copy in copies:
        copy.wait()


def start_all(copies):
    for copy in copies:
        copy.start()
    return copies


def adapted(rows_in, weights_ref, down_ref, up_ref, refs):
    rank = down_ref.shape[0] // 2
    low = dot_t(rows_in, down_ref[...]).astype(jnp.bfloat16)
    first = lane_range(low.shape, 0, 0, rank)
    refs[0][...] = (
        dot_t(rows_in, weights_ref[0]) + dot(only(low, first), up_ref[...])
    ).astype(jnp.bfloat16)
    refs[1][...] = dot_t(rows_in, weights_ref[1]).astype(jnp.bfloat16)
    refs[2][...] = (
        dot_t(rows_in, weights_ref[2]) + dot(only(low, jnp.logical_not(first)), up_ref[...])
    ).astype(jnp.bfloat16)


def student_rows_kernel(layout, counts, seat_ref, shift_ref, down_ref, up_ref, *rest):
    weight_count, piece_count = counts
    weight_pieces, rest = rest[:weight_count], rest[weight_count:]
    pieces, rest = rest[:piece_count], rest[piece_count:]
    rows_out_ref, primal_ref, weights_ref, came_ref, rows_ref, weight_sems, piece_sems = rest
    chunk = rows_out_ref.shape[0]

    @pl.when(pl.program_id(0) == 0)
    def _():
        weights = weight_copies(seat_ref, layout, weight_pieces, weights_ref, weight_sems)
        lines = piece_count - 1
        copies = []
        for index in range(2 * lines):
            piece = pieces[lines].at[index // 2] if index % 2 else pieces[index // 2].at[0]
            count = piece.shape[0]
            copies.append(
                pltpu.make_async_copy(
                    piece,
                    came_ref.at[pl.ds((seat_ref[1] ^ index) * count, count)],
                    piece_sems.at[index],
                )
            )
        start_all(copies)
        start_all(weights)
        wait_all(copies)
        by_position(came_ref, rows_ref)
        wait_all(weights)

    here = pl.ds(pl.multiple_of(pl.program_id(0) * chunk, chunk), chunk)
    rows_out_ref[...] = rows_ref[here, :]
    entry = rows_ref[here, :].astype(jnp.float32) + shift_ref[...]
    normed = (entry * inverse_rms(entry)).astype(jnp.bfloat16)
    adapted(normed, weights_ref, down_ref, up_ref, [primal_ref.at[i] for i in range(3)])


def student_mix_kernel(layout, frames, seat_ref, shift_ref, rows_ref, primal_ref, *rest):
    weight_pieces, out_refs, rest = rest[:-7], rest[-7:-5], rest[-5:]
    weights_ref, done_ref, mixed_ref, weight_sems, piece_sems = rest
    step, chunk = pl.program_id(0), mixed_ref.shape[0]
    weights = weight_copies(seat_ref, layout, weight_pieces, weights_ref, weight_sems)

    @pl.when(step == 0)
    def _():
        start_all(weights)

    time_mix(frames, [primal_ref.at[i] for i in range(3)] + [mixed_ref])

    @pl.when(step == 0)
    def _():
        wait_all(weights)

    here = pl.ds(pl.multiple_of(step * chunk, chunk), chunk)
    entry = rows_ref[...].astype(jnp.float32) + shift_ref[...]
    done_ref[0, here, :] = (entry + dot(mixed_ref[...], weights_ref[3])).astype(jnp.bfloat16)

    @pl.when(step == pl.num_programs(0) - 1)
    def _():
        by_frame(done_ref.at[0], done_ref.at[1], frames)
        pieces = [ref.at[line] for line in range(out_refs[0].shape[0]) for ref in out_refs]
        wait_all(start_all(departures(seat_ref, done_ref.at[1], pieces, piece_sems)))


def teacher(frames, rows_ref, weights_ref, refs, here):
    entry = rows_ref[here, :].astype(jnp.float32)
    normed = (entry * inverse_rms(entry)).astype(jnp.bfloat16)
    for index, ref in enumerate(refs[:3]):
        ref[...] = dot_t(normed, weights_ref[index]).astype(jnp.bfloat16)
    time_mix(frames, refs)
    entry = rows_ref[here, :].astype(jnp.float32)
    return (entry + dot(refs[3][...], weights_ref[3])).astype(jnp.bfloat16)


def teacher_kernel(layout, counts, seat_ref, *rest):
    weight_count, piece_count = counts
    weight_pieces, rest = rest[:weight_count], rest[weight_count:]
    pieces, rest = rest[:piece_count], rest[piece_count:]
    velocity_ref, weights_ref, came_ref, rows_ref = rest[:4]
    refs, (weight_sems, piece_sems) = rest[4:8], rest[8:]
    frames = came_ref.shape[0]
    chunk = refs[0].shape[0]

    @pl.when(pl.program_id(0) == 0)
    def _():
        came = start_all(arrivals(seat_ref, pieces, came_ref, piece_sems))
        weights = start_all(
            weight_copies(seat_ref, layout, weight_pieces, weights_ref, weight_sems)
        )
        wait_all(came)
        by_position(came_ref, rows_ref)
        wait_all(weights)

    here = pl.ds(pl.multiple_of(pl.program_id(0) * chunk, chunk), chunk)
    velocity_ref[...] = teacher(frames, rows_ref, weights_ref, refs, here)


def tangent_kernel(layout, counts, seat_ref, strength_ref, shift_ref, down_ref, up_ref, *rest):
    weight_count, piece_count, out_count = counts
    velocity_ref, noisy_ref, primal_ref = rest[:3]
    rest = rest[3:]
    weight_pieces, rest = rest[:weight_count], rest[weight_count:]
    pieces, rest = rest[:piece_count], rest[piece_count:]
    out_pieces, rest = rest[:out_count], rest[out_count:]
    weights_ref, done_ref, going_ref, guided_ref, *tail = rest[-14:]
    refs, dots, (weight_sems, piece_sems) = tail[:4], tail[4:8], tail[8:10]
    frames = done_ref.shape[0] // (ROW_TILE // 2)
    chunk = refs[0].shape[0]
    step = pl.program_id(0)
    first = piece_count > 1

    @pl.when(step == 0)
    def _():
        weights = weight_copies(seat_ref, layout, weight_pieces, weights_ref, weight_sems)
        if first:
            other_ref, came_ref, rows_ref = rest[:3]
            came = start_all(arrivals(seat_ref, pieces, came_ref, piece_sems))
        start_all(weights)
        if first:
            wait_all(came)
            by_position(came_ref, rows_ref)
            half = other_ref.shape[0]
            other_ref[...] = rows_ref[pl.ds(half, half), :]
        wait_all(weights)

    here = pl.ds(pl.multiple_of(step * chunk, chunk), chunk)
    rows_ref = rest[2].at[here] if first else pieces[0]
    uncond = teacher(frames, rows_ref, weights_ref, refs, slice(None)).astype(jnp.float32)
    guided = (
        uncond + strength_ref[0] * (velocity_ref[...].astype(jnp.float32) - uncond)
    ).astype(jnp.bfloat16)
    guided_ref[...] = guided
    guided = guided.astype(jnp.float32)
    entry = noisy_ref[...].astype(jnp.float32) + shift_ref[...]
    inverse = inverse_rms(entry)
    inverse_dot = -(inverse * inverse * inverse) * jnp.mean(
        entry * guided, axis=-1, keepdims=True
    )
    normed_dot = (guided * inverse + entry * inverse_dot).astype(jnp.bfloat16)
    adapted(normed_dot, weights_ref, down_ref, up_ref, dots)
    primal = [primal_ref.at[i] for i in range(3)] + [refs[3]]
    time_mix(frames, primal, dots)
    done_ref[here, :] = (
        guided_ref[...].astype(jnp.float32) + dot(dots[3][...], weights_ref[3])
    ).astype(jnp.bfloat16)

    @pl.when(step == pl.num_programs(0) - 1)
    def _():
        by_frame(done_ref, going_ref, frames)
        wait_all(start_all(departures(seat_ref, going_ref, out_pieces, piece_sems)))


IN_VMEM = pl.BlockSpec(memory_space=pltpu.VMEM)
IN_SMEM = pl.BlockSpec(memory_space=pltpu.SMEM)
ANYWHERE = pl.BlockSpec(memory_space=pl.ANY)


def time_call(kernel, passes, rows, width, **settings):
    return pl.pallas_call(
        kernel,
        compiler_params=pltpu.CompilerParams(vmem_limit_bytes=VMEM_LIMIT),
        cost_estimate=pl.CostEstimate(
            flops=int(12 * passes * rows * width * width),
            bytes_accessed=8 * width * width + 8 * rows * width,
            transcendentals=rows * LANES * width // HEAD_DIM,
        ),
        **settings,
    )


def student_rows(seat, shift, down, up, weights, pieces, frames):
    weights, layout = weights
    width = shift.shape[-1]
    rows, chunk = frames * ROW_TILE, BLOCK * frames
    vmem = lambda *shape: pltpu.VMEM(shape, jnp.bfloat16)
    fixed = lambda value: pl.BlockSpec(value.shape, lambda i: (0,) * value.ndim)
    return time_call(
        functools.partial(student_rows_kernel, layout, (len(weights), len(pieces))),
        0.6,
        rows,
        width,
        grid=(rows // chunk,),
        out_shape=[
            jax.ShapeDtypeStruct((rows, width), jnp.bfloat16),
            jax.ShapeDtypeStruct((3, rows, width), jnp.bfloat16),
        ],
        in_specs=[IN_SMEM, fixed(shift), fixed(down), fixed(up)]
        + [ANYWHERE] * (len(weights) + len(pieces)),
        out_specs=[
            pl.BlockSpec((chunk, width), lambda i: (i, 0)),
            pl.BlockSpec((3, chunk, width), lambda i: (0, i, 0)),
        ],
        scratch_shapes=[
            vmem(4, width, width),
            vmem(frames, ROW_TILE, width),
            vmem(rows, width),
            pltpu.SemaphoreType.DMA((len(layout),)),
            pltpu.SemaphoreType.DMA((2 * len(pieces),)),
        ],
    )(seat, shift, down, up, *weights, *pieces)


def student_mix(seat, shift, rows_in, primal, weights, frames, seats):
    weights, layout = weights
    rows, width = rows_in.shape
    chunk = BLOCK * frames
    vmem = lambda *shape: pltpu.VMEM(shape, jnp.bfloat16)
    piece = jax.ShapeDtypeStruct((seats // 2, rows // seats, width), jnp.bfloat16)
    return time_call(
        functools.partial(student_mix_kernel, layout, frames),
        0.6,
        rows,
        width,
        grid=(rows // chunk,),
        out_shape=[piece] * 2,
        in_specs=[
            IN_SMEM,
            pl.BlockSpec(shift.shape, lambda i: (0, 0)),
            pl.BlockSpec((chunk, width), lambda i: (i, 0)),
            pl.BlockSpec((3, chunk, width), lambda i: (0, i, 0)),
        ]
        + [ANYWHERE] * len(weights),
        out_specs=[ANYWHERE] * 2,
        scratch_shapes=[
            vmem(4, width, width),
            vmem(2, rows, width),
            vmem(chunk, width),
            pltpu.SemaphoreType.DMA((len(layout),)),
            pltpu.SemaphoreType.DMA((seats,)),
        ],
    )(seat, shift, rows_in, primal, *weights)


def teacher_velocity(seat, weights, pieces, frames):
    weights, layout = weights
    width = pieces[0].shape[-1]
    rows = frames * ROW_TILE
    vmem = lambda *shape: pltpu.VMEM(shape, jnp.bfloat16)
    return time_call(
        functools.partial(teacher_kernel, layout, (len(weights), len(pieces))),
        1,
        rows,
        width,
        out_shape=jax.ShapeDtypeStruct((rows, width), jnp.bfloat16),
        grid=(ROW_TILE // BLOCK,),
        in_specs=[IN_SMEM] + [ANYWHERE] * (len(weights) + len(pieces)),
        out_specs=pl.BlockSpec((BLOCK * frames, width), lambda i: (i, 0)),
        scratch_shapes=[
            vmem(4, width, width),
            vmem(frames, ROW_TILE, width),
            vmem(rows, width),
        ]
        + [vmem(BLOCK * frames, width)] * 4
        + [
            pltpu.SemaphoreType.DMA((len(layout),)),
            pltpu.SemaphoreType.DMA((4 * len(pieces),)),
        ],
    )(seat, *weights, *pieces)


def student_tangent(
    seat, strength, shift, down, up, velocity, noisy, primal, weights, pieces, frames, seats
):
    weights, layout = weights
    first = len(pieces) > 1
    width = shift.shape[-1]
    rows = frames * ROW_TILE // 2
    piece = jax.ShapeDtypeStruct((rows // seats, width), jnp.bfloat16)
    vmem = lambda *shape: pltpu.VMEM(shape, jnp.bfloat16)
    chunk = TANGENT_BLOCK * frames
    steps = rows // chunk
    part = 0 if first else steps
    half = pl.BlockSpec((chunk, width), lambda i: (part + i, 0))
    halves = pl.BlockSpec((3, chunk, width), lambda i: (0, part + i, 0))
    fixed = lambda value: pl.BlockSpec(value.shape, lambda i: (0,) * value.ndim)
    other = jax.ShapeDtypeStruct((rows, width), jnp.bfloat16)
    return time_call(
        functools.partial(tangent_kernel, layout, (len(weights), len(pieces), seats)),
        1,
        rows,
        width,
        grid=(steps,),
        out_shape=[piece] * seats + [other] * first,
        in_specs=[IN_SMEM] * 2
        + [fixed(shift), fixed(down), fixed(up), half, half, halves]
        + [ANYWHERE] * len(weights)
        + ([ANYWHERE] * len(pieces) if first else [pl.BlockSpec((chunk, width), lambda i: (i, 0))]),
        out_specs=[ANYWHERE] * seats + [fixed(other)] * first,
        scratch_shapes=[vmem(frames, ROW_TILE, width), vmem(2 * rows, width)] * first
        + [vmem(4, width, width), vmem(rows, width), vmem(rows, width)]
        + [vmem(chunk, width)] * 9
        + [
            pltpu.SemaphoreType.DMA((len(layout),)),
            pltpu.SemaphoreType.DMA((4 * max(4, seats),)),
        ],
    )(seat, strength, shift, down, up, velocity, noisy, primal, *weights, *pieces)


def place_kernel(count, seat_ref, *rest):
    result_ref = rest[-1]
    frames, _, width = result_ref.shape
    for index in range(count):
        if len(rest[0].shape) > 2:
            parts = [rest[index // 2][index % 2].astype(jnp.float32)]
        else:
            parts = [piece[...].astype(jnp.float32) for piece in rest[index:-1:count]]
        parts = [part.reshape(frames, -1, width) for part in parts]
        start = pl.multiple_of((seat_ref[1] ^ index) * ROW_TILE, ROW_TILE)
        result_ref[:, pl.ds(start, ROW_TILE), :] = jnp.concatenate(parts, axis=1).astype(
            jnp.bfloat16
        )


def placed(seat, pieces, seats, frames):
    width = pieces[0].shape[-1]
    steps = max(1, frames // 4)
    half = frames // steps

    def block(piece):
        lead, (rows, width) = piece.shape[:-2], piece.shape[-2:]
        return pl.BlockSpec((*lead, rows // steps, width), lambda f: (0,) * len(lead) + (f, 0))

    return pl.pallas_call(
        functools.partial(place_kernel, seats),
        out_shape=jax.ShapeDtypeStruct((frames, seats * ROW_TILE, width), jnp.bfloat16),
        grid=(steps,),
        in_specs=[IN_SMEM]
        + [block(piece) for piece in pieces],
        out_specs=pl.BlockSpec((half, seats * ROW_TILE, width), lambda f: (f, 0, 0)),
        compiler_params=pltpu.CompilerParams(vmem_limit_bytes=VMEM_LIMIT),
    )(seat, *pieces)


def flip(value, axis, mask):
    pairs = [(source, source ^ mask) for source in range(lax.axis_size(axis))]
    return lax.ppermute(value, axis, pairs)


def half_weights(qkv, out_weight, core):
    stacked = jnp.concatenate([jnp.swapaxes(qkv, 1, 2), out_weight[None]], axis=0)
    return lax.dynamic_slice_in_dim(stacked, core * 2, 2, axis=0)


def z_pair(value, across):
    other = flip(value, "seq", lax.axis_size("seq") // 4)
    return jnp.where(
        across % 2 == 0,
        jnp.concatenate([value, other], axis=1),
        jnp.concatenate([other, value], axis=1),
    )


def over_middle(near):
    step = lax.axis_size("seq") // 4
    pairs = [
        pair
        for low in range(step)
        for pair in ((step + low, 2 * step + low), (2 * step + low, step + low))
    ]
    return lax.ppermute(near, "seq", pairs)


def to_ends(inside, across):
    step = lax.axis_size("seq") // 4
    pairs = [
        pair
        for low in range(step)
        for pair in ((step + low, low), (2 * step + low, 3 * step + low))
    ]
    outside = lax.ppermute(inside, "seq", pairs)
    return jnp.where((across == 1) | (across == 2), inside, outside)


NEAR = ((0, 0, 0), (0, 0, 1), (1, 0, 0), (1, 0, 1))
FAR = ((0, 1, 0), (0, 1, 1), (1, 1, 0), (1, 1, 1))


def own_layout():
    return [(index, None, 0, place) for index, place in enumerate(NEAR + FAR)]


def other_core(pieces):
    swapped = []
    for piece in pieces:
        if swapped:
            piece, swapped[-1] = together(piece, swapped[-1])
        swapped.append(flip(piece, "clip", 1))
    return swapped


def send(pieces):
    return [pieces[0]] + [flip(piece, "seq", i) for i, piece in enumerate(pieces) if i > 0]


def together(*groups):
    return lax.optimization_barrier(groups)


def along_line(neighbours):
    pieces = [
        jnp.stack([given[line] for given in neighbours])
        for line in range(neighbours[0].shape[0])
    ]
    return [flip(piece, "seq", 2 * i) if i > 0 else piece for i, piece in enumerate(pieces)]


def over_both(value):
    size = lax.axis_size("cfg") * lax.axis_size("seq")
    pairs = [(d, d ^ (size // 2 + 1)) for d in range(size)]
    return lax.ppermute(value, ("cfg", "seq"), pairs)


def to_neighbours(kept, low, across, both):
    return [kept, flip(low, "seq", 1), flip(across, "cfg", 1), over_both(both)]


def on_device(
    clean,
    noise,
    timestep,
    guidance,
    condition_vector,
    empty_prompt_vector,
    timestep_direction,
    spatial_query_key_value,
    spatial_output_weight,
    temporal_query_key_value,
    temporal_output_weight,
    adapter_down_maps,
    adapter_up_maps,
):
    sides, seats = lax.axis_size("cfg"), lax.axis_size("seq")
    side, place, core = (lax.axis_index(a) for a in ("cfg", "seq", "clip"))
    frames = clean.shape[0] * seats
    width = clean.shape[2]
    seat = jnp.stack([side, place, core]).astype(jnp.int32)
    moved = timestep[0] * timestep_direction.astype(jnp.float32)
    cond_shift = (moved + condition_vector.astype(jnp.float32))[None]
    uncond_shift = (moved + empty_prompt_vector.astype(jnp.float32))[None]
    down = jnp.swapaxes(adapter_down_maps, 1, 2).reshape(-1, width)
    up = adapter_up_maps.reshape(-1, sides, 2, 2, seats // 4, HEAD_DIM)
    up = jnp.swapaxes(up, 3, 4).reshape(-1, width)

    noisy_lines = noisy_pieces(seat, timestep, clean, noise, seats)
    space_own = half_weights(spatial_query_key_value, spatial_output_weight, core)
    time_own = half_weights(temporal_query_key_value, temporal_output_weight, core)
    across = place // (seats // 4)

    space_near = z_pair(space_own, across)
    space_near, time_own = together(space_near, time_own)
    space_in = over_middle(space_near)
    space = [space_near, flip(space_near, "seq", 1), flip(space_near, "cfg", 1)]
    time_near = z_pair(time_own, across)
    space_other = other_core([space_near])
    space, space_other, space_in, time_near = together(space, space_other, space_in, time_near)

    space_far = to_ends(space_in, across)
    space_xy = flip(space[2], "seq", 1)
    time_in = over_middle(time_near)
    time_x = flip(time_near, "cfg", 1)
    space_other += other_core(space[1:])
    space += [space_xy, space_far]
    space, space_other, time_in, time_x, time_near, noisy_lines, down, up = together(
        space, space_other, time_in, time_x, time_near, noisy_lines, down, up
    )

    space_far_x = flip(space[4], "cfg", 1)
    space_far_y = flip(space[4], "seq", 1)
    time_far = to_ends(time_in, across)
    space_xy_other, time_near_other = other_core([space[3], time_near])
    space += [space_far_y, space_far_x]
    space_other += [space_xy_other]
    time_other = [time_near_other]
    space, space_other, time_other, time_far, time_near, time_x, noisy_lines = together(
        space, space_other, time_other, time_far, time_near, time_x, noisy_lines
    )

    space_far_xy = flip(space[5], "cfg", 1)
    time_y = flip(time_near, "seq", 1)
    noisy_1 = flip(noisy_lines[1], "seq", 2)
    *space_far_other, time_x_other = other_core(space[4:] + [time_x])
    space.append(space_far_xy)
    space_other += space_far_other
    time_other += [time_x_other]
    space, space_other, time_x, time_y, time_far, time_near, time_other, noisy_came = together(
        space, space_other, time_x, time_y, time_far, time_near, time_other,
        [noisy_lines[0], noisy_1, *noisy_lines[2:]],
    )

    space_last, time_far_other, time_y_other = (
        flip(piece, "clip", 1) for piece in (space[7], time_far, time_y)
    )
    space_other += [space_last]
    time_other += [time_far_other, time_y_other]
    space, space_other, time_x, time_y, time_far, time_near, time_other, noisy_came = together(
        space, space_other, time_x, time_y, time_far, time_near, time_other, noisy_came
    )
    space_weights = (
        list(space) + list(space_other),
        [(index, None, index // 8, (NEAR + FAR)[index % 8]) for index in range(16)],
    )
    cond, uncond = [
        functools.partial(
            spatial_layer, seat, timestep, clean, noise, shift,
            frames=clean.shape[0] // sides, seats=seats,
        )
        for shift in (cond_shift, uncond_shift)
    ]
    time_xy = flip(time_y, "cfg", 1)
    time_far_x = flip(time_far, "cfg", 1)
    time_far_y = flip(time_far, "seq", 1)
    noisy_came = list(noisy_came[:2]) + [
        flip(line, "seq", 2 * index) for index, line in enumerate(noisy_came) if index > 1
    ]
    cond = cond(weights=space_weights)
    cond, time_xy, time_far_x, time_far_y, noisy_came = together(
        cond, time_xy, time_far_x, time_far_y, noisy_came
    )
    time_late = [flip(piece, "clip", 1) for piece in (time_xy, time_far_y, time_far_x)]
    noisy_low = jnp.stack([line[1] for line in noisy_came])
    cond, time_far_y, time_late, noisy_low = together(cond, time_far_y, time_late, noisy_low)
    uncond = uncond(weights=space_weights)
    time_far_xy = flip(time_far_y, "cfg", 1)
    noisy_low = flip(noisy_low, "seq", 1)
    cond, uncond, time_far_xy, noisy_low = together(
        to_neighbours(*cond), uncond, time_far_xy, noisy_low
    )
    lines = [jnp.stack([given[line] for given in cond]) for line in range(seats // 2)]
    far_lines = [flip(lines[i], "seq", 2 * i) for i in range(2, seats // 2)]
    time_last = flip(time_far_xy, "clip", 1)
    uncond, time_last = together(uncond, time_last)
    time_weights = (
        [time_near, time_y, time_x, time_xy, time_far, time_far_y, time_far_x, time_far_xy]
        + list(time_other) + list(time_late) + [time_last],
        [(index, None, 0, at) for index, at in enumerate(NEAR + FAR)]
        + [
            (8 + index, None, 1, at)
            for index, at in enumerate(
                [NEAR[0], NEAR[2], FAR[0], NEAR[1], NEAR[3], FAR[1], FAR[2], FAR[3]]
            )
        ],
    )
    noisy_in = list(noisy_came) + [noisy_low]
    kept, low, across, both = uncond
    low, across, both = flip(low, "seq", 1), flip(across, "cfg", 1), over_both(both)
    rows, primal = student_rows(seat, cond_shift, down, up, time_weights, noisy_in, frames)
    rows, primal, low, across, both, lines = together(rows, primal, low, across, both, lines)
    near_line = flip(lines[1], "seq", 2)
    uncond = along_line([kept, low, across, both])
    student_kept, student_low = student_mix(
        seat, cond_shift, rows, primal, time_weights, frames, seats
    )
    cond = [lines[0], near_line, *far_lines]
    student_kept, student_low, cond = together(student_kept, student_low, cond)
    velocity = teacher_velocity(seat, time_weights, cond, frames)
    student_low, velocity, uncond = together(flip(student_low, "seq", 1), velocity, uncond)
    student_back = along_line([student_kept, student_low])
    tangent = functools.partial(
        student_tangent, seat, guidance, cond_shift, down, up, velocity, rows, primal,
        time_weights, frames=frames, seats=seats,
    )
    *tangent_pieces, other = tangent(uncond)
    student_back, other, tangent_pieces = together(student_back, other, tangent_pieces)
    tangent_back = send(tangent_pieces)
    rest, tangent_back = together(tangent([other]), tangent_back)
    tangent_back = list(tangent_back) + send(rest)
    here = clean.shape[0]
    return placed(seat, student_back, seats, here), placed(seat, tangent_back, seats, here)


def fits(mesh, frames, positions, width):
    sides, seats = mesh.shape["cfg"], mesh.shape["seq"]
    groups = sides * seats
    return (
        sides == 2
        and mesh.shape["clip"] == 2
        and seats == 4 * sides
        and frames % (groups * ROW_TILE // 4) == 0
        and frames // groups % PAIR == 0
        and positions == groups * ROW_TILE
        and 2 * frames == LANES
        and width % LANES == 0
        and width == groups * HEAD_DIM
    )

def solution(mesh):
    specs = dict(
        mesh=mesh,
        in_specs=(
            P(("clip", "seq"), None, None),
            P(("clip", "seq"), None, None),
            P("clip"),
            P("clip"),
            P("clip"),
            P(),
            P(),
            P(None, None, ("cfg", "seq")),
            P(("cfg", "seq"), None),
            P(None, None, ("cfg", "seq")),
            P(("cfg", "seq"), None),
            P(),
            P(),
        ),
        out_specs=(P(("clip", "seq"), "cfg", None), P(("clip", "seq"), "cfg", None)),
        check_vma=False,
    )

    def whole(clean, *rest):
        frames = clean.shape[0] // mesh.shape["clip"]
        fast = fits(mesh, frames, clean.shape[1], clean.shape[2])
        return jax.shard_map(on_device if fast else plain_on_device, **specs)(clean, *rest)

    return whole
```

```python
import functools
import math

import jax
import jax.numpy as jnp
from jax import lax
from jax.experimental import pallas as pl
from jax.experimental.pallas import tpu as pltpu
from jax.sharding import PartitionSpec as P

HEAD_DIM = 72
LANES = 128
ROW_TILE = 16
BLOCK = 8
EXPONENT_SCALE = HEAD_DIM ** (-0.5) * math.log2(math.e)
VMEM_LIMIT = 40 * 1024 * 1024
SPACE_VMEM_LIMIT = 26 * 1024 * 1024
TANGENT_VMEM_LIMIT = 60 * 1024 * 1024

epsilon = 1e-06


def partner(value, axis, bit):
    mask = 2**bit
    pairs = [(source, source ^ mask) for source in range(lax.axis_size(axis))]
    return lax.ppermute(value, axis, pairs)


def rms_scale(features):
    return features * lax.rsqrt(jnp.mean(features * features, axis=-1, keepdims=True) + epsilon)


def project(rows_in, matrix):
    return jnp.einsum("...d,dk->...k", rows_in, matrix, preferred_element_type=jnp.float32)


def space_attend(queries, key_rows, value_rows):
    head_count = queries.shape[-1] // HEAD_DIM
    split_dims = queries.shape[:-1] + (head_count, HEAD_DIM)
    scores = jnp.einsum(
        "...qhd,...khd->...hqk",
        queries.reshape(split_dims),
        key_rows.reshape(split_dims),
        preferred_element_type=jnp.float32,
    ) * HEAD_DIM ** (-0.5)
    scores = scores - jnp.max(scores, axis=-1, keepdims=True)
    exponent = jnp.exp(scores)
    soft_weights = (exponent / jnp.sum(exponent, axis=-1, keepdims=True)).astype(jnp.bfloat16)
    result = jnp.einsum(
        "...hqk,...khd->...qhd",
        soft_weights,
        value_rows.reshape(split_dims),
        preferred_element_type=jnp.float32,
    )
    return result.astype(jnp.bfloat16).reshape(queries.shape)


def time_attend(queries, key_rows, value_rows):
    head_count = queries.shape[-1] // HEAD_DIM
    split_dims = queries.shape[:-1] + (head_count, HEAD_DIM)
    scores = jnp.einsum(
        "...fxhd,...gxhd->...xhfg",
        queries.reshape(split_dims),
        key_rows.reshape(split_dims),
        preferred_element_type=jnp.float32,
    ) * HEAD_DIM ** (-0.5)
    scores = scores - jnp.max(scores, axis=-1, keepdims=True)
    exponent = jnp.exp(scores)
    soft_weights = (exponent / jnp.sum(exponent, axis=-1, keepdims=True)).astype(jnp.bfloat16)
    result = jnp.einsum(
        "...xhfg,...gxhd->...fxhd",
        soft_weights,
        value_rows.reshape(split_dims),
        preferred_element_type=jnp.float32,
    )
    return result.astype(jnp.bfloat16).reshape(queries.shape)


def time_core(embedding_rows, query_weight, key_weight, value_weight, out_weight):
    normed = rms_scale(embedding_rows).astype(jnp.bfloat16)
    queries = project(normed, query_weight).astype(jnp.bfloat16)
    key_rows = project(normed, key_weight).astype(jnp.bfloat16)
    value_rows = project(normed, value_weight).astype(jnp.bfloat16)
    return project(time_attend(queries, key_rows, value_rows), out_weight)


def student_network(
    embedding_rows,
    query_weight,
    key_weight,
    value_weight,
    out_weight,
    down_query,
    query_up_map,
    down_value,
    value_up_map,
):
    normed = rms_scale(embedding_rows).astype(jnp.bfloat16)
    low_query = project(normed, down_query).astype(jnp.bfloat16)
    low_value = project(normed, down_value).astype(jnp.bfloat16)
    queries = (project(normed, query_weight) + project(low_query, query_up_map)).astype(
        jnp.bfloat16
    )
    key_rows = project(normed, key_weight).astype(jnp.bfloat16)
    value_rows = (project(normed, value_weight) + project(low_value, value_up_map)).astype(
        jnp.bfloat16
    )
    return project(time_attend(queries, key_rows, value_rows), out_weight)


def plain_on_device(
    clean,
    noise,
    timestep,
    guidance,
    condition_vector,
    empty_prompt_vector,
    timestep_direction,
    spatial_query_key_value,
    spatial_output_weight,
    temporal_query_key_value,
    temporal_output_weight,
    adapter_down_maps,
    adapter_up_maps,
):
    moment = timestep[0]
    strength = guidance[0]
    pair_side = lax.axis_index("cfg")
    noisy_rows = (
        (1.0 - moment) * clean.astype(jnp.float32) + moment * noise.astype(jnp.float32)
    ).astype(jnp.bfloat16)
    shifted = noisy_rows.astype(jnp.float32) + moment * timestep_direction.astype(jnp.float32)
    embeds = jnp.where(pair_side == 0, condition_vector, empty_prompt_vector)[None]
    branch_count = embeds.shape[0]
    entries = shifted[None] + embeds.astype(jnp.float32)[:, None, None, :]
    normed = rms_scale(entries).astype(jnp.bfloat16)
    triple = jnp.einsum(
        "bfpd,jdk->jbfpk",
        normed,
        lax.all_gather(spatial_query_key_value, ("cfg", "seq"), axis=2, tiled=True),
        preferred_element_type=jnp.float32,
    ).astype(jnp.bfloat16)
    attended = space_attend(triple[0], triple[1], triple[2])
    partial_value = jnp.einsum(
        "bfpk,kd->bfpd",
        attended,
        lax.all_gather(spatial_output_weight, ("cfg", "seq"), axis=0, tiled=True),
        preferred_element_type=jnp.float32,
    )
    layer_one = (entries + partial_value).astype(jnp.bfloat16)
    frame_count = layer_one.shape[1]
    position_count = layer_one.shape[2]
    width = layer_one.shape[3]
    stacked = jnp.concatenate([layer_one, noisy_rows[None]], axis=0).reshape(
        branch_count + 1, frame_count, 2, position_count // 2, width
    )
    regrouped = lax.all_to_all(stacked, "seq", split_axis=3, concat_axis=1, tiled=True)
    frames = regrouped.shape[1]
    local_rows = regrouped.shape[3]
    teacher_in = regrouped[:branch_count].reshape(branch_count, frames, 2 * local_rows, width)
    noisy_local = regrouped[branch_count]
    time_qkv, time_out = (
        lax.all_gather(temporal_query_key_value, ("cfg", "seq"), axis=2, tiled=True),
        lax.all_gather(temporal_output_weight, ("cfg", "seq"), axis=0, tiled=True),
    )
    teacher_part = time_core(
        teacher_in.astype(jnp.float32), time_qkv[0], time_qkv[1], time_qkv[2], time_out
    )
    velocity = (
        (teacher_in.astype(jnp.float32) + teacher_part)
        .astype(jnp.bfloat16)
        .reshape(branch_count, frames, 2, local_rows, width)
    )
    own_velocity = velocity[0]
    own_half = lax.dynamic_index_in_dim(own_velocity, pair_side, 1, keepdims=False)
    outgoing = lax.dynamic_index_in_dim(own_velocity, 1 - pair_side, 1, keepdims=False)
    other_half = partner(outgoing, "cfg", 0)
    is_first = pair_side == 0
    cond_velocity = jnp.where(is_first, own_half, other_half)
    uncond_velocity = jnp.where(is_first, other_half, own_half)
    student_noisy = lax.dynamic_index_in_dim(noisy_local, pair_side, 1, keepdims=False)
    query_up_map = adapter_up_maps[0]
    value_up_map = adapter_up_maps[1]
    uncond_float = uncond_velocity.astype(jnp.float32)
    guided = (uncond_float + strength * (cond_velocity.astype(jnp.float32) - uncond_float)).astype(
        jnp.bfloat16
    )
    student_in = (
        student_noisy.astype(jnp.float32)
        + moment * timestep_direction.astype(jnp.float32)
        + condition_vector.astype(jnp.float32)
    )

    def student_map(embedding_rows):
        return student_network(
            embedding_rows,
            time_qkv[0],
            time_qkv[1],
            time_qkv[2],
            time_out,
            adapter_down_maps[0],
            query_up_map,
            adapter_down_maps[1],
            value_up_map,
        )

    partial_value, tangent_part = jax.jvp(student_map, (student_in,), (guided.astype(jnp.float32),))
    primal = (student_in + partial_value).astype(jnp.bfloat16)
    tangent = (guided.astype(jnp.float32) + tangent_part).astype(jnp.bfloat16)
    returned = lax.all_to_all(
        jnp.stack([primal, tangent]), "seq", split_axis=1, concat_axis=2, tiled=True
    )
    return (returned[0], returned[1])


def dot(left, right):
    return lax.dot_general(
        left, right, (((1,), (0,)), ((), ())), preferred_element_type=jnp.float32
    )


def dot_t(left, right):
    return lax.dot_general(
        left, right, (((1,), (1,)), ((), ())), preferred_element_type=jnp.float32
    )


def lane_range(shape, start, low, high):
    lane = lax.broadcasted_iota(jnp.int32, shape, len(shape) - 1) + start
    return (lane >= low) & (lane < high)


def only(value, keep):
    return jnp.where(keep, value, jnp.zeros_like(value))


def window_of(low, high):
    start = low // LANES * LANES
    return start, -(-high // LANES) * LANES - start


def inverse_rms(features):
    return lax.rsqrt(jnp.mean(features * features, axis=-1, keepdims=True) + epsilon)


def weight_copies(seat, layout, pieces, weights_ref, sems):
    side, place, core = seat[0], seat[1], seat[2]
    across, along = place // 4, lax.rem(place, 2)
    copies = []
    for array, part, sibling, (x, z, y) in layout:
        piece = pieces[array] if part is None else pieces[array].at[part]
        count, rows = piece.shape[:2]
        block = ((side ^ x) * 2 + (across ^ z)) * 2 + (along ^ y)
        start = pl.multiple_of(block * rows, ROW_TILE)
        copies.append(
            pltpu.make_async_copy(
                piece,
                weights_ref.at[pl.ds((core ^ sibling) * count, count), pl.ds(start, rows), :],
                sems.at[len(copies)],
            )
        )
    return copies


def noisy_kernel(seat_ref, moment_ref, clean_ref, noise_ref, *rest):
    line_refs, rows_ref = rest[:-1], rest[-1]
    moment = moment_ref[0]
    rows_ref[...] = (
        (1.0 - moment) * clean_ref[0].astype(jnp.float32)
        + moment * noise_ref[0].astype(jnp.float32)
    ).astype(jnp.bfloat16)
    for index in range(2 * len(line_refs)):
        start = pl.multiple_of((seat_ref[1] ^ index) * ROW_TILE, ROW_TILE)
        line_refs[index // 2][index % 2, 0] = rows_ref[pl.ds(start, ROW_TILE), :]


def noisy_pieces(seat, moment, clean, noise, seats):
    frames, positions, width = clean.shape
    rows = seats * ROW_TILE
    block = pl.BlockSpec((1, rows, width), lambda f, seat: (f, seat[0], 0))
    half = seats // 2
    piece = jax.ShapeDtypeStruct((2, frames, ROW_TILE, width), jnp.bfloat16)
    out_block = pl.BlockSpec((2, 1, ROW_TILE, width), lambda f, seat: (0, f, 0, 0))
    return pl.pallas_call(
        noisy_kernel,
        out_shape=[piece] * half,
        grid_spec=pltpu.PrefetchScalarGridSpec(
            num_scalar_prefetch=1,
            grid=(frames,),
            in_specs=[pl.BlockSpec(memory_space=pltpu.SMEM), block, block],
            out_specs=[out_block] * half,
            scratch_shapes=[pltpu.VMEM((rows, width), jnp.bfloat16)],
        ),
        compiler_params=pltpu.CompilerParams(vmem_limit_bytes=VMEM_LIMIT),
    )(seat, moment, clean, noise)


def space_kernel(layout, pieces, targets, seat_ref, moment_ref, clean_ref, noise_ref, shift_ref, *rest):
    weight_pieces, sent_refs = rest[:pieces], rest[pieces : pieces + targets]
    weights_ref, query_ref, key_ref, value_ref, mixed_ref, sems = rest[pieces + targets :]
    moment = moment_ref[0]
    positions, width = key_ref.shape

    @pl.when(pl.program_id(0) == 0)
    def _():
        wait_all(start_all(weight_copies(seat_ref, layout, weight_pieces, weights_ref, sems)))

    noisy = (
        (1.0 - moment) * clean_ref[0].astype(jnp.float32)
        + moment * noise_ref[0].astype(jnp.float32)
    ).astype(jnp.bfloat16)
    entry = noisy.astype(jnp.float32) + shift_ref[...]
    normed = (entry * inverse_rms(entry)).astype(jnp.bfloat16)
    query_ref[...] = dot_t(normed, weights_ref[0]).astype(jnp.bfloat16)
    key_ref[...] = dot_t(normed, weights_ref[1]).astype(jnp.bfloat16)
    value_ref[...] = dot_t(normed, weights_ref[2]).astype(jnp.bfloat16)

    weights = []
    for head in range(width // HEAD_DIM):
        low, high = head * HEAD_DIM, (head + 1) * HEAD_DIM
        start, extent = window_of(low, high)
        keep = lane_range((positions, extent), start, low, high)
        queries = only(query_ref[:, pl.ds(start, extent)], keep)
        scores = dot_t(queries, key_ref[:, pl.ds(start, extent)])
        top = jnp.max(scores, axis=-1, keepdims=True)
        exponent = jnp.exp2((scores - top) * EXPONENT_SCALE)
        total = jnp.sum(exponent, axis=-1, keepdims=True)
        weights.append((exponent * (1.0 / total)).astype(jnp.bfloat16))
        tile = high // (2 * LANES)
        done = [low // (2 * LANES)] if tile > low // (2 * LANES) else []
        if head == width // HEAD_DIM - 1:
            done = [(width - 1) // (2 * LANES)]
        for full in done:
            left_edge = full * 2 * LANES
            edge = min(width, left_edge + 2 * LANES)
            heads = range(left_edge // HEAD_DIM, -(-edge // HEAD_DIM))
            values = value_ref[:, pl.ds(left_edge, edge - left_edge)]
            parts = [
                only(
                    values,
                    lane_range(values.shape, left_edge, h * HEAD_DIM, (h + 1) * HEAD_DIM),
                )
                for h in heads
            ]
            mixed = dot(
                jnp.concatenate([weights[h] for h in heads], axis=1),
                jnp.concatenate(parts, axis=0),
            )
            mixed_ref[:, pl.ds(left_edge, edge - left_edge)] = mixed.astype(jnp.bfloat16)

    query_ref[...] = (entry + dot(mixed_ref[...], weights_ref[3])).astype(jnp.bfloat16)
    lines = sent_refs[0].shape[0]
    for index, ref in enumerate(sent_refs):
        for line in range(lines):
            seat = (seat_ref[0] ^ (index // 2)) * lines * 2 + (
                seat_ref[1] ^ (line * 2 + index % 2)
            )
            start = pl.multiple_of(seat * ROW_TILE, ROW_TILE)
            ref[line, 0] = query_ref[pl.ds(start, ROW_TILE), :]


def spatial_layer(seat, moment, clean, noise, shift, weights, frames, seats):
    pieces, layout = weights
    positions, width = clean.shape[1:]
    frame_block = pl.BlockSpec(
        (1, positions, width), lambda f, seat: (seat[0] * frames + f, 0, 0)
    )
    lines = seats // 2
    piece = jax.ShapeDtypeStruct((lines, frames, ROW_TILE, width), jnp.bfloat16)
    vmem = lambda *shape: pltpu.VMEM(shape, jnp.bfloat16)
    rows = frames * positions
    return pl.pallas_call(
        functools.partial(space_kernel, layout, len(pieces), 4),
        out_shape=[piece] * 4,
        grid_spec=pltpu.PrefetchScalarGridSpec(
            num_scalar_prefetch=1,
            grid=(frames,),
            in_specs=[
                pl.BlockSpec(memory_space=pltpu.SMEM),
                frame_block,
                frame_block,
                pl.BlockSpec(shift.shape, lambda f, seat: (0, 0)),
            ]
            + [pl.BlockSpec(memory_space=pl.ANY)] * len(pieces),
            out_specs=[
                pl.BlockSpec((lines, 1, ROW_TILE, width), lambda f, seat: (0, f, 0, 0))
            ]
            * 4,
            scratch_shapes=[vmem(4, width, width)]
            + [vmem(positions, width)] * 4
            + [pltpu.SemaphoreType.DMA((len(layout),))],
        ),
        compiler_params=pltpu.CompilerParams(vmem_limit_bytes=SPACE_VMEM_LIMIT),
        cost_estimate=pl.CostEstimate(
            flops=14 * rows * width * width,
            bytes_accessed=8 * width * width + 6 * rows * width,
            transcendentals=rows * positions * width // HEAD_DIM,
        ),
    )(seat, moment, clean, noise, shift, *pieces)


def swap_matrix(rows, columns):
    count = rows * columns
    target = lax.broadcasted_iota(jnp.int32, (count, count), 0)
    source = lax.broadcasted_iota(jnp.int32, (count, count), 1)
    moved = lax.rem(target, rows) * columns + lax.div(target, rows)
    return jnp.where(source == moved, 1.0, 0.0).astype(jnp.bfloat16)


def halves(value, frames, reduce):
    first = lane_range(value.shape, 0, 0, frames)
    if reduce == "max":
        low = jnp.max(jnp.where(first, value, -jnp.inf), axis=-1, keepdims=True)
        high = jnp.max(jnp.where(first, -jnp.inf, value), axis=-1, keepdims=True)
    else:
        low = jnp.sum(jnp.where(first, value, 0.0), axis=-1, keepdims=True)
        high = jnp.sum(jnp.where(first, 0.0, value), axis=-1, keepdims=True)
    return first, low, high


def time_mix(frames, refs, tangents=None):
    query_ref, key_ref, value_ref, mixed_ref = refs
    rows, width = query_ref.shape
    scale = HEAD_DIM ** (-0.5)
    tiles = [[] for _ in range(width // LANES)]
    tangent_tiles = [[] for _ in range(width // LANES)]
    pairs = width // (2 * HEAD_DIM)
    blocks = [pl.ds(i * frames, frames) for i in range(rows // frames)]

    def stack(value, start, low):
        shape = value.shape
        return jnp.concatenate(
            [
                only(value, lane_range(shape, start, low, low + HEAD_DIM)),
                only(value, lane_range(shape, start, low + HEAD_DIM, low + 2 * HEAD_DIM)),
            ],
            axis=0,
        )

    for pair in range(pairs):
        low = pair * 2 * HEAD_DIM
        start, extent = window_of(low, low + 2 * HEAD_DIM)
        columns = pl.ds(start, extent)
        keys = [stack(key_ref[b, columns], start, low) for b in blocks]
        values = [stack(value_ref[b, columns], start, low) for b in blocks]
        scores = jnp.concatenate(
            [dot_t(query_ref[b, columns], k) for b, k in zip(blocks, keys)], axis=0
        )
        first, top_low, top_high = halves(scores, frames, "max")
        exponent = jnp.exp2((scores - jnp.where(first, top_low, top_high)) * EXPONENT_SCALE)
        _, sum_low, sum_high = halves(exponent, frames, "sum")
        weights = exponent * jnp.where(first, 1.0 / sum_low, 1.0 / sum_high)
        rounded = weights.astype(jnp.bfloat16)
        mixed = jnp.concatenate(
            [
                dot(rounded[i * frames : (i + 1) * frames], v)
                for i, v in enumerate(values)
            ],
            axis=0,
        )
        for tile in range(extent // LANES):
            tiles[start // LANES + tile].append(mixed[:, tile * LANES : (tile + 1) * LANES])
        if tangents is not None:
            query_dot, key_dot, value_dot, _ = tangents
            score_dots = jnp.concatenate(
                [
                    dot_t(query_dot[b, columns], k)
                    + dot_t(query_ref[b, columns], stack(key_dot[b, columns], start, low))
                    for b, k in zip(blocks, keys)
                ],
                axis=0,
            ) * scale
            _, mean_low, mean_high = halves(weights * score_dots, frames, "sum")
            weight_dots = (
                weights * (score_dots - jnp.where(first, mean_low, mean_high))
            ).astype(jnp.bfloat16)
            mixed_dots = jnp.concatenate(
                [
                    dot(
                        jnp.concatenate(
                            [
                                weight_dots[i * frames : (i + 1) * frames],
                                rounded[i * frames : (i + 1) * frames],
                            ],
                            axis=1,
                        ),
                        jnp.concatenate(
                            [v, stack(value_dot[b, columns], start, low)], axis=0
                        ),
                    )
                    for i, (b, v) in enumerate(zip(blocks, values))
                ],
                axis=0,
            )
            for tile in range(extent // LANES):
                tangent_tiles[start // LANES + tile].append(
                    mixed_dots[:, tile * LANES : (tile + 1) * LANES]
                )
    for tile in range(width // LANES):
        columns = pl.ds(tile * LANES, LANES)
        mixed_ref[:, columns] = functools.reduce(jnp.add, tiles[tile]).astype(jnp.bfloat16)
        if tangents is not None:
            tangents[3][:, columns] = functools.reduce(jnp.add, tangent_tiles[tile]).astype(
                jnp.bfloat16
            )


def arrivals(seat, pieces, came_ref, sems):
    copies = []
    for line, piece in enumerate(pieces):
        neighbours, frames = piece.shape[:2]
        for index in range(neighbours):
            first = (seat[1] ^ (line * 2 + index % 2)) * frames * (neighbours // 2)
            if neighbours > 2:
                first = first + (seat[0] ^ (index // 2)) * frames
            copies.append(
                pltpu.make_async_copy(
                    piece.at[index], came_ref.at[pl.ds(first, frames)], sems.at[len(copies)]
                )
            )
    return copies


def departures(seat, going_ref, pieces, sems):
    rows = pieces[0].shape[0]
    return [
        pltpu.make_async_copy(
            going_ref.at[pl.ds(pl.multiple_of((seat[1] ^ index) * rows, ROW_TILE), rows)],
            piece,
            sems.at[index],
        )
        for index, piece in enumerate(pieces)
    ]


def by_position(came_ref, rows_ref):
    frames, positions, width = came_ref.shape
    turn = swap_matrix(ROW_TILE, positions)
    for part in range(frames // ROW_TILE):
        first = part * ROW_TILE
        piece = came_ref[first : first + ROW_TILE].reshape(ROW_TILE * positions, width)
        turned = dot(turn, piece).astype(jnp.bfloat16)
        for position in range(positions):
            rows_ref[pl.ds(position * frames + first, ROW_TILE), :] = turned[
                position * ROW_TILE : (position + 1) * ROW_TILE
            ]


def by_frame(rows_ref, going_ref, frames):
    positions = rows_ref.shape[0] // frames
    group = min(frames, 2 * LANES // positions)
    turn = swap_matrix(positions, group)
    for part in range(frames // group):
        piece = jnp.concatenate(
            [rows_ref[pl.ds(p * frames + part * group, group), :] for p in range(positions)],
            axis=0,
        )
        here = pl.ds(part * group * positions, group * positions)
        going_ref[here, :] = dot(turn, piece).astype(jnp.bfloat16)


def wait_all(copies):
    for copy in copies:
        copy.wait()


def start_all(copies):
    for copy in copies:
        copy.start()
    return copies


def adapted(rows_in, weights_ref, down_ref, up_ref, refs):
    rank = down_ref.shape[0] // 2
    low = dot_t(rows_in, down_ref[...]).astype(jnp.bfloat16)
    first = lane_range(low.shape, 0, 0, rank)
    refs[0][...] = (
        dot_t(rows_in, weights_ref[0]) + dot(only(low, first), up_ref[...])
    ).astype(jnp.bfloat16)
    refs[1][...] = dot_t(rows_in, weights_ref[1]).astype(jnp.bfloat16)
    refs[2][...] = (
        dot_t(rows_in, weights_ref[2]) + dot(only(low, jnp.logical_not(first)), up_ref[...])
    ).astype(jnp.bfloat16)


def student_rows_kernel(layout, counts, seat_ref, shift_ref, down_ref, up_ref, *rest):
    weight_count, piece_count = counts
    weight_pieces, rest = rest[:weight_count], rest[weight_count:]
    pieces, rest = rest[:piece_count], rest[piece_count:]
    rows_out_ref, primal_ref, weights_ref, came_ref, rows_ref, weight_sems, piece_sems = rest
    chunk = rows_out_ref.shape[0]

    @pl.when(pl.program_id(0) == 0)
    def _():
        weights = weight_copies(seat_ref, layout, weight_pieces, weights_ref, weight_sems)
        lines = piece_count - 1
        copies = []
        for index in range(2 * lines):
            piece = pieces[lines].at[index // 2] if index % 2 else pieces[index // 2].at[0]
            count = piece.shape[0]
            copies.append(
                pltpu.make_async_copy(
                    piece,
                    came_ref.at[pl.ds((seat_ref[1] ^ index) * count, count)],
                    piece_sems.at[index],
                )
            )
        start_all(copies)
        start_all(weights)
        wait_all(copies)
        by_position(came_ref, rows_ref)
        wait_all(weights)

    here = pl.ds(pl.multiple_of(pl.program_id(0) * chunk, chunk), chunk)
    rows_out_ref[...] = rows_ref[here, :]
    entry = rows_ref[here, :].astype(jnp.float32) + shift_ref[...]
    normed = (entry * inverse_rms(entry)).astype(jnp.bfloat16)
    adapted(normed, weights_ref, down_ref, up_ref, [primal_ref.at[i] for i in range(3)])


def student_mix_kernel(layout, frames, seat_ref, shift_ref, rows_ref, primal_ref, *rest):
    weight_pieces, out_refs, rest = rest[:-7], rest[-7:-5], rest[-5:]
    weights_ref, done_ref, mixed_ref, weight_sems, piece_sems = rest
    step, chunk = pl.program_id(0), mixed_ref.shape[0]
    weights = weight_copies(seat_ref, layout, weight_pieces, weights_ref, weight_sems)

    @pl.when(step == 0)
    def _():
        start_all(weights)

    time_mix(frames, [primal_ref.at[i] for i in range(3)] + [mixed_ref])

    @pl.when(step == 0)
    def _():
        wait_all(weights)

    here = pl.ds(pl.multiple_of(step * chunk, chunk), chunk)
    entry = rows_ref[...].astype(jnp.float32) + shift_ref[...]
    done_ref[0, here, :] = (entry + dot(mixed_ref[...], weights_ref[3])).astype(jnp.bfloat16)

    @pl.when(step == pl.num_programs(0) - 1)
    def _():
        by_frame(done_ref.at[0], done_ref.at[1], frames)
        pieces = [ref.at[line] for line in range(out_refs[0].shape[0]) for ref in out_refs]
        wait_all(start_all(departures(seat_ref, done_ref.at[1], pieces, piece_sems)))


def teacher(frames, rows_ref, weights_ref, refs, here):
    entry = rows_ref[here, :].astype(jnp.float32)
    normed = (entry * inverse_rms(entry)).astype(jnp.bfloat16)
    for index, ref in enumerate(refs[:3]):
        ref[...] = dot_t(normed, weights_ref[index]).astype(jnp.bfloat16)
    time_mix(frames, refs)
    entry = rows_ref[here, :].astype(jnp.float32)
    return (entry + dot(refs[3][...], weights_ref[3])).astype(jnp.bfloat16)


def teacher_kernel(layout, counts, seat_ref, *rest):
    weight_count, piece_count = counts
    weight_pieces, rest = rest[:weight_count], rest[weight_count:]
    pieces, rest = rest[:piece_count], rest[piece_count:]
    velocity_ref, weights_ref, came_ref, rows_ref = rest[:4]
    refs, (weight_sems, piece_sems) = rest[4:8], rest[8:]
    frames = came_ref.shape[0]
    chunk = refs[0].shape[0]

    @pl.when(pl.program_id(0) == 0)
    def _():
        came = start_all(arrivals(seat_ref, pieces, came_ref, piece_sems))
        weights = start_all(
            weight_copies(seat_ref, layout, weight_pieces, weights_ref, weight_sems)
        )
        wait_all(came)
        by_position(came_ref, rows_ref)
        wait_all(weights)

    here = pl.ds(pl.multiple_of(pl.program_id(0) * chunk, chunk), chunk)
    velocity_ref[...] = teacher(frames, rows_ref, weights_ref, refs, here)


def tangent_kernel(layout, counts, seat_ref, strength_ref, shift_ref, down_ref, up_ref, *rest):
    weight_count, piece_count, out_count = counts
    velocity_ref, noisy_ref, primal_ref = rest[:3]
    rest = rest[3:]
    weight_pieces, rest = rest[:weight_count], rest[weight_count:]
    pieces, rest = rest[:piece_count], rest[piece_count:]
    out_pieces, rest = rest[:out_count], rest[out_count:]
    weights_ref, done_ref, going_ref, guided_ref, *tail = rest[-14:]
    refs, dots, (weight_sems, piece_sems) = tail[:4], tail[4:8], tail[8:10]
    frames = done_ref.shape[0] // (ROW_TILE // 2)
    chunk = refs[0].shape[0]
    step = pl.program_id(0)
    first = piece_count > 1

    @pl.when(step == 0)
    def _():
        weights = weight_copies(seat_ref, layout, weight_pieces, weights_ref, weight_sems)
        if first:
            other_ref, came_ref, rows_ref = rest[:3]
            came = start_all(arrivals(seat_ref, pieces, came_ref, piece_sems))
        start_all(weights)
        if first:
            wait_all(came)
            by_position(came_ref, rows_ref)
            half = other_ref.shape[0]
            other_ref[...] = rows_ref[pl.ds(half, half), :]
        wait_all(weights)

    here = pl.ds(pl.multiple_of(step * chunk, chunk), chunk)
    rows_ref = rest[2].at[here] if first else pieces[0]
    uncond = teacher(frames, rows_ref, weights_ref, refs, slice(None)).astype(jnp.float32)
    guided = (
        uncond + strength_ref[0] * (velocity_ref[...].astype(jnp.float32) - uncond)
    ).astype(jnp.bfloat16)
    guided_ref[...] = guided
    guided = guided.astype(jnp.float32)
    entry = noisy_ref[...].astype(jnp.float32) + shift_ref[...]
    inverse = inverse_rms(entry)
    inverse_dot = -(inverse * inverse * inverse) * jnp.mean(
        entry * guided, axis=-1, keepdims=True
    )
    normed_dot = (guided * inverse + entry * inverse_dot).astype(jnp.bfloat16)
    adapted(normed_dot, weights_ref, down_ref, up_ref, dots)
    primal = [primal_ref.at[i] for i in range(3)] + [refs[3]]
    time_mix(frames, primal, dots)
    done_ref[here, :] = (
        guided_ref[...].astype(jnp.float32) + dot(dots[3][...], weights_ref[3])
    ).astype(jnp.bfloat16)

    @pl.when(step == pl.num_programs(0) - 1)
    def _():
        by_frame(done_ref, going_ref, frames)
        wait_all(start_all(departures(seat_ref, going_ref, out_pieces, piece_sems)))


IN_VMEM = pl.BlockSpec(memory_space=pltpu.VMEM)
IN_SMEM = pl.BlockSpec(memory_space=pltpu.SMEM)
ANYWHERE = pl.BlockSpec(memory_space=pl.ANY)


def time_call(kernel, passes, rows, width, limit=VMEM_LIMIT, **settings):
    return pl.pallas_call(
        kernel,
        compiler_params=pltpu.CompilerParams(vmem_limit_bytes=limit),
        cost_estimate=pl.CostEstimate(
            flops=int(12 * passes * rows * width * width),
            bytes_accessed=8 * width * width + 8 * rows * width,
            transcendentals=rows * LANES * width // HEAD_DIM,
        ),
        **settings,
    )


def student_rows(seat, shift, down, up, weights, pieces, frames):
    weights, layout = weights
    width = shift.shape[-1]
    rows, chunk = frames * ROW_TILE, BLOCK * frames
    vmem = lambda *shape: pltpu.VMEM(shape, jnp.bfloat16)
    fixed = lambda value: pl.BlockSpec(value.shape, lambda i: (0,) * value.ndim)
    return time_call(
        functools.partial(student_rows_kernel, layout, (len(weights), len(pieces))),
        0.6,
        rows,
        width,
        grid=(rows // chunk,),
        out_shape=[
            jax.ShapeDtypeStruct((rows, width), jnp.bfloat16),
            jax.ShapeDtypeStruct((3, rows, width), jnp.bfloat16),
        ],
        in_specs=[IN_SMEM, fixed(shift), fixed(down), fixed(up)]
        + [ANYWHERE] * (len(weights) + len(pieces)),
        out_specs=[
            pl.BlockSpec((chunk, width), lambda i: (i, 0)),
            pl.BlockSpec((3, chunk, width), lambda i: (0, i, 0)),
        ],
        scratch_shapes=[
            vmem(4, width, width),
            vmem(frames, ROW_TILE, width),
            vmem(rows, width),
            pltpu.SemaphoreType.DMA((len(layout),)),
            pltpu.SemaphoreType.DMA((2 * len(pieces),)),
        ],
    )(seat, shift, down, up, *weights, *pieces)


def student_mix(seat, shift, rows_in, primal, weights, frames, seats):
    weights, layout = weights
    rows, width = rows_in.shape
    chunk = BLOCK * frames
    vmem = lambda *shape: pltpu.VMEM(shape, jnp.bfloat16)
    piece = jax.ShapeDtypeStruct((seats // 2, rows // seats, width), jnp.bfloat16)
    return time_call(
        functools.partial(student_mix_kernel, layout, frames),
        0.6,
        rows,
        width,
        grid=(rows // chunk,),
        out_shape=[piece] * 2,
        in_specs=[
            IN_SMEM,
            pl.BlockSpec(shift.shape, lambda i: (0, 0)),
            pl.BlockSpec((chunk, width), lambda i: (i, 0)),
            pl.BlockSpec((3, chunk, width), lambda i: (0, i, 0)),
        ]
        + [ANYWHERE] * len(weights),
        out_specs=[ANYWHERE] * 2,
        scratch_shapes=[
            vmem(4, width, width),
            vmem(2, rows, width),
            vmem(chunk, width),
            pltpu.SemaphoreType.DMA((len(layout),)),
            pltpu.SemaphoreType.DMA((seats,)),
        ],
    )(seat, shift, rows_in, primal, *weights)


def teacher_velocity(seat, weights, pieces, frames):
    weights, layout = weights
    width = pieces[0].shape[-1]
    rows = frames * ROW_TILE
    vmem = lambda *shape: pltpu.VMEM(shape, jnp.bfloat16)
    return time_call(
        functools.partial(teacher_kernel, layout, (len(weights), len(pieces))),
        1,
        rows,
        width,
        out_shape=jax.ShapeDtypeStruct((rows, width), jnp.bfloat16),
        grid=(ROW_TILE // BLOCK,),
        in_specs=[IN_SMEM] + [ANYWHERE] * (len(weights) + len(pieces)),
        out_specs=pl.BlockSpec((BLOCK * frames, width), lambda i: (i, 0)),
        scratch_shapes=[
            vmem(4, width, width),
            vmem(frames, ROW_TILE, width),
            vmem(rows, width),
        ]
        + [vmem(BLOCK * frames, width)] * 4
        + [
            pltpu.SemaphoreType.DMA((len(layout),)),
            pltpu.SemaphoreType.DMA((4 * len(pieces),)),
        ],
    )(seat, *weights, *pieces)


def student_tangent(
    seat, strength, shift, down, up, velocity, noisy, primal, weights, pieces, frames, seats
):
    weights, layout = weights
    first = len(pieces) > 1
    width = shift.shape[-1]
    rows = frames * ROW_TILE // 2
    piece = jax.ShapeDtypeStruct((rows // seats, width), jnp.bfloat16)
    vmem = lambda *shape: pltpu.VMEM(shape, jnp.bfloat16)
    chunk = BLOCK * frames
    steps = rows // chunk
    part = 0 if first else steps
    half = pl.BlockSpec((chunk, width), lambda i: (part + i, 0))
    halves = pl.BlockSpec((3, chunk, width), lambda i: (0, part + i, 0))
    fixed = lambda value: pl.BlockSpec(value.shape, lambda i: (0,) * value.ndim)
    other = jax.ShapeDtypeStruct((rows, width), jnp.bfloat16)
    return time_call(
        functools.partial(tangent_kernel, layout, (len(weights), len(pieces), seats)),
        1,
        rows,
        width,
        TANGENT_VMEM_LIMIT,
        grid=(steps,),
        out_shape=[piece] * seats + [other] * first,
        in_specs=[IN_SMEM] * 2
        + [fixed(shift), fixed(down), fixed(up), half, half, halves]
        + [ANYWHERE] * len(weights)
        + ([ANYWHERE] * len(pieces) if first else [pl.BlockSpec((chunk, width), lambda i: (i, 0))]),
        out_specs=[ANYWHERE] * seats + [fixed(other)] * first,
        scratch_shapes=[vmem(frames, ROW_TILE, width), vmem(2 * rows, width)] * first
        + [vmem(4, width, width), vmem(rows, width), vmem(rows, width)]
        + [vmem(chunk, width)] * 9
        + [
            pltpu.SemaphoreType.DMA((len(layout),)),
            pltpu.SemaphoreType.DMA((4 * max(4, seats),)),
        ],
    )(seat, strength, shift, down, up, velocity, noisy, primal, *weights, *pieces)


def place_kernel(count, seat_ref, *rest):
    result_ref = rest[-1]
    frames, _, width = result_ref.shape
    for index in range(count):
        if len(rest[0].shape) > 2:
            parts = [rest[index // 2][index % 2].astype(jnp.float32)]
        else:
            parts = [piece[...].astype(jnp.float32) for piece in rest[index:-1:count]]
        parts = [part.reshape(frames, -1, width) for part in parts]
        start = pl.multiple_of((seat_ref[1] ^ index) * ROW_TILE, ROW_TILE)
        result_ref[:, pl.ds(start, ROW_TILE), :] = jnp.concatenate(parts, axis=1).astype(
            jnp.bfloat16
        )


def placed(seat, pieces, seats, frames):
    width = pieces[0].shape[-1]
    steps = max(1, frames // 4)
    half = frames // steps

    def block(piece):
        lead, (rows, width) = piece.shape[:-2], piece.shape[-2:]
        return pl.BlockSpec((*lead, rows // steps, width), lambda f: (0,) * len(lead) + (f, 0))

    return pl.pallas_call(
        functools.partial(place_kernel, seats),
        out_shape=jax.ShapeDtypeStruct((frames, seats * ROW_TILE, width), jnp.bfloat16),
        grid=(steps,),
        in_specs=[IN_SMEM]
        + [block(piece) for piece in pieces],
        out_specs=pl.BlockSpec((half, seats * ROW_TILE, width), lambda f: (f, 0, 0)),
        compiler_params=pltpu.CompilerParams(vmem_limit_bytes=VMEM_LIMIT),
    )(seat, *pieces)


def flip(value, axis, mask):
    pairs = [(source, source ^ mask) for source in range(lax.axis_size(axis))]
    return lax.ppermute(value, axis, pairs)


def half_weights(qkv, out_weight, core):
    stacked = jnp.concatenate([jnp.swapaxes(qkv, 1, 2), out_weight[None]], axis=0)
    return lax.dynamic_slice_in_dim(stacked, core * 2, 2, axis=0)


def z_pair(value, across):
    other = flip(value, "seq", lax.axis_size("seq") // 4)
    return jnp.where(
        across % 2 == 0,
        jnp.concatenate([value, other], axis=1),
        jnp.concatenate([other, value], axis=1),
    )


def over_middle(near):
    step = lax.axis_size("seq") // 4
    pairs = [
        pair
        for low in range(step)
        for pair in ((step + low, 2 * step + low), (2 * step + low, step + low))
    ]
    return lax.ppermute(near, "seq", pairs)


def to_ends(inside, across):
    step = lax.axis_size("seq") // 4
    pairs = [
        pair
        for low in range(step)
        for pair in ((step + low, low), (2 * step + low, 3 * step + low))
    ]
    outside = lax.ppermute(inside, "seq", pairs)
    return jnp.where((across == 1) | (across == 2), inside, outside)


NEAR = ((0, 0, 0), (0, 0, 1), (1, 0, 0), (1, 0, 1))
FAR = ((0, 1, 0), (0, 1, 1), (1, 1, 0), (1, 1, 1))


def own_layout():
    return [(index, None, 0, place) for index, place in enumerate(NEAR + FAR)]


def other_core(pieces):
    swapped = []
    for piece in pieces:
        if swapped:
            piece, swapped[-1] = together(piece, swapped[-1])
        swapped.append(flip(piece, "clip", 1))
    return swapped


def send(pieces):
    return [pieces[0]] + [flip(piece, "seq", i) for i, piece in enumerate(pieces) if i > 0]


def together(*groups):
    return lax.optimization_barrier(groups)


def along_line(neighbours):
    pieces = [
        jnp.stack([given[line] for given in neighbours])
        for line in range(neighbours[0].shape[0])
    ]
    return [flip(piece, "seq", 2 * i) if i > 0 else piece for i, piece in enumerate(pieces)]


def over_both(value):
    size = lax.axis_size("cfg") * lax.axis_size("seq")
    pairs = [(d, d ^ (size // 2 + 1)) for d in range(size)]
    return lax.ppermute(value, ("cfg", "seq"), pairs)


def to_neighbours(kept, low, across, both):
    return [kept, flip(low, "seq", 1), flip(across, "cfg", 1), over_both(both)]


def on_device(
    clean,
    noise,
    timestep,
    guidance,
    condition_vector,
    empty_prompt_vector,
    timestep_direction,
    spatial_query_key_value,
    spatial_output_weight,
    temporal_query_key_value,
    temporal_output_weight,
    adapter_down_maps,
    adapter_up_maps,
):
    sides, seats = lax.axis_size("cfg"), lax.axis_size("seq")
    side, place, core = (lax.axis_index(a) for a in ("cfg", "seq", "clip"))
    frames = clean.shape[0] * seats
    width = clean.shape[2]
    seat = jnp.stack([side, place, core]).astype(jnp.int32)
    moved = timestep[0] * timestep_direction.astype(jnp.float32)
    cond_shift = (moved + condition_vector.astype(jnp.float32))[None]
    uncond_shift = (moved + empty_prompt_vector.astype(jnp.float32))[None]
    down = jnp.swapaxes(adapter_down_maps, 1, 2).reshape(-1, width)
    up = adapter_up_maps.reshape(-1, sides, 2, 2, seats // 4, HEAD_DIM)
    up = jnp.swapaxes(up, 3, 4).reshape(-1, width)

    noisy_lines = noisy_pieces(seat, timestep, clean, noise, seats)
    space_own = half_weights(spatial_query_key_value, spatial_output_weight, core)
    time_own = half_weights(temporal_query_key_value, temporal_output_weight, core)
    across = place // (seats // 4)

    space_near = z_pair(space_own, across)
    space_near, time_own = together(space_near, time_own)
    space_in = over_middle(space_near)
    space = [space_near, flip(space_near, "seq", 1), flip(space_near, "cfg", 1)]
    time_near = z_pair(time_own, across)
    space_other = other_core([space_near])
    space, space_other, space_in, time_near = together(space, space_other, space_in, time_near)

    space_far = to_ends(space_in, across)
    space_xy = flip(space[2], "seq", 1)
    time_in = over_middle(time_near)
    time_x = flip(time_near, "cfg", 1)
    space_other += other_core(space[1:])
    space += [space_xy, space_far]
    space, space_other, time_in, time_x, time_near, noisy_lines, down, up = together(
        space, space_other, time_in, time_x, time_near, noisy_lines, down, up
    )

    space_far_x = flip(space[4], "cfg", 1)
    space_far_y = flip(space[4], "seq", 1)
    time_far = to_ends(time_in, across)
    space_xy_other, time_near_other = other_core([space[3], time_near])
    space += [space_far_y, space_far_x]
    space_other += [space_xy_other]
    time_other = [time_near_other]
    space, space_other, time_other, time_far, time_near, time_x, noisy_lines = together(
        space, space_other, time_other, time_far, time_near, time_x, noisy_lines
    )

    space_far_xy = flip(space[5], "cfg", 1)
    time_y = flip(time_near, "seq", 1)
    noisy_1 = flip(noisy_lines[1], "seq", 2)
    *space_far_other, time_x_other = other_core(space[4:] + [time_x])
    space.append(space_far_xy)
    space_other += space_far_other
    time_other += [time_x_other]
    space, space_other, time_x, time_y, time_far, time_near, time_other, noisy_came = together(
        space, space_other, time_x, time_y, time_far, time_near, time_other,
        [noisy_lines[0], noisy_1, *noisy_lines[2:]],
    )

    space_last, time_far_other, time_y_other = (
        flip(piece, "clip", 1) for piece in (space[7], time_far, time_y)
    )
    space_other += [space_last]
    time_other += [time_far_other, time_y_other]
    space, space_other, time_x, time_y, time_far, time_near, time_other, noisy_came = together(
        space, space_other, time_x, time_y, time_far, time_near, time_other, noisy_came
    )
    space_weights = (
        list(space) + list(space_other),
        [(index, None, index // 8, (NEAR + FAR)[index % 8]) for index in range(16)],
    )
    cond, uncond = [
        functools.partial(
            spatial_layer, seat, timestep, clean, noise, shift,
            frames=clean.shape[0] // sides, seats=seats,
        )
        for shift in (cond_shift, uncond_shift)
    ]
    time_xy = flip(time_y, "cfg", 1)
    time_far_x = flip(time_far, "cfg", 1)
    time_far_y = flip(time_far, "seq", 1)
    noisy_came = list(noisy_came[:2]) + [
        flip(line, "seq", 2 * index) for index, line in enumerate(noisy_came) if index > 1
    ]
    cond = cond(weights=space_weights)
    cond, time_xy, time_far_x, time_far_y, noisy_came = together(
        cond, time_xy, time_far_x, time_far_y, noisy_came
    )
    time_late = [flip(piece, "clip", 1) for piece in (time_xy, time_far_y, time_far_x)]
    noisy_low = jnp.stack([line[1] for line in noisy_came])
    cond, time_far_y, time_late, noisy_low = together(cond, time_far_y, time_late, noisy_low)
    uncond = uncond(weights=space_weights)
    time_far_xy = flip(time_far_y, "cfg", 1)
    noisy_low = flip(noisy_low, "seq", 1)
    cond, uncond, time_far_xy, noisy_low = together(
        to_neighbours(*cond), uncond, time_far_xy, noisy_low
    )
    lines = [jnp.stack([given[line] for given in cond]) for line in range(seats // 2)]
    far_lines = [flip(lines[i], "seq", 2 * i) for i in range(2, seats // 2)]
    time_last = flip(time_far_xy, "clip", 1)
    uncond, time_last = together(uncond, time_last)
    time_weights = (
        [time_near, time_y, time_x, time_xy, time_far, time_far_y, time_far_x, time_far_xy]
        + list(time_other) + list(time_late) + [time_last],
        [(index, None, 0, at) for index, at in enumerate(NEAR + FAR)]
        + [
            (8 + index, None, 1, at)
            for index, at in enumerate(
                [NEAR[0], NEAR[2], FAR[0], NEAR[1], NEAR[3], FAR[1], FAR[2], FAR[3]]
            )
        ],
    )
    noisy_in = list(noisy_came) + [noisy_low]
    kept, low, across, both = uncond
    low, across, both = flip(low, "seq", 1), flip(across, "cfg", 1), over_both(both)
    rows, primal = student_rows(seat, cond_shift, down, up, time_weights, noisy_in, frames)
    rows, primal, low, across, both, lines = together(rows, primal, low, across, both, lines)
    near_line = flip(lines[1], "seq", 2)
    uncond = [
        jnp.stack([given[line] for given in (kept, low, across, both)])
        for line in range(seats // 2)
    ]
    uncond_last = flip(uncond[-1], "seq", seats - 2)
    student_kept, student_low = student_mix(
        seat, cond_shift, rows, primal, time_weights, frames, seats
    )
    cond = [lines[0], near_line, *far_lines]
    student_kept, student_low, cond, uncond = together(student_kept, student_low, cond, uncond)
    uncond = [
        flip(line, "seq", 2 * index) if index > 0 else line
        for index, line in enumerate(uncond[:-1])
    ] + [uncond_last]
    velocity = teacher_velocity(seat, time_weights, cond, frames)
    student_low, velocity, uncond = together(flip(student_low, "seq", 1), velocity, uncond)
    student_back = along_line([student_kept, student_low])
    tangent = functools.partial(
        student_tangent, seat, guidance, cond_shift, down, up, velocity, rows, primal,
        time_weights, frames=frames, seats=seats,
    )
    *tangent_pieces, other = tangent(uncond)
    student_back, other, tangent_pieces = together(student_back, other, tangent_pieces)
    tangent_back = send(tangent_pieces)
    rest, tangent_back = together(tangent([other]), tangent_back)
    tangent_back = list(tangent_back) + send(rest)
    here = clean.shape[0]
    return placed(seat, student_back, seats, here), placed(seat, tangent_back, seats, here)


def fits(mesh, frames, positions, width):
    sides, seats = mesh.shape["cfg"], mesh.shape["seq"]
    groups = sides * seats
    return (
        sides == 2
        and mesh.shape["clip"] == 2
        and seats == 4 * sides
        and frames % (groups * ROW_TILE // 4) == 0
        and positions == groups * ROW_TILE
        and 2 * frames == LANES
        and width % LANES == 0
        and width == groups * HEAD_DIM
    )

def solution(mesh):
    specs = dict(
        mesh=mesh,
        in_specs=(
            P(("clip", "seq"), None, None),
            P(("clip", "seq"), None, None),
            P("clip"),
            P("clip"),
            P("clip"),
            P(),
            P(),
            P(None, None, ("cfg", "seq")),
            P(("cfg", "seq"), None),
            P(None, None, ("cfg", "seq")),
            P(("cfg", "seq"), None),
            P(),
            P(),
        ),
        out_specs=(P(("clip", "seq"), "cfg", None), P(("clip", "seq"), "cfg", None)),
        check_vma=False,
    )

    def whole(clean, *rest):
        frames = clean.shape[0] // mesh.shape["clip"]
        fast = fits(mesh, frames, clean.shape[1], clean.shape[2])
        return jax.shard_map(on_device if fast else plain_on_device, **specs)(clean, *rest)

    return whole
```

```python
import functools
import math

import jax
import jax.numpy as jnp
from jax import lax
from jax.experimental import pallas as pl
from jax.experimental.pallas import tpu as pltpu
from jax.sharding import PartitionSpec as P

HEAD_DIM = 72
LANES = 128
ROW_TILE = 16
BLOCK = 8
EXPONENT_SCALE = HEAD_DIM ** (-0.5) * math.log2(math.e)
VMEM_LIMIT = 40 * 1024 * 1024
SPACE_VMEM_LIMIT = 26 * 1024 * 1024
FULL_VMEM_LIMIT = 60 * 1024 * 1024

epsilon = 1e-06


def partner(value, axis, bit):
    mask = 2**bit
    pairs = [(source, source ^ mask) for source in range(lax.axis_size(axis))]
    return lax.ppermute(value, axis, pairs)


def rms_scale(features):
    return features * lax.rsqrt(jnp.mean(features * features, axis=-1, keepdims=True) + epsilon)


def project(rows_in, matrix):
    return jnp.einsum("...d,dk->...k", rows_in, matrix, preferred_element_type=jnp.float32)


def space_attend(queries, key_rows, value_rows):
    head_count = queries.shape[-1] // HEAD_DIM
    split_dims = queries.shape[:-1] + (head_count, HEAD_DIM)
    scores = jnp.einsum(
        "...qhd,...khd->...hqk",
        queries.reshape(split_dims),
        key_rows.reshape(split_dims),
        preferred_element_type=jnp.float32,
    ) * HEAD_DIM ** (-0.5)
    scores = scores - jnp.max(scores, axis=-1, keepdims=True)
    exponent = jnp.exp(scores)
    soft_weights = (exponent / jnp.sum(exponent, axis=-1, keepdims=True)).astype(jnp.bfloat16)
    result = jnp.einsum(
        "...hqk,...khd->...qhd",
        soft_weights,
        value_rows.reshape(split_dims),
        preferred_element_type=jnp.float32,
    )
    return result.astype(jnp.bfloat16).reshape(queries.shape)


def time_attend(queries, key_rows, value_rows):
    head_count = queries.shape[-1] // HEAD_DIM
    split_dims = queries.shape[:-1] + (head_count, HEAD_DIM)
    scores = jnp.einsum(
        "...fxhd,...gxhd->...xhfg",
        queries.reshape(split_dims),
        key_rows.reshape(split_dims),
        preferred_element_type=jnp.float32,
    ) * HEAD_DIM ** (-0.5)
    scores = scores - jnp.max(scores, axis=-1, keepdims=True)
    exponent = jnp.exp(scores)
    soft_weights = (exponent / jnp.sum(exponent, axis=-1, keepdims=True)).astype(jnp.bfloat16)
    result = jnp.einsum(
        "...xhfg,...gxhd->...fxhd",
        soft_weights,
        value_rows.reshape(split_dims),
        preferred_element_type=jnp.float32,
    )
    return result.astype(jnp.bfloat16).reshape(queries.shape)


def time_core(embedding_rows, query_weight, key_weight, value_weight, out_weight):
    normed = rms_scale(embedding_rows).astype(jnp.bfloat16)
    queries = project(normed, query_weight).astype(jnp.bfloat16)
    key_rows = project(normed, key_weight).astype(jnp.bfloat16)
    value_rows = project(normed, value_weight).astype(jnp.bfloat16)
    return project(time_attend(queries, key_rows, value_rows), out_weight)


def student_network(
    embedding_rows,
    query_weight,
    key_weight,
    value_weight,
    out_weight,
    down_query,
    query_up_map,
    down_value,
    value_up_map,
):
    normed = rms_scale(embedding_rows).astype(jnp.bfloat16)
    low_query = project(normed, down_query).astype(jnp.bfloat16)
    low_value = project(normed, down_value).astype(jnp.bfloat16)
    queries = (project(normed, query_weight) + project(low_query, query_up_map)).astype(
        jnp.bfloat16
    )
    key_rows = project(normed, key_weight).astype(jnp.bfloat16)
    value_rows = (project(normed, value_weight) + project(low_value, value_up_map)).astype(
        jnp.bfloat16
    )
    return project(time_attend(queries, key_rows, value_rows), out_weight)


def plain_on_device(
    clean,
    noise,
    timestep,
    guidance,
    condition_vector,
    empty_prompt_vector,
    timestep_direction,
    spatial_query_key_value,
    spatial_output_weight,
    temporal_query_key_value,
    temporal_output_weight,
    adapter_down_maps,
    adapter_up_maps,
):
    moment = timestep[0]
    strength = guidance[0]
    pair_side = lax.axis_index("cfg")
    noisy_rows = (
        (1.0 - moment) * clean.astype(jnp.float32) + moment * noise.astype(jnp.float32)
    ).astype(jnp.bfloat16)
    shifted = noisy_rows.astype(jnp.float32) + moment * timestep_direction.astype(jnp.float32)
    embeds = jnp.where(pair_side == 0, condition_vector, empty_prompt_vector)[None]
    branch_count = embeds.shape[0]
    entries = shifted[None] + embeds.astype(jnp.float32)[:, None, None, :]
    normed = rms_scale(entries).astype(jnp.bfloat16)
    triple = jnp.einsum(
        "bfpd,jdk->jbfpk",
        normed,
        lax.all_gather(spatial_query_key_value, ("cfg", "seq"), axis=2, tiled=True),
        preferred_element_type=jnp.float32,
    ).astype(jnp.bfloat16)
    attended = space_attend(triple[0], triple[1], triple[2])
    partial_value = jnp.einsum(
        "bfpk,kd->bfpd",
        attended,
        lax.all_gather(spatial_output_weight, ("cfg", "seq"), axis=0, tiled=True),
        preferred_element_type=jnp.float32,
    )
    layer_one = (entries + partial_value).astype(jnp.bfloat16)
    frame_count = layer_one.shape[1]
    position_count = layer_one.shape[2]
    width = layer_one.shape[3]
    stacked = jnp.concatenate([layer_one, noisy_rows[None]], axis=0).reshape(
        branch_count + 1, frame_count, 2, position_count // 2, width
    )
    regrouped = lax.all_to_all(stacked, "seq", split_axis=3, concat_axis=1, tiled=True)
    frames = regrouped.shape[1]
    local_rows = regrouped.shape[3]
    teacher_in = regrouped[:branch_count].reshape(branch_count, frames, 2 * local_rows, width)
    noisy_local = regrouped[branch_count]
    time_qkv, time_out = (
        lax.all_gather(temporal_query_key_value, ("cfg", "seq"), axis=2, tiled=True),
        lax.all_gather(temporal_output_weight, ("cfg", "seq"), axis=0, tiled=True),
    )
    teacher_part = time_core(
        teacher_in.astype(jnp.float32), time_qkv[0], time_qkv[1], time_qkv[2], time_out
    )
    velocity = (
        (teacher_in.astype(jnp.float32) + teacher_part)
        .astype(jnp.bfloat16)
        .reshape(branch_count, frames, 2, local_rows, width)
    )
    own_velocity = velocity[0]
    own_half = lax.dynamic_index_in_dim(own_velocity, pair_side, 1, keepdims=False)
    outgoing = lax.dynamic_index_in_dim(own_velocity, 1 - pair_side, 1, keepdims=False)
    other_half = partner(outgoing, "cfg", 0)
    is_first = pair_side == 0
    cond_velocity = jnp.where(is_first, own_half, other_half)
    uncond_velocity = jnp.where(is_first, other_half, own_half)
    student_noisy = lax.dynamic_index_in_dim(noisy_local, pair_side, 1, keepdims=False)
    query_up_map = adapter_up_maps[0]
    value_up_map = adapter_up_maps[1]
    uncond_float = uncond_velocity.astype(jnp.float32)
    guided = (uncond_float + strength * (cond_velocity.astype(jnp.float32) - uncond_float)).astype(
        jnp.bfloat16
    )
    student_in = (
        student_noisy.astype(jnp.float32)
        + moment * timestep_direction.astype(jnp.float32)
        + condition_vector.astype(jnp.float32)
    )

    def student_map(embedding_rows):
        return student_network(
            embedding_rows,
            time_qkv[0],
            time_qkv[1],
            time_qkv[2],
            time_out,
            adapter_down_maps[0],
            query_up_map,
            adapter_down_maps[1],
            value_up_map,
        )

    partial_value, tangent_part = jax.jvp(student_map, (student_in,), (guided.astype(jnp.float32),))
    primal = (student_in + partial_value).astype(jnp.bfloat16)
    tangent = (guided.astype(jnp.float32) + tangent_part).astype(jnp.bfloat16)
    returned = lax.all_to_all(
        jnp.stack([primal, tangent]), "seq", split_axis=1, concat_axis=2, tiled=True
    )
    return (returned[0], returned[1])


def dot(left, right):
    return lax.dot_general(
        left, right, (((1,), (0,)), ((), ())), preferred_element_type=jnp.float32
    )


def dot_t(left, right):
    return lax.dot_general(
        left, right, (((1,), (1,)), ((), ())), preferred_element_type=jnp.float32
    )


def lane_range(shape, start, low, high):
    lane = lax.broadcasted_iota(jnp.int32, shape, len(shape) - 1) + start
    return (lane >= low) & (lane < high)


def only(value, keep):
    return jnp.where(keep, value, jnp.zeros_like(value))


def window_of(low, high):
    start = low // LANES * LANES
    return start, -(-high // LANES) * LANES - start


def inverse_rms(features):
    return lax.rsqrt(jnp.mean(features * features, axis=-1, keepdims=True) + epsilon)


def weight_copies(seat, layout, pieces, weights_ref, sems):
    side, place, core = seat[0], seat[1], seat[2]
    across, along = place // 4, lax.rem(place, 2)
    copies = []
    for array, part, sibling, (x, z, y) in layout:
        piece = pieces[array] if part is None else pieces[array].at[part]
        count, rows = piece.shape[:2]
        block = ((side ^ x) * 2 + (across ^ z)) * 2 + (along ^ y)
        start = pl.multiple_of(block * rows, ROW_TILE)
        copies.append(
            pltpu.make_async_copy(
                piece,
                weights_ref.at[pl.ds((core ^ sibling) * count, count), pl.ds(start, rows), :],
                sems.at[len(copies)],
            )
        )
    return copies


def noisy_kernel(seat_ref, moment_ref, clean_ref, noise_ref, *rest):
    line_refs, rows_ref = rest[:-1], rest[-1]
    moment = moment_ref[0]
    rows_ref[...] = (
        (1.0 - moment) * clean_ref[0].astype(jnp.float32)
        + moment * noise_ref[0].astype(jnp.float32)
    ).astype(jnp.bfloat16)
    for index in range(2 * len(line_refs)):
        start = pl.multiple_of((seat_ref[1] ^ index) * ROW_TILE, ROW_TILE)
        line_refs[index // 2][index % 2, 0] = rows_ref[pl.ds(start, ROW_TILE), :]


def noisy_pieces(seat, moment, clean, noise, seats):
    frames, positions, width = clean.shape
    rows = seats * ROW_TILE
    block = pl.BlockSpec((1, rows, width), lambda f, seat: (f, seat[0], 0))
    half = seats // 2
    piece = jax.ShapeDtypeStruct((2, frames, ROW_TILE, width), jnp.bfloat16)
    out_block = pl.BlockSpec((2, 1, ROW_TILE, width), lambda f, seat: (0, f, 0, 0))
    return pl.pallas_call(
        noisy_kernel,
        out_shape=[piece] * half,
        grid_spec=pltpu.PrefetchScalarGridSpec(
            num_scalar_prefetch=1,
            grid=(frames,),
            in_specs=[pl.BlockSpec(memory_space=pltpu.SMEM), block, block],
            out_specs=[out_block] * half,
            scratch_shapes=[pltpu.VMEM((rows, width), jnp.bfloat16)],
        ),
        compiler_params=pltpu.CompilerParams(vmem_limit_bytes=VMEM_LIMIT),
    )(seat, moment, clean, noise)


def space_kernel(layout, pieces, targets, seat_ref, moment_ref, clean_ref, noise_ref, shift_ref, *rest):
    weight_pieces, sent_refs = rest[:pieces], rest[pieces : pieces + targets]
    weights_ref, query_ref, key_ref, value_ref, mixed_ref, sems = rest[pieces + targets :]
    moment = moment_ref[0]
    positions, width = key_ref.shape

    @pl.when(pl.program_id(0) == 0)
    def _():
        wait_all(start_all(weight_copies(seat_ref, layout, weight_pieces, weights_ref, sems)))

    noisy = (
        (1.0 - moment) * clean_ref[0].astype(jnp.float32)
        + moment * noise_ref[0].astype(jnp.float32)
    ).astype(jnp.bfloat16)
    entry = noisy.astype(jnp.float32) + shift_ref[...]
    normed = (entry * inverse_rms(entry)).astype(jnp.bfloat16)
    query_ref[...] = dot_t(normed, weights_ref[0]).astype(jnp.bfloat16)
    key_ref[...] = dot_t(normed, weights_ref[1]).astype(jnp.bfloat16)
    value_ref[...] = dot_t(normed, weights_ref[2]).astype(jnp.bfloat16)

    weights = []
    for head in range(width // HEAD_DIM):
        low, high = head * HEAD_DIM, (head + 1) * HEAD_DIM
        start, extent = window_of(low, high)
        keep = lane_range((positions, extent), start, low, high)
        queries = only(query_ref[:, pl.ds(start, extent)], keep)
        scores = dot_t(queries, key_ref[:, pl.ds(start, extent)])
        top = jnp.max(scores, axis=-1, keepdims=True)
        exponent = jnp.exp2((scores - top) * EXPONENT_SCALE)
        total = jnp.sum(exponent, axis=-1, keepdims=True)
        weights.append((exponent * (1.0 / total)).astype(jnp.bfloat16))
        tile = high // (2 * LANES)
        done = [low // (2 * LANES)] if tile > low // (2 * LANES) else []
        if head == width // HEAD_DIM - 1:
            done = [(width - 1) // (2 * LANES)]
        for full in done:
            left_edge = full * 2 * LANES
            edge = min(width, left_edge + 2 * LANES)
            heads = range(left_edge // HEAD_DIM, -(-edge // HEAD_DIM))
            values = value_ref[:, pl.ds(left_edge, edge - left_edge)]
            parts = [
                only(
                    values,
                    lane_range(values.shape, left_edge, h * HEAD_DIM, (h + 1) * HEAD_DIM),
                )
                for h in heads
            ]
            mixed = dot(
                jnp.concatenate([weights[h] for h in heads], axis=1),
                jnp.concatenate(parts, axis=0),
            )
            mixed_ref[:, pl.ds(left_edge, edge - left_edge)] = mixed.astype(jnp.bfloat16)

    query_ref[...] = (entry + dot(mixed_ref[...], weights_ref[3])).astype(jnp.bfloat16)
    lines = sent_refs[0].shape[0]
    for index, ref in enumerate(sent_refs):
        for line in range(lines):
            seat = (seat_ref[0] ^ (index // 2)) * lines * 2 + (
                seat_ref[1] ^ (line * 2 + index % 2)
            )
            start = pl.multiple_of(seat * ROW_TILE, ROW_TILE)
            ref[line, 0] = query_ref[pl.ds(start, ROW_TILE), :]


def spatial_layer(seat, moment, clean, noise, shift, limit, weights, frames, seats):
    pieces, layout = weights
    positions, width = clean.shape[1:]
    frame_block = pl.BlockSpec(
        (1, positions, width), lambda f, seat: (seat[0] * frames + f, 0, 0)
    )
    lines = seats // 2
    piece = jax.ShapeDtypeStruct((lines, frames, ROW_TILE, width), jnp.bfloat16)
    vmem = lambda *shape: pltpu.VMEM(shape, jnp.bfloat16)
    rows = frames * positions
    return pl.pallas_call(
        functools.partial(space_kernel, layout, len(pieces), 4),
        out_shape=[piece] * 4,
        grid_spec=pltpu.PrefetchScalarGridSpec(
            num_scalar_prefetch=1,
            grid=(frames,),
            in_specs=[
                pl.BlockSpec(memory_space=pltpu.SMEM),
                frame_block,
                frame_block,
                pl.BlockSpec(shift.shape, lambda f, seat: (0, 0)),
            ]
            + [pl.BlockSpec(memory_space=pl.ANY)] * len(pieces),
            out_specs=[
                pl.BlockSpec((lines, 1, ROW_TILE, width), lambda f, seat: (0, f, 0, 0))
            ]
            * 4,
            scratch_shapes=[vmem(4, width, width)]
            + [vmem(positions, width)] * 4
            + [pltpu.SemaphoreType.DMA((len(layout),))],
        ),
        compiler_params=pltpu.CompilerParams(vmem_limit_bytes=limit),
        cost_estimate=pl.CostEstimate(
            flops=14 * rows * width * width,
            bytes_accessed=8 * width * width + 6 * rows * width,
            transcendentals=rows * positions * width // HEAD_DIM,
        ),
    )(seat, moment, clean, noise, shift, *pieces)


def swap_matrix(rows, columns):
    count = rows * columns
    target = lax.broadcasted_iota(jnp.int32, (count, count), 0)
    source = lax.broadcasted_iota(jnp.int32, (count, count), 1)
    moved = lax.rem(target, rows) * columns + lax.div(target, rows)
    return jnp.where(source == moved, 1.0, 0.0).astype(jnp.bfloat16)


def halves(value, frames, reduce):
    first = lane_range(value.shape, 0, 0, frames)
    if reduce == "max":
        low = jnp.max(jnp.where(first, value, -jnp.inf), axis=-1, keepdims=True)
        high = jnp.max(jnp.where(first, -jnp.inf, value), axis=-1, keepdims=True)
    else:
        low = jnp.sum(jnp.where(first, value, 0.0), axis=-1, keepdims=True)
        high = jnp.sum(jnp.where(first, 0.0, value), axis=-1, keepdims=True)
    return first, low, high


def time_mix(frames, refs, tangents=None):
    query_ref, key_ref, value_ref, mixed_ref = refs
    rows, width = query_ref.shape
    scale = HEAD_DIM ** (-0.5)
    tiles = [[] for _ in range(width // LANES)]
    tangent_tiles = [[] for _ in range(width // LANES)]
    pairs = width // (2 * HEAD_DIM)
    blocks = [pl.ds(i * frames, frames) for i in range(rows // frames)]

    def stack(value, start, low):
        shape = value.shape
        return jnp.concatenate(
            [
                only(value, lane_range(shape, start, low, low + HEAD_DIM)),
                only(value, lane_range(shape, start, low + HEAD_DIM, low + 2 * HEAD_DIM)),
            ],
            axis=0,
        )

    for pair in range(pairs):
        low = pair * 2 * HEAD_DIM
        start, extent = window_of(low, low + 2 * HEAD_DIM)
        columns = pl.ds(start, extent)
        keys = [stack(key_ref[b, columns], start, low) for b in blocks]
        values = [stack(value_ref[b, columns], start, low) for b in blocks]
        scores = jnp.concatenate(
            [dot_t(query_ref[b, columns], k) for b, k in zip(blocks, keys)], axis=0
        )
        first, top_low, top_high = halves(scores, frames, "max")
        exponent = jnp.exp2((scores - jnp.where(first, top_low, top_high)) * EXPONENT_SCALE)
        _, sum_low, sum_high = halves(exponent, frames, "sum")
        weights = exponent * jnp.where(first, 1.0 / sum_low, 1.0 / sum_high)
        rounded = weights.astype(jnp.bfloat16)
        mixed = jnp.concatenate(
            [
                dot(rounded[i * frames : (i + 1) * frames], v)
                for i, v in enumerate(values)
            ],
            axis=0,
        )
        for tile in range(extent // LANES):
            tiles[start // LANES + tile].append(mixed[:, tile * LANES : (tile + 1) * LANES])
        if tangents is not None:
            query_dot, key_dot, value_dot, _ = tangents
            score_dots = jnp.concatenate(
                [
                    dot_t(query_dot[b, columns], k)
                    + dot_t(query_ref[b, columns], stack(key_dot[b, columns], start, low))
                    for b, k in zip(blocks, keys)
                ],
                axis=0,
            ) * scale
            _, mean_low, mean_high = halves(weights * score_dots, frames, "sum")
            weight_dots = (
                weights * (score_dots - jnp.where(first, mean_low, mean_high))
            ).astype(jnp.bfloat16)
            mixed_dots = jnp.concatenate(
                [
                    dot(
                        jnp.concatenate(
                            [
                                weight_dots[i * frames : (i + 1) * frames],
                                rounded[i * frames : (i + 1) * frames],
                            ],
                            axis=1,
                        ),
                        jnp.concatenate(
                            [v, stack(value_dot[b, columns], start, low)], axis=0
                        ),
                    )
                    for i, (b, v) in enumerate(zip(blocks, values))
                ],
                axis=0,
            )
            for tile in range(extent // LANES):
                tangent_tiles[start // LANES + tile].append(
                    mixed_dots[:, tile * LANES : (tile + 1) * LANES]
                )
    for tile in range(width // LANES):
        columns = pl.ds(tile * LANES, LANES)
        mixed_ref[:, columns] = functools.reduce(jnp.add, tiles[tile]).astype(jnp.bfloat16)
        if tangents is not None:
            tangents[3][:, columns] = functools.reduce(jnp.add, tangent_tiles[tile]).astype(
                jnp.bfloat16
            )


def arrivals(seat, pieces, came_ref, sems):
    copies = []
    for line, piece in enumerate(pieces):
        neighbours, frames = piece.shape[:2]
        for index in range(neighbours):
            first = (seat[1] ^ (line * 2 + index % 2)) * frames * (neighbours // 2)
            if neighbours > 2:
                first = first + (seat[0] ^ (index // 2)) * frames
            copies.append(
                pltpu.make_async_copy(
                    piece.at[index], came_ref.at[pl.ds(first, frames)], sems.at[len(copies)]
                )
            )
    return copies


def departures(seat, going_ref, pieces, sems):
    rows = pieces[0].shape[0]
    return [
        pltpu.make_async_copy(
            going_ref.at[pl.ds(pl.multiple_of((seat[1] ^ index) * rows, ROW_TILE), rows)],
            piece,
            sems.at[index],
        )
        for index, piece in enumerate(pieces)
    ]


def by_position(came_ref, rows_ref):
    frames, positions, width = came_ref.shape
    turn = swap_matrix(ROW_TILE, positions)
    for part in range(frames // ROW_TILE):
        first = part * ROW_TILE
        piece = came_ref[first : first + ROW_TILE].reshape(ROW_TILE * positions, width)
        turned = dot(turn, piece).astype(jnp.bfloat16)
        for position in range(positions):
            rows_ref[pl.ds(position * frames + first, ROW_TILE), :] = turned[
                position * ROW_TILE : (position + 1) * ROW_TILE
            ]


def by_frame(rows_ref, going_ref, frames):
    positions = rows_ref.shape[0] // frames
    group = min(frames, 2 * LANES // positions)
    turn = swap_matrix(positions, group)
    for part in range(frames // group):
        piece = jnp.concatenate(
            [rows_ref[pl.ds(p * frames + part * group, group), :] for p in range(positions)],
            axis=0,
        )
        here = pl.ds(part * group * positions, group * positions)
        going_ref[here, :] = dot(turn, piece).astype(jnp.bfloat16)


def wait_all(copies):
    for copy in copies:
        copy.wait()


def start_all(copies):
    for copy in copies:
        copy.start()
    return copies


def adapted(rows_in, weights_ref, down_ref, up_ref, refs):
    rank = down_ref.shape[0] // 2
    low = dot_t(rows_in, down_ref[...]).astype(jnp.bfloat16)
    first = lane_range(low.shape, 0, 0, rank)
    refs[0][...] = (
        dot_t(rows_in, weights_ref[0]) + dot(only(low, first), up_ref[...])
    ).astype(jnp.bfloat16)
    refs[1][...] = dot_t(rows_in, weights_ref[1]).astype(jnp.bfloat16)
    refs[2][...] = (
        dot_t(rows_in, weights_ref[2]) + dot(only(low, jnp.logical_not(first)), up_ref[...])
    ).astype(jnp.bfloat16)


def student_rows_kernel(layout, counts, seat_ref, shift_ref, down_ref, up_ref, *rest):
    weight_count, piece_count = counts
    weight_pieces, rest = rest[:weight_count], rest[weight_count:]
    pieces, rest = rest[:piece_count], rest[piece_count:]
    rows_out_ref, primal_ref, weights_ref, came_ref, rows_ref, weight_sems, piece_sems = rest
    chunk = rows_out_ref.shape[0]

    @pl.when(pl.program_id(0) == 0)
    def _():
        weights = weight_copies(seat_ref, layout, weight_pieces, weights_ref, weight_sems)
        lines = piece_count - 2
        copies = []
        for index in range(2 * lines):
            if index % 2:
                part, line = divmod(index // 2, lines // 2)
                piece = pieces[lines + part].at[line]
            else:
                piece = pieces[index // 2].at[0]
            count = piece.shape[0]
            copies.append(
                pltpu.make_async_copy(
                    piece,
                    came_ref.at[pl.ds((seat_ref[1] ^ index) * count, count)],
                    piece_sems.at[index],
                )
            )
        start_all(copies)
        start_all(weights)
        wait_all(copies)
        by_position(came_ref, rows_ref)
        wait_all(weights)

    here = pl.ds(pl.multiple_of(pl.program_id(0) * chunk, chunk), chunk)
    rows_out_ref[...] = rows_ref[here, :]
    entry = rows_ref[here, :].astype(jnp.float32) + shift_ref[...]
    normed = (entry * inverse_rms(entry)).astype(jnp.bfloat16)
    adapted(normed, weights_ref, down_ref, up_ref, [primal_ref.at[i] for i in range(3)])


def student_mix_kernel(layout, frames, seat_ref, shift_ref, rows_ref, primal_ref, *rest):
    weight_pieces, out_refs, rest = rest[:-7], rest[-7:-5], rest[-5:]
    weights_ref, done_ref, mixed_ref, weight_sems, piece_sems = rest
    step, chunk = pl.program_id(0), mixed_ref.shape[0]
    weights = weight_copies(seat_ref, layout, weight_pieces, weights_ref, weight_sems)

    @pl.when(step == 0)
    def _():
        start_all(weights)

    time_mix(frames, [primal_ref.at[i] for i in range(3)] + [mixed_ref])

    @pl.when(step == 0)
    def _():
        wait_all(weights)

    here = pl.ds(pl.multiple_of(step * chunk, chunk), chunk)
    entry = rows_ref[...].astype(jnp.float32) + shift_ref[...]
    done_ref[0, here, :] = (entry + dot(mixed_ref[...], weights_ref[3])).astype(jnp.bfloat16)

    @pl.when(step == pl.num_programs(0) - 1)
    def _():
        by_frame(done_ref.at[0], done_ref.at[1], frames)
        pieces = [ref.at[line] for line in range(out_refs[0].shape[0]) for ref in out_refs]
        wait_all(start_all(departures(seat_ref, done_ref.at[1], pieces, piece_sems)))


def teacher(frames, rows_ref, weights_ref, refs, here):
    entry = rows_ref[here, :].astype(jnp.float32)
    normed = (entry * inverse_rms(entry)).astype(jnp.bfloat16)
    for index, ref in enumerate(refs[:3]):
        ref[...] = dot_t(normed, weights_ref[index]).astype(jnp.bfloat16)
    time_mix(frames, refs)
    entry = rows_ref[here, :].astype(jnp.float32)
    return (entry + dot(refs[3][...], weights_ref[3])).astype(jnp.bfloat16)


def teacher_kernel(layout, counts, seat_ref, *rest):
    weight_count, piece_count = counts
    weight_pieces, rest = rest[:weight_count], rest[weight_count:]
    pieces, rest = rest[:piece_count], rest[piece_count:]
    velocity_ref, weights_ref, came_ref, rows_ref = rest[:4]
    refs, (weight_sems, piece_sems) = rest[4:8], rest[8:]
    frames = came_ref.shape[0]
    chunk = refs[0].shape[0]

    @pl.when(pl.program_id(0) == 0)
    def _():
        came = start_all(arrivals(seat_ref, pieces, came_ref, piece_sems))
        weights = start_all(
            weight_copies(seat_ref, layout, weight_pieces, weights_ref, weight_sems)
        )
        wait_all(came)
        by_position(came_ref, rows_ref)
        wait_all(weights)

    here = pl.ds(pl.multiple_of(pl.program_id(0) * chunk, chunk), chunk)
    velocity_ref[...] = teacher(frames, rows_ref, weights_ref, refs, here)


def tangent_kernel(layout, counts, seat_ref, strength_ref, shift_ref, down_ref, up_ref, *rest):
    weight_count, piece_count, out_count = counts
    velocity_ref, noisy_ref, primal_ref = rest[:3]
    rest = rest[3:]
    weight_pieces, rest = rest[:weight_count], rest[weight_count:]
    pieces, rest = rest[:piece_count], rest[piece_count:]
    out_pieces, rest = rest[:out_count], rest[out_count:]
    weights_ref, done_ref, going_ref, guided_ref, *tail = rest[-14:]
    refs, dots, (weight_sems, piece_sems) = tail[:4], tail[4:8], tail[8:10]
    frames = done_ref.shape[0] // (ROW_TILE // 2)
    chunk = refs[0].shape[0]
    step = pl.program_id(0)
    first = piece_count > 1

    @pl.when(step == 0)
    def _():
        weights = weight_copies(seat_ref, layout, weight_pieces, weights_ref, weight_sems)
        if first:
            other_ref, came_ref, rows_ref = rest[:3]
            came = start_all(arrivals(seat_ref, pieces, came_ref, piece_sems))
        start_all(weights)
        if first:
            wait_all(came)
            by_position(came_ref, rows_ref)
            half = other_ref.shape[0]
            other_ref[...] = rows_ref[pl.ds(half, half), :]
        wait_all(weights)

    here = pl.ds(pl.multiple_of(step * chunk, chunk), chunk)
    rows_ref = rest[2].at[here] if first else pieces[0]
    uncond = teacher(frames, rows_ref, weights_ref, refs, slice(None)).astype(jnp.float32)
    guided = (
        uncond + strength_ref[0] * (velocity_ref[...].astype(jnp.float32) - uncond)
    ).astype(jnp.bfloat16)
    guided_ref[...] = guided
    guided = guided.astype(jnp.float32)
    entry = noisy_ref[...].astype(jnp.float32) + shift_ref[...]
    inverse = inverse_rms(entry)
    inverse_dot = -(inverse * inverse * inverse) * jnp.mean(
        entry * guided, axis=-1, keepdims=True
    )
    normed_dot = (guided * inverse + entry * inverse_dot).astype(jnp.bfloat16)
    adapted(normed_dot, weights_ref, down_ref, up_ref, dots)
    primal = [primal_ref.at[i] for i in range(3)] + [refs[3]]
    time_mix(frames, primal, dots)
    done_ref[here, :] = (
        guided_ref[...].astype(jnp.float32) + dot(dots[3][...], weights_ref[3])
    ).astype(jnp.bfloat16)

    @pl.when(step == pl.num_programs(0) - 1)
    def _():
        by_frame(done_ref, going_ref, frames)
        wait_all(start_all(departures(seat_ref, going_ref, out_pieces, piece_sems)))


IN_VMEM = pl.BlockSpec(memory_space=pltpu.VMEM)
IN_SMEM = pl.BlockSpec(memory_space=pltpu.SMEM)
ANYWHERE = pl.BlockSpec(memory_space=pl.ANY)


def time_call(kernel, passes, rows, width, limit=VMEM_LIMIT, **settings):
    return pl.pallas_call(
        kernel,
        compiler_params=pltpu.CompilerParams(vmem_limit_bytes=limit),
        cost_estimate=pl.CostEstimate(
            flops=int(12 * passes * rows * width * width),
            bytes_accessed=8 * width * width + 8 * rows * width,
            transcendentals=rows * LANES * width // HEAD_DIM,
        ),
        **settings,
    )


def student_rows(seat, shift, down, up, weights, pieces, frames):
    weights, layout = weights
    width = shift.shape[-1]
    rows, chunk = frames * ROW_TILE, BLOCK * frames
    vmem = lambda *shape: pltpu.VMEM(shape, jnp.bfloat16)
    fixed = lambda value: pl.BlockSpec(value.shape, lambda i: (0,) * value.ndim)
    return time_call(
        functools.partial(student_rows_kernel, layout, (len(weights), len(pieces))),
        0.6,
        rows,
        width,
        grid=(rows // chunk,),
        out_shape=[
            jax.ShapeDtypeStruct((rows, width), jnp.bfloat16),
            jax.ShapeDtypeStruct((3, rows, width), jnp.bfloat16),
        ],
        in_specs=[IN_SMEM, fixed(shift), fixed(down), fixed(up)]
        + [ANYWHERE] * (len(weights) + len(pieces)),
        out_specs=[
            pl.BlockSpec((chunk, width), lambda i: (i, 0)),
            pl.BlockSpec((3, chunk, width), lambda i: (0, i, 0)),
        ],
        scratch_shapes=[
            vmem(4, width, width),
            vmem(frames, ROW_TILE, width),
            vmem(rows, width),
            pltpu.SemaphoreType.DMA((len(layout),)),
            pltpu.SemaphoreType.DMA((2 * len(pieces),)),
        ],
    )(seat, shift, down, up, *weights, *pieces)


def student_mix(seat, shift, rows_in, primal, weights, frames, seats):
    weights, layout = weights
    rows, width = rows_in.shape
    chunk = BLOCK * frames
    vmem = lambda *shape: pltpu.VMEM(shape, jnp.bfloat16)
    piece = jax.ShapeDtypeStruct((seats // 2, rows // seats, width), jnp.bfloat16)
    return time_call(
        functools.partial(student_mix_kernel, layout, frames),
        0.6,
        rows,
        width,
        grid=(rows // chunk,),
        out_shape=[piece] * 2,
        in_specs=[
            IN_SMEM,
            pl.BlockSpec(shift.shape, lambda i: (0, 0)),
            pl.BlockSpec((chunk, width), lambda i: (i, 0)),
            pl.BlockSpec((3, chunk, width), lambda i: (0, i, 0)),
        ]
        + [ANYWHERE] * len(weights),
        out_specs=[ANYWHERE] * 2,
        scratch_shapes=[
            vmem(4, width, width),
            vmem(2, rows, width),
            vmem(chunk, width),
            pltpu.SemaphoreType.DMA((len(layout),)),
            pltpu.SemaphoreType.DMA((seats,)),
        ],
    )(seat, shift, rows_in, primal, *weights)


def teacher_velocity(seat, weights, pieces, frames):
    weights, layout = weights
    width = pieces[0].shape[-1]
    rows = frames * ROW_TILE
    vmem = lambda *shape: pltpu.VMEM(shape, jnp.bfloat16)
    return time_call(
        functools.partial(teacher_kernel, layout, (len(weights), len(pieces))),
        1,
        rows,
        width,
        out_shape=jax.ShapeDtypeStruct((rows, width), jnp.bfloat16),
        grid=(ROW_TILE // BLOCK,),
        in_specs=[IN_SMEM] + [ANYWHERE] * (len(weights) + len(pieces)),
        out_specs=pl.BlockSpec((BLOCK * frames, width), lambda i: (i, 0)),
        scratch_shapes=[
            vmem(4, width, width),
            vmem(frames, ROW_TILE, width),
            vmem(rows, width),
        ]
        + [vmem(BLOCK * frames, width)] * 4
        + [
            pltpu.SemaphoreType.DMA((len(layout),)),
            pltpu.SemaphoreType.DMA((4 * len(pieces),)),
        ],
    )(seat, *weights, *pieces)


def student_tangent(
    seat, strength, shift, down, up, velocity, noisy, primal, weights, pieces, frames, seats
):
    weights, layout = weights
    first = len(pieces) > 1
    width = shift.shape[-1]
    rows = frames * ROW_TILE // 2
    piece = jax.ShapeDtypeStruct((rows // seats, width), jnp.bfloat16)
    vmem = lambda *shape: pltpu.VMEM(shape, jnp.bfloat16)
    chunk = BLOCK * frames
    steps = rows // chunk
    part = 0 if first else steps
    half = pl.BlockSpec((chunk, width), lambda i: (part + i, 0))
    halves = pl.BlockSpec((3, chunk, width), lambda i: (0, part + i, 0))
    fixed = lambda value: pl.BlockSpec(value.shape, lambda i: (0,) * value.ndim)
    other = jax.ShapeDtypeStruct((rows, width), jnp.bfloat16)
    return time_call(
        functools.partial(tangent_kernel, layout, (len(weights), len(pieces), seats)),
        1,
        rows,
        width,
        FULL_VMEM_LIMIT,
        grid=(steps,),
        out_shape=[piece] * seats + [other] * first,
        in_specs=[IN_SMEM] * 2
        + [fixed(shift), fixed(down), fixed(up), half, half, halves]
        + [ANYWHERE] * len(weights)
        + ([ANYWHERE] * len(pieces) if first else [pl.BlockSpec((chunk, width), lambda i: (i, 0))]),
        out_specs=[ANYWHERE] * seats + [fixed(other)] * first,
        scratch_shapes=[vmem(frames, ROW_TILE, width), vmem(2 * rows, width)] * first
        + [vmem(4, width, width), vmem(rows, width), vmem(rows, width)]
        + [vmem(chunk, width)] * 9
        + [
            pltpu.SemaphoreType.DMA((len(layout),)),
            pltpu.SemaphoreType.DMA((4 * max(4, seats),)),
        ],
    )(seat, strength, shift, down, up, velocity, noisy, primal, *weights, *pieces)


def place_kernel(count, seat_ref, *rest):
    result_ref = rest[-1]
    frames, _, width = result_ref.shape
    for index in range(count):
        if len(rest[0].shape) > 2:
            parts = [rest[index // 2][index % 2].astype(jnp.float32)]
        else:
            parts = [piece[...].astype(jnp.float32) for piece in rest[index:-1:count]]
        parts = [part.reshape(frames, -1, width) for part in parts]
        start = pl.multiple_of((seat_ref[1] ^ index) * ROW_TILE, ROW_TILE)
        result_ref[:, pl.ds(start, ROW_TILE), :] = jnp.concatenate(parts, axis=1).astype(
            jnp.bfloat16
        )


def placed(seat, pieces, seats, frames):
    width = pieces[0].shape[-1]
    steps = max(1, frames // 4)
    half = frames // steps

    def block(piece):
        lead, (rows, width) = piece.shape[:-2], piece.shape[-2:]
        return pl.BlockSpec((*lead, rows // steps, width), lambda f: (0,) * len(lead) + (f, 0))

    return pl.pallas_call(
        functools.partial(place_kernel, seats),
        out_shape=jax.ShapeDtypeStruct((frames, seats * ROW_TILE, width), jnp.bfloat16),
        grid=(steps,),
        in_specs=[IN_SMEM]
        + [block(piece) for piece in pieces],
        out_specs=pl.BlockSpec((half, seats * ROW_TILE, width), lambda f: (f, 0, 0)),
        compiler_params=pltpu.CompilerParams(vmem_limit_bytes=VMEM_LIMIT),
    )(seat, *pieces)


def flip(value, axis, mask):
    pairs = [(source, source ^ mask) for source in range(lax.axis_size(axis))]
    return lax.ppermute(value, axis, pairs)


def half_weights(qkv, out_weight, core):
    stacked = jnp.concatenate([jnp.swapaxes(qkv, 1, 2), out_weight[None]], axis=0)
    return lax.dynamic_slice_in_dim(stacked, core * 2, 2, axis=0)


def z_pair(value, across):
    other = flip(value, "seq", lax.axis_size("seq") // 4)
    return jnp.where(
        across % 2 == 0,
        jnp.concatenate([value, other], axis=1),
        jnp.concatenate([other, value], axis=1),
    )


def over_middle(near):
    step = lax.axis_size("seq") // 4
    pairs = [
        pair
        for low in range(step)
        for pair in ((step + low, 2 * step + low), (2 * step + low, step + low))
    ]
    return lax.ppermute(near, "seq", pairs)


def to_ends(inside, across):
    step = lax.axis_size("seq") // 4
    pairs = [
        pair
        for low in range(step)
        for pair in ((step + low, low), (2 * step + low, 3 * step + low))
    ]
    outside = lax.ppermute(inside, "seq", pairs)
    return jnp.where((across == 1) | (across == 2), inside, outside)


NEAR = ((0, 0, 0), (0, 0, 1), (1, 0, 0), (1, 0, 1))
FAR = ((0, 1, 0), (0, 1, 1), (1, 1, 0), (1, 1, 1))


def own_layout():
    return [(index, None, 0, place) for index, place in enumerate(NEAR + FAR)]


def other_core(pieces):
    swapped = []
    for piece in pieces:
        if swapped:
            piece, swapped[-1] = together(piece, swapped[-1])
        swapped.append(flip(piece, "clip", 1))
    return swapped


def send(pieces):
    return [pieces[0]] + [flip(piece, "seq", i) for i, piece in enumerate(pieces) if i > 0]


def together(*groups):
    return lax.optimization_barrier(groups)


def along_line(neighbours):
    pieces = [
        jnp.stack([given[line] for given in neighbours])
        for line in range(neighbours[0].shape[0])
    ]
    return [flip(piece, "seq", 2 * i) if i > 0 else piece for i, piece in enumerate(pieces)]


def over_both(value):
    size = lax.axis_size("cfg") * lax.axis_size("seq")
    pairs = [(d, d ^ (size // 2 + 1)) for d in range(size)]
    return lax.ppermute(value, ("cfg", "seq"), pairs)


def to_neighbours(kept, low, across, both):
    return [kept, flip(low, "seq", 1), flip(across, "cfg", 1), over_both(both)]


def on_device(
    clean,
    noise,
    timestep,
    guidance,
    condition_vector,
    empty_prompt_vector,
    timestep_direction,
    spatial_query_key_value,
    spatial_output_weight,
    temporal_query_key_value,
    temporal_output_weight,
    adapter_down_maps,
    adapter_up_maps,
):
    sides, seats = lax.axis_size("cfg"), lax.axis_size("seq")
    side, place, core = (lax.axis_index(a) for a in ("cfg", "seq", "clip"))
    frames = clean.shape[0] * seats
    width = clean.shape[2]
    seat = jnp.stack([side, place, core]).astype(jnp.int32)
    moved = timestep[0] * timestep_direction.astype(jnp.float32)
    cond_shift = (moved + condition_vector.astype(jnp.float32))[None]
    uncond_shift = (moved + empty_prompt_vector.astype(jnp.float32))[None]
    down = jnp.swapaxes(adapter_down_maps, 1, 2).reshape(-1, width)
    up = adapter_up_maps.reshape(-1, sides, 2, 2, seats // 4, HEAD_DIM)
    up = jnp.swapaxes(up, 3, 4).reshape(-1, width)

    noisy_lines = noisy_pieces(seat, timestep, clean, noise, seats)
    space_own = half_weights(spatial_query_key_value, spatial_output_weight, core)
    time_own = half_weights(temporal_query_key_value, temporal_output_weight, core)
    across = place // (seats // 4)

    space_near = z_pair(space_own, across)
    space_near, time_own = together(space_near, time_own)
    space_in = over_middle(space_near)
    space = [space_near, flip(space_near, "seq", 1), flip(space_near, "cfg", 1)]
    time_near = z_pair(time_own, across)
    space_other = other_core([space_near])
    space, space_other, space_in, time_near = together(space, space_other, space_in, time_near)

    space_far = to_ends(space_in, across)
    space_xy = flip(space[2], "seq", 1)
    time_in = over_middle(time_near)
    time_x = flip(time_near, "cfg", 1)
    space_other += other_core(space[1:])
    space += [space_xy, space_far]
    space, space_other, time_in, time_x, time_near, noisy_lines, down, up = together(
        space, space_other, time_in, time_x, time_near, noisy_lines, down, up
    )

    space_far_x = flip(space[4], "cfg", 1)
    space_far_y = flip(space[4], "seq", 1)
    time_far = to_ends(time_in, across)
    space_xy_other, time_near_other = other_core([space[3], time_near])
    space += [space_far_y, space_far_x]
    space_other += [space_xy_other]
    time_other = [time_near_other]
    space, space_other, time_other, time_far, time_near, time_x, noisy_lines = together(
        space, space_other, time_other, time_far, time_near, time_x, noisy_lines
    )

    space_far_xy = flip(space[5], "cfg", 1)
    time_y = flip(time_near, "seq", 1)
    noisy_1 = flip(noisy_lines[1], "seq", 2)
    *space_far_other, time_x_other = other_core(space[4:] + [time_x])
    space.append(space_far_xy)
    space_other += space_far_other
    time_other += [time_x_other]
    space, space_other, time_x, time_y, time_far, time_near, time_other, noisy_came = together(
        space, space_other, time_x, time_y, time_far, time_near, time_other,
        [noisy_lines[0], noisy_1, *noisy_lines[2:]],
    )

    space_last, time_far_other, time_y_other = (
        flip(piece, "clip", 1) for piece in (space[7], time_far, time_y)
    )
    space_other += [space_last]
    time_other += [time_far_other, time_y_other]
    space, space_other, time_x, time_y, time_far, time_near, time_other, noisy_came = together(
        space, space_other, time_x, time_y, time_far, time_near, time_other, noisy_came
    )
    space_weights = (
        list(space) + list(space_other),
        [(index, None, index // 8, (NEAR + FAR)[index % 8]) for index in range(16)],
    )
    cond, uncond = [
        functools.partial(
            spatial_layer, seat, timestep, clean, noise, shift, limit,
            frames=clean.shape[0] // sides, seats=seats,
        )
        for shift, limit in (
            (cond_shift, SPACE_VMEM_LIMIT), (uncond_shift, FULL_VMEM_LIMIT)
        )
    ]
    time_xy = flip(time_y, "cfg", 1)
    time_far_x = flip(time_far, "cfg", 1)
    time_far_y = flip(time_far, "seq", 1)
    noisy_came = list(noisy_came[:2]) + [
        flip(line, "seq", 2 * index) for index, line in enumerate(noisy_came) if index > 1
    ]
    cond = cond(weights=space_weights)
    cond, time_xy, time_far_x, time_far_y, noisy_came = together(
        cond, time_xy, time_far_x, time_far_y, noisy_came
    )
    time_late = [flip(piece, "clip", 1) for piece in (time_xy, time_far_y, time_far_x)]
    half = len(noisy_came) // 2
    noisy_low = jnp.stack([line[1] for line in noisy_came[:half]])
    noisy_last = jnp.stack([line[1] for line in noisy_came[half:]])
    cond, time_far_y, time_late, noisy_low, noisy_last = together(
        cond, time_far_y, time_late, noisy_low, noisy_last
    )
    uncond = uncond(weights=space_weights)
    time_far_xy = flip(time_far_y, "cfg", 1)
    noisy_low = flip(noisy_low, "seq", 1)
    cond, uncond, time_far_xy, noisy_low, noisy_last = together(
        to_neighbours(*cond), uncond, time_far_xy, noisy_low, noisy_last
    )
    noisy_last = flip(noisy_last, "seq", 1)
    lines = [jnp.stack([given[line] for given in cond]) for line in range(seats // 2)]
    far_lines = [flip(lines[i], "seq", 2 * i) for i in range(2, seats // 2)]
    time_last = flip(time_far_xy, "clip", 1)
    uncond, time_last, noisy_last = together(uncond, time_last, noisy_last)
    time_weights = (
        [time_near, time_y, time_x, time_xy, time_far, time_far_y, time_far_x, time_far_xy]
        + list(time_other) + list(time_late) + [time_last],
        [(index, None, 0, at) for index, at in enumerate(NEAR + FAR)]
        + [
            (8 + index, None, 1, at)
            for index, at in enumerate(
                [NEAR[0], NEAR[2], FAR[0], NEAR[1], NEAR[3], FAR[1], FAR[2], FAR[3]]
            )
        ],
    )
    noisy_in = list(noisy_came) + [noisy_low, noisy_last]
    kept, low, across, both = uncond
    low, across, both = flip(low, "seq", 1), flip(across, "cfg", 1), over_both(both)
    rows, primal = student_rows(seat, cond_shift, down, up, time_weights, noisy_in, frames)
    rows, primal, low, across, both, lines = together(rows, primal, low, across, both, lines)
    near_line = flip(lines[1], "seq", 2)
    uncond = [
        jnp.stack([given[line] for given in (kept, low, across, both)])
        for line in range(seats // 2)
    ]
    uncond_last = flip(uncond[-1], "seq", seats - 2)
    student_kept, student_low = student_mix(
        seat, cond_shift, rows, primal, time_weights, frames, seats
    )
    cond = [lines[0], near_line, *far_lines]
    student_kept, student_low, cond, uncond = together(student_kept, student_low, cond, uncond)
    uncond = [
        flip(line, "seq", 2 * index) if index > 0 else line
        for index, line in enumerate(uncond[:-1])
    ] + [uncond_last]
    velocity = teacher_velocity(seat, time_weights, cond, frames)
    student_low, velocity, uncond = together(flip(student_low, "seq", 1), velocity, uncond)
    student_back = along_line([student_kept, student_low])
    tangent = functools.partial(
        student_tangent, seat, guidance, cond_shift, down, up, velocity, rows, primal,
        time_weights, frames=frames, seats=seats,
    )
    *tangent_pieces, other = tangent(uncond)
    student_back, other, tangent_pieces = together(student_back, other, tangent_pieces)
    tangent_back = send(tangent_pieces)
    rest, tangent_back = together(tangent([other]), tangent_back)
    tangent_back = list(tangent_back) + send(rest)
    here = clean.shape[0]
    return placed(seat, student_back, seats, here), placed(seat, tangent_back, seats, here)


def fits(mesh, frames, positions, width):
    sides, seats = mesh.shape["cfg"], mesh.shape["seq"]
    groups = sides * seats
    return (
        sides == 2
        and mesh.shape["clip"] == 2
        and seats == 4 * sides
        and frames % (groups * ROW_TILE // 4) == 0
        and positions == groups * ROW_TILE
        and 2 * frames == LANES
        and width % LANES == 0
        and width == groups * HEAD_DIM
    )

def solution(mesh):
    specs = dict(
        mesh=mesh,
        in_specs=(
            P(("clip", "seq"), None, None),
            P(("clip", "seq"), None, None),
            P("clip"),
            P("clip"),
            P("clip"),
            P(),
            P(),
            P(None, None, ("cfg", "seq")),
            P(("cfg", "seq"), None),
            P(None, None, ("cfg", "seq")),
            P(("cfg", "seq"), None),
            P(),
            P(),
        ),
        out_specs=(P(("clip", "seq"), "cfg", None), P(("clip", "seq"), "cfg", None)),
        check_vma=False,
    )

    def whole(clean, *rest):
        frames = clean.shape[0] // mesh.shape["clip"]
        fast = fits(mesh, frames, clean.shape[1], clean.shape[2])
        return jax.shard_map(on_device if fast else plain_on_device, **specs)(clean, *rest)

    return whole
```

```python
import functools
import math

import jax
import jax.numpy as jnp
from jax import lax
from jax.experimental import pallas as pl
from jax.experimental.pallas import tpu as pltpu
from jax.sharding import PartitionSpec as P

HEAD_DIM = 72
LANES = 128
ROW_TILE = 16
BLOCK = 8
EXPONENT_SCALE = HEAD_DIM ** (-0.5) * math.log2(math.e)
VMEM_LIMIT = 40 * 1024 * 1024
SPACE_VMEM_LIMIT = 26 * 1024 * 1024
FULL_VMEM_LIMIT = 60 * 1024 * 1024
TANGENT_VMEM_LIMIT = 50 * 1024 * 1024

epsilon = 1e-06


def partner(value, axis, bit):
    mask = 2**bit
    pairs = [(source, source ^ mask) for source in range(lax.axis_size(axis))]
    return lax.ppermute(value, axis, pairs)


def rms_scale(features):
    return features * lax.rsqrt(jnp.mean(features * features, axis=-1, keepdims=True) + epsilon)


def project(rows_in, matrix):
    return jnp.einsum("...d,dk->...k", rows_in, matrix, preferred_element_type=jnp.float32)


def space_attend(queries, key_rows, value_rows):
    head_count = queries.shape[-1] // HEAD_DIM
    split_dims = queries.shape[:-1] + (head_count, HEAD_DIM)
    scores = jnp.einsum(
        "...qhd,...khd->...hqk",
        queries.reshape(split_dims),
        key_rows.reshape(split_dims),
        preferred_element_type=jnp.float32,
    ) * HEAD_DIM ** (-0.5)
    scores = scores - jnp.max(scores, axis=-1, keepdims=True)
    exponent = jnp.exp(scores)
    soft_weights = (exponent / jnp.sum(exponent, axis=-1, keepdims=True)).astype(jnp.bfloat16)
    result = jnp.einsum(
        "...hqk,...khd->...qhd",
        soft_weights,
        value_rows.reshape(split_dims),
        preferred_element_type=jnp.float32,
    )
    return result.astype(jnp.bfloat16).reshape(queries.shape)


def time_attend(queries, key_rows, value_rows):
    head_count = queries.shape[-1] // HEAD_DIM
    split_dims = queries.shape[:-1] + (head_count, HEAD_DIM)
    scores = jnp.einsum(
        "...fxhd,...gxhd->...xhfg",
        queries.reshape(split_dims),
        key_rows.reshape(split_dims),
        preferred_element_type=jnp.float32,
    ) * HEAD_DIM ** (-0.5)
    scores = scores - jnp.max(scores, axis=-1, keepdims=True)
    exponent = jnp.exp(scores)
    soft_weights = (exponent / jnp.sum(exponent, axis=-1, keepdims=True)).astype(jnp.bfloat16)
    result = jnp.einsum(
        "...xhfg,...gxhd->...fxhd",
        soft_weights,
        value_rows.reshape(split_dims),
        preferred_element_type=jnp.float32,
    )
    return result.astype(jnp.bfloat16).reshape(queries.shape)


def time_core(embedding_rows, query_weight, key_weight, value_weight, out_weight):
    normed = rms_scale(embedding_rows).astype(jnp.bfloat16)
    queries = project(normed, query_weight).astype(jnp.bfloat16)
    key_rows = project(normed, key_weight).astype(jnp.bfloat16)
    value_rows = project(normed, value_weight).astype(jnp.bfloat16)
    return project(time_attend(queries, key_rows, value_rows), out_weight)


def student_network(
    embedding_rows,
    query_weight,
    key_weight,
    value_weight,
    out_weight,
    down_query,
    query_up_map,
    down_value,
    value_up_map,
):
    normed = rms_scale(embedding_rows).astype(jnp.bfloat16)
    low_query = project(normed, down_query).astype(jnp.bfloat16)
    low_value = project(normed, down_value).astype(jnp.bfloat16)
    queries = (project(normed, query_weight) + project(low_query, query_up_map)).astype(
        jnp.bfloat16
    )
    key_rows = project(normed, key_weight).astype(jnp.bfloat16)
    value_rows = (project(normed, value_weight) + project(low_value, value_up_map)).astype(
        jnp.bfloat16
    )
    return project(time_attend(queries, key_rows, value_rows), out_weight)


def plain_on_device(
    clean,
    noise,
    timestep,
    guidance,
    condition_vector,
    empty_prompt_vector,
    timestep_direction,
    spatial_query_key_value,
    spatial_output_weight,
    temporal_query_key_value,
    temporal_output_weight,
    adapter_down_maps,
    adapter_up_maps,
):
    moment = timestep[0]
    strength = guidance[0]
    pair_side = lax.axis_index("cfg")
    noisy_rows = (
        (1.0 - moment) * clean.astype(jnp.float32) + moment * noise.astype(jnp.float32)
    ).astype(jnp.bfloat16)
    shifted = noisy_rows.astype(jnp.float32) + moment * timestep_direction.astype(jnp.float32)
    embeds = jnp.where(pair_side == 0, condition_vector, empty_prompt_vector)[None]
    branch_count = embeds.shape[0]
    entries = shifted[None] + embeds.astype(jnp.float32)[:, None, None, :]
    normed = rms_scale(entries).astype(jnp.bfloat16)
    triple = jnp.einsum(
        "bfpd,jdk->jbfpk",
        normed,
        lax.all_gather(spatial_query_key_value, ("cfg", "seq"), axis=2, tiled=True),
        preferred_element_type=jnp.float32,
    ).astype(jnp.bfloat16)
    attended = space_attend(triple[0], triple[1], triple[2])
    partial_value = jnp.einsum(
        "bfpk,kd->bfpd",
        attended,
        lax.all_gather(spatial_output_weight, ("cfg", "seq"), axis=0, tiled=True),
        preferred_element_type=jnp.float32,
    )
    layer_one = (entries + partial_value).astype(jnp.bfloat16)
    frame_count = layer_one.shape[1]
    position_count = layer_one.shape[2]
    width = layer_one.shape[3]
    stacked = jnp.concatenate([layer_one, noisy_rows[None]], axis=0).reshape(
        branch_count + 1, frame_count, 2, position_count // 2, width
    )
    regrouped = lax.all_to_all(stacked, "seq", split_axis=3, concat_axis=1, tiled=True)
    frames = regrouped.shape[1]
    local_rows = regrouped.shape[3]
    teacher_in = regrouped[:branch_count].reshape(branch_count, frames, 2 * local_rows, width)
    noisy_local = regrouped[branch_count]
    time_qkv, time_out = (
        lax.all_gather(temporal_query_key_value, ("cfg", "seq"), axis=2, tiled=True),
        lax.all_gather(temporal_output_weight, ("cfg", "seq"), axis=0, tiled=True),
    )
    teacher_part = time_core(
        teacher_in.astype(jnp.float32), time_qkv[0], time_qkv[1], time_qkv[2], time_out
    )
    velocity = (
        (teacher_in.astype(jnp.float32) + teacher_part)
        .astype(jnp.bfloat16)
        .reshape(branch_count, frames, 2, local_rows, width)
    )
    own_velocity = velocity[0]
    own_half = lax.dynamic_index_in_dim(own_velocity, pair_side, 1, keepdims=False)
    outgoing = lax.dynamic_index_in_dim(own_velocity, 1 - pair_side, 1, keepdims=False)
    other_half = partner(outgoing, "cfg", 0)
    is_first = pair_side == 0
    cond_velocity = jnp.where(is_first, own_half, other_half)
    uncond_velocity = jnp.where(is_first, other_half, own_half)
    student_noisy = lax.dynamic_index_in_dim(noisy_local, pair_side, 1, keepdims=False)
    query_up_map = adapter_up_maps[0]
    value_up_map = adapter_up_maps[1]
    uncond_float = uncond_velocity.astype(jnp.float32)
    guided = (uncond_float + strength * (cond_velocity.astype(jnp.float32) - uncond_float)).astype(
        jnp.bfloat16
    )
    student_in = (
        student_noisy.astype(jnp.float32)
        + moment * timestep_direction.astype(jnp.float32)
        + condition_vector.astype(jnp.float32)
    )

    def student_map(embedding_rows):
        return student_network(
            embedding_rows,
            time_qkv[0],
            time_qkv[1],
            time_qkv[2],
            time_out,
            adapter_down_maps[0],
            query_up_map,
            adapter_down_maps[1],
            value_up_map,
        )

    partial_value, tangent_part = jax.jvp(student_map, (student_in,), (guided.astype(jnp.float32),))
    primal = (student_in + partial_value).astype(jnp.bfloat16)
    tangent = (guided.astype(jnp.float32) + tangent_part).astype(jnp.bfloat16)
    returned = lax.all_to_all(
        jnp.stack([primal, tangent]), "seq", split_axis=1, concat_axis=2, tiled=True
    )
    return (returned[0], returned[1])


def dot(left, right):
    return lax.dot_general(
        left, right, (((1,), (0,)), ((), ())), preferred_element_type=jnp.float32
    )


def dot_t(left, right):
    return lax.dot_general(
        left, right, (((1,), (1,)), ((), ())), preferred_element_type=jnp.float32
    )


def lane_range(shape, start, low, high):
    lane = lax.broadcasted_iota(jnp.int32, shape, len(shape) - 1) + start
    return (lane >= low) & (lane < high)


def only(value, keep):
    return jnp.where(keep, value, jnp.zeros_like(value))


def window_of(low, high):
    start = low // LANES * LANES
    return start, -(-high // LANES) * LANES - start


def inverse_rms(features):
    return lax.rsqrt(jnp.mean(features * features, axis=-1, keepdims=True) + epsilon)


def weight_copies(seat, layout, pieces, weights_ref, sems):
    side, place, core = seat[0], seat[1], seat[2]
    across, along = place // 4, lax.rem(place, 2)
    copies = []
    for array, part, sibling, (x, z, y) in layout:
        piece = pieces[array] if part is None else pieces[array].at[part]
        count, rows = piece.shape[:2]
        block = ((side ^ x) * 2 + (across ^ z)) * 2 + (along ^ y)
        start = pl.multiple_of(block * rows, ROW_TILE)
        copies.append(
            pltpu.make_async_copy(
                piece,
                weights_ref.at[pl.ds((core ^ sibling) * count, count), pl.ds(start, rows), :],
                sems.at[len(copies)],
            )
        )
    return copies


def noisy_kernel(seat_ref, moment_ref, clean_ref, noise_ref, *rest):
    line_refs, rows_ref = rest[:-1], rest[-1]
    moment = moment_ref[0]
    rows_ref[...] = (
        (1.0 - moment) * clean_ref[0].astype(jnp.float32)
        + moment * noise_ref[0].astype(jnp.float32)
    ).astype(jnp.bfloat16)
    for index in range(2 * len(line_refs)):
        start = pl.multiple_of((seat_ref[1] ^ index) * ROW_TILE, ROW_TILE)
        line_refs[index // 2][index % 2, 0] = rows_ref[pl.ds(start, ROW_TILE), :]


def noisy_pieces(seat, moment, clean, noise, seats):
    frames, positions, width = clean.shape
    rows = seats * ROW_TILE
    block = pl.BlockSpec((1, rows, width), lambda f, seat: (f, seat[0], 0))
    half = seats // 2
    piece = jax.ShapeDtypeStruct((2, frames, ROW_TILE, width), jnp.bfloat16)
    out_block = pl.BlockSpec((2, 1, ROW_TILE, width), lambda f, seat: (0, f, 0, 0))
    return pl.pallas_call(
        noisy_kernel,
        out_shape=[piece] * half,
        grid_spec=pltpu.PrefetchScalarGridSpec(
            num_scalar_prefetch=1,
            grid=(frames,),
            in_specs=[pl.BlockSpec(memory_space=pltpu.SMEM), block, block],
            out_specs=[out_block] * half,
            scratch_shapes=[pltpu.VMEM((rows, width), jnp.bfloat16)],
        ),
        compiler_params=pltpu.CompilerParams(vmem_limit_bytes=VMEM_LIMIT),
    )(seat, moment, clean, noise)


def space_kernel(layout, pieces, targets, seat_ref, moment_ref, clean_ref, noise_ref, shift_ref, *rest):
    weight_pieces, sent_refs = rest[:pieces], rest[pieces : pieces + targets]
    weights_ref, query_ref, key_ref, value_ref, mixed_ref, sems = rest[pieces + targets :]
    moment = moment_ref[0]
    positions, width = key_ref.shape

    @pl.when(pl.program_id(0) == 0)
    def _():
        wait_all(start_all(weight_copies(seat_ref, layout, weight_pieces, weights_ref, sems)))

    noisy = (
        (1.0 - moment) * clean_ref[0].astype(jnp.float32)
        + moment * noise_ref[0].astype(jnp.float32)
    ).astype(jnp.bfloat16)
    entry = noisy.astype(jnp.float32) + shift_ref[...]
    normed = (entry * inverse_rms(entry)).astype(jnp.bfloat16)
    query_ref[...] = dot_t(normed, weights_ref[0]).astype(jnp.bfloat16)
    key_ref[...] = dot_t(normed, weights_ref[1]).astype(jnp.bfloat16)
    value_ref[...] = dot_t(normed, weights_ref[2]).astype(jnp.bfloat16)

    weights = []
    for head in range(width // HEAD_DIM):
        low, high = head * HEAD_DIM, (head + 1) * HEAD_DIM
        start, extent = window_of(low, high)
        keep = lane_range((positions, extent), start, low, high)
        queries = only(query_ref[:, pl.ds(start, extent)], keep)
        scores = dot_t(queries, key_ref[:, pl.ds(start, extent)])
        top = jnp.max(scores, axis=-1, keepdims=True)
        exponent = jnp.exp2((scores - top) * EXPONENT_SCALE)
        total = jnp.sum(exponent, axis=-1, keepdims=True)
        weights.append((exponent * (1.0 / total)).astype(jnp.bfloat16))
        tile = high // (2 * LANES)
        done = [low // (2 * LANES)] if tile > low // (2 * LANES) else []
        if head == width // HEAD_DIM - 1:
            done = [(width - 1) // (2 * LANES)]
        for full in done:
            left_edge = full * 2 * LANES
            edge = min(width, left_edge + 2 * LANES)
            heads = range(left_edge // HEAD_DIM, -(-edge // HEAD_DIM))
            values = value_ref[:, pl.ds(left_edge, edge - left_edge)]
            parts = [
                only(
                    values,
                    lane_range(values.shape, left_edge, h * HEAD_DIM, (h + 1) * HEAD_DIM),
                )
                for h in heads
            ]
            mixed = dot(
                jnp.concatenate([weights[h] for h in heads], axis=1),
                jnp.concatenate(parts, axis=0),
            )
            mixed_ref[:, pl.ds(left_edge, edge - left_edge)] = mixed.astype(jnp.bfloat16)

    query_ref[...] = (entry + dot(mixed_ref[...], weights_ref[3])).astype(jnp.bfloat16)
    lines = sent_refs[0].shape[0]
    for index, ref in enumerate(sent_refs):
        for line in range(lines):
            seat = (seat_ref[0] ^ (index // 2)) * lines * 2 + (
                seat_ref[1] ^ (line * 2 + index % 2)
            )
            start = pl.multiple_of(seat * ROW_TILE, ROW_TILE)
            ref[line, 0] = query_ref[pl.ds(start, ROW_TILE), :]


def spatial_layer(seat, moment, clean, noise, shift, limit, weights, frames, seats):
    pieces, layout = weights
    positions, width = clean.shape[1:]
    frame_block = pl.BlockSpec(
        (1, positions, width), lambda f, seat: (seat[0] * frames + f, 0, 0)
    )
    lines = seats // 2
    piece = jax.ShapeDtypeStruct((lines, frames, ROW_TILE, width), jnp.bfloat16)
    vmem = lambda *shape: pltpu.VMEM(shape, jnp.bfloat16)
    rows = frames * positions
    return pl.pallas_call(
        functools.partial(space_kernel, layout, len(pieces), 4),
        out_shape=[piece] * 4,
        grid_spec=pltpu.PrefetchScalarGridSpec(
            num_scalar_prefetch=1,
            grid=(frames,),
            in_specs=[
                pl.BlockSpec(memory_space=pltpu.SMEM),
                frame_block,
                frame_block,
                pl.BlockSpec(shift.shape, lambda f, seat: (0, 0)),
            ]
            + [pl.BlockSpec(memory_space=pl.ANY)] * len(pieces),
            out_specs=[
                pl.BlockSpec((lines, 1, ROW_TILE, width), lambda f, seat: (0, f, 0, 0))
            ]
            * 4,
            scratch_shapes=[vmem(4, width, width)]
            + [vmem(positions, width)] * 4
            + [pltpu.SemaphoreType.DMA((len(layout),))],
        ),
        compiler_params=pltpu.CompilerParams(vmem_limit_bytes=limit),
        cost_estimate=pl.CostEstimate(
            flops=14 * rows * width * width,
            bytes_accessed=8 * width * width + 6 * rows * width,
            transcendentals=rows * positions * width // HEAD_DIM,
        ),
    )(seat, moment, clean, noise, shift, *pieces)


def swap_matrix(rows, columns):
    count = rows * columns
    target = lax.broadcasted_iota(jnp.int32, (count, count), 0)
    source = lax.broadcasted_iota(jnp.int32, (count, count), 1)
    moved = lax.rem(target, rows) * columns + lax.div(target, rows)
    return jnp.where(source == moved, 1.0, 0.0).astype(jnp.bfloat16)


def halves(value, frames, reduce):
    first = lane_range(value.shape, 0, 0, frames)
    if reduce == "max":
        low = jnp.max(jnp.where(first, value, -jnp.inf), axis=-1, keepdims=True)
        high = jnp.max(jnp.where(first, -jnp.inf, value), axis=-1, keepdims=True)
    else:
        low = jnp.sum(jnp.where(first, value, 0.0), axis=-1, keepdims=True)
        high = jnp.sum(jnp.where(first, 0.0, value), axis=-1, keepdims=True)
    return first, low, high


def time_mix(frames, refs, tangents=None):
    query_ref, key_ref, value_ref, mixed_ref = refs
    rows, width = query_ref.shape
    scale = HEAD_DIM ** (-0.5)
    tiles = [[] for _ in range(width // LANES)]
    tangent_tiles = [[] for _ in range(width // LANES)]
    pairs = width // (2 * HEAD_DIM)
    blocks = [pl.ds(i * frames, frames) for i in range(rows // frames)]

    def stack(value, start, low):
        shape = value.shape
        return jnp.concatenate(
            [
                only(value, lane_range(shape, start, low, low + HEAD_DIM)),
                only(value, lane_range(shape, start, low + HEAD_DIM, low + 2 * HEAD_DIM)),
            ],
            axis=0,
        )

    for pair in range(pairs):
        low = pair * 2 * HEAD_DIM
        start, extent = window_of(low, low + 2 * HEAD_DIM)
        columns = pl.ds(start, extent)
        keys = [stack(key_ref[b, columns], start, low) for b in blocks]
        values = [stack(value_ref[b, columns], start, low) for b in blocks]
        scores = jnp.concatenate(
            [dot_t(query_ref[b, columns], k) for b, k in zip(blocks, keys)], axis=0
        )
        first, top_low, top_high = halves(scores, frames, "max")
        exponent = jnp.exp2((scores - jnp.where(first, top_low, top_high)) * EXPONENT_SCALE)
        _, sum_low, sum_high = halves(exponent, frames, "sum")
        weights = exponent * jnp.where(first, 1.0 / sum_low, 1.0 / sum_high)
        rounded = weights.astype(jnp.bfloat16)
        mixed = jnp.concatenate(
            [
                dot(rounded[i * frames : (i + 1) * frames], v)
                for i, v in enumerate(values)
            ],
            axis=0,
        )
        for tile in range(extent // LANES):
            tiles[start // LANES + tile].append(mixed[:, tile * LANES : (tile + 1) * LANES])
        if tangents is not None:
            query_dot, key_dot, value_dot, _ = tangents
            score_dots = jnp.concatenate(
                [
                    dot_t(query_dot[b, columns], k)
                    + dot_t(query_ref[b, columns], stack(key_dot[b, columns], start, low))
                    for b, k in zip(blocks, keys)
                ],
                axis=0,
            ) * scale
            _, mean_low, mean_high = halves(weights * score_dots, frames, "sum")
            weight_dots = (
                weights * (score_dots - jnp.where(first, mean_low, mean_high))
            ).astype(jnp.bfloat16)
            mixed_dots = jnp.concatenate(
                [
                    dot(
                        jnp.concatenate(
                            [
                                weight_dots[i * frames : (i + 1) * frames],
                                rounded[i * frames : (i + 1) * frames],
                            ],
                            axis=1,
                        ),
                        jnp.concatenate(
                            [v, stack(value_dot[b, columns], start, low)], axis=0
                        ),
                    )
                    for i, (b, v) in enumerate(zip(blocks, values))
                ],
                axis=0,
            )
            for tile in range(extent // LANES):
                tangent_tiles[start // LANES + tile].append(
                    mixed_dots[:, tile * LANES : (tile + 1) * LANES]
                )
    for tile in range(width // LANES):
        columns = pl.ds(tile * LANES, LANES)
        mixed_ref[:, columns] = functools.reduce(jnp.add, tiles[tile]).astype(jnp.bfloat16)
        if tangents is not None:
            tangents[3][:, columns] = functools.reduce(jnp.add, tangent_tiles[tile]).astype(
                jnp.bfloat16
            )


def arrivals(seat, pieces, came_ref, sems):
    copies = []
    for line, piece in enumerate(pieces):
        neighbours, frames = piece.shape[:2]
        for index in range(neighbours):
            first = (seat[1] ^ (line * 2 + index % 2)) * frames * (neighbours // 2)
            if neighbours > 2:
                first = first + (seat[0] ^ (index // 2)) * frames
            copies.append(
                pltpu.make_async_copy(
                    piece.at[index], came_ref.at[pl.ds(first, frames)], sems.at[len(copies)]
                )
            )
    return copies


def departures(seat, going_ref, pieces, sems):
    rows = pieces[0].shape[0]
    return [
        pltpu.make_async_copy(
            going_ref.at[pl.ds(pl.multiple_of((seat[1] ^ index) * rows, ROW_TILE), rows)],
            piece,
            sems.at[index],
        )
        for index, piece in enumerate(pieces)
    ]


def by_position(came_ref, rows_ref):
    frames, positions, width = came_ref.shape
    turn = swap_matrix(ROW_TILE, positions)
    for part in range(frames // ROW_TILE):
        first = part * ROW_TILE
        piece = came_ref[first : first + ROW_TILE].reshape(ROW_TILE * positions, width)
        turned = dot(turn, piece).astype(jnp.bfloat16)
        for position in range(positions):
            rows_ref[pl.ds(position * frames + first, ROW_TILE), :] = turned[
                position * ROW_TILE : (position + 1) * ROW_TILE
            ]


def by_frame(rows_ref, going_ref, frames):
    positions = rows_ref.shape[0] // frames
    group = min(frames, 2 * LANES // positions)
    turn = swap_matrix(positions, group)
    for part in range(frames // group):
        piece = jnp.concatenate(
            [rows_ref[pl.ds(p * frames + part * group, group), :] for p in range(positions)],
            axis=0,
        )
        here = pl.ds(part * group * positions, group * positions)
        going_ref[here, :] = dot(turn, piece).astype(jnp.bfloat16)


def wait_all(copies):
    for copy in copies:
        copy.wait()


def start_all(copies):
    for copy in copies:
        copy.start()
    return copies


def adapted(rows_in, weights_ref, down_ref, up_ref, refs):
    rank = down_ref.shape[0] // 2
    low = dot_t(rows_in, down_ref[...]).astype(jnp.bfloat16)
    first = lane_range(low.shape, 0, 0, rank)
    refs[0][...] = (
        dot_t(rows_in, weights_ref[0]) + dot(only(low, first), up_ref[...])
    ).astype(jnp.bfloat16)
    refs[1][...] = dot_t(rows_in, weights_ref[1]).astype(jnp.bfloat16)
    refs[2][...] = (
        dot_t(rows_in, weights_ref[2]) + dot(only(low, jnp.logical_not(first)), up_ref[...])
    ).astype(jnp.bfloat16)


def student_rows_kernel(layout, counts, seat_ref, shift_ref, down_ref, up_ref, *rest):
    weight_count, piece_count = counts
    weight_pieces, rest = rest[:weight_count], rest[weight_count:]
    pieces, rest = rest[:piece_count], rest[piece_count:]
    rows_out_ref, primal_ref, weights_ref, came_ref, rows_ref, weight_sems, piece_sems = rest
    chunk = rows_out_ref.shape[0]

    @pl.when(pl.program_id(0) == 0)
    def _():
        weights = weight_copies(seat_ref, layout, weight_pieces, weights_ref, weight_sems)
        lines = piece_count - 2
        copies = []
        for index in range(2 * lines):
            if index % 2:
                part, line = divmod(index // 2, lines // 2)
                piece = pieces[lines + part].at[line]
            else:
                piece = pieces[index // 2].at[0]
            count = piece.shape[0]
            copies.append(
                pltpu.make_async_copy(
                    piece,
                    came_ref.at[pl.ds((seat_ref[1] ^ index) * count, count)],
                    piece_sems.at[index],
                )
            )
        start_all(copies)
        start_all(weights)
        wait_all(copies)
        by_position(came_ref, rows_ref)
        wait_all(weights)

    here = pl.ds(pl.multiple_of(pl.program_id(0) * chunk, chunk), chunk)
    rows_out_ref[...] = rows_ref[here, :]
    entry = rows_ref[here, :].astype(jnp.float32) + shift_ref[...]
    normed = (entry * inverse_rms(entry)).astype(jnp.bfloat16)
    adapted(normed, weights_ref, down_ref, up_ref, [primal_ref.at[i] for i in range(3)])


def student_mix_kernel(layout, frames, seat_ref, shift_ref, rows_ref, primal_ref, *rest):
    weight_pieces, out_refs, rest = rest[:-7], rest[-7:-5], rest[-5:]
    weights_ref, done_ref, mixed_ref, weight_sems, piece_sems = rest
    step, chunk = pl.program_id(0), mixed_ref.shape[0]
    weights = weight_copies(seat_ref, layout, weight_pieces, weights_ref, weight_sems)

    @pl.when(step == 0)
    def _():
        start_all(weights)

    time_mix(frames, [primal_ref.at[i] for i in range(3)] + [mixed_ref])

    @pl.when(step == 0)
    def _():
        wait_all(weights)

    here = pl.ds(pl.multiple_of(step * chunk, chunk), chunk)
    entry = rows_ref[...].astype(jnp.float32) + shift_ref[...]
    done_ref[0, here, :] = (entry + dot(mixed_ref[...], weights_ref[3])).astype(jnp.bfloat16)

    @pl.when(step == pl.num_programs(0) - 1)
    def _():
        by_frame(done_ref.at[0], done_ref.at[1], frames)
        pieces = [ref.at[line] for line in range(out_refs[0].shape[0]) for ref in out_refs]
        wait_all(start_all(departures(seat_ref, done_ref.at[1], pieces, piece_sems)))


def teacher(frames, rows_ref, weights_ref, refs, here):
    entry = rows_ref[here, :].astype(jnp.float32)
    normed = (entry * inverse_rms(entry)).astype(jnp.bfloat16)
    for index, ref in enumerate(refs[:3]):
        ref[...] = dot_t(normed, weights_ref[index]).astype(jnp.bfloat16)
    time_mix(frames, refs)
    entry = rows_ref[here, :].astype(jnp.float32)
    return (entry + dot(refs[3][...], weights_ref[3])).astype(jnp.bfloat16)


def teacher_kernel(layout, counts, seat_ref, *rest):
    weight_count, piece_count = counts
    weight_pieces, rest = rest[:weight_count], rest[weight_count:]
    pieces, rest = rest[:piece_count], rest[piece_count:]
    velocity_ref, weights_ref, came_ref, rows_ref = rest[:4]
    refs, (weight_sems, piece_sems) = rest[4:8], rest[8:]
    frames = came_ref.shape[0]
    chunk = refs[0].shape[0]

    @pl.when(pl.program_id(0) == 0)
    def _():
        came = start_all(arrivals(seat_ref, pieces, came_ref, piece_sems))
        weights = start_all(
            weight_copies(seat_ref, layout, weight_pieces, weights_ref, weight_sems)
        )
        wait_all(came)
        by_position(came_ref, rows_ref)
        wait_all(weights)

    here = pl.ds(pl.multiple_of(pl.program_id(0) * chunk, chunk), chunk)
    velocity_ref[...] = teacher(frames, rows_ref, weights_ref, refs, here)


def tangent_kernel(layout, counts, seat_ref, strength_ref, shift_ref, down_ref, up_ref, *rest):
    weight_count, piece_count, out_count = counts
    velocity_ref, noisy_ref, primal_ref = rest[:3]
    rest = rest[3:]
    weight_pieces, rest = rest[:weight_count], rest[weight_count:]
    pieces, rest = rest[:piece_count], rest[piece_count:]
    out_pieces, rest = rest[:out_count], rest[out_count:]
    weights_ref, done_ref, going_ref, guided_ref, *tail = rest[-14:]
    refs, dots, (weight_sems, piece_sems) = tail[:4], tail[4:8], tail[8:10]
    frames = done_ref.shape[0] // (ROW_TILE // 2)
    chunk = refs[0].shape[0]
    step = pl.program_id(0)
    first = piece_count > 1

    @pl.when(step == 0)
    def _():
        weights = weight_copies(seat_ref, layout, weight_pieces, weights_ref, weight_sems)
        if first:
            other_ref, came_ref, rows_ref = rest[:3]
            came = start_all(arrivals(seat_ref, pieces, came_ref, piece_sems))
        start_all(weights)
        if first:
            wait_all(came)
            by_position(came_ref, rows_ref)
            half = other_ref.shape[0]
            other_ref[...] = rows_ref[pl.ds(half, half), :]
        wait_all(weights)

    here = pl.ds(pl.multiple_of(step * chunk, chunk), chunk)
    rows_ref = rest[2].at[here] if first else pieces[0]
    uncond = teacher(frames, rows_ref, weights_ref, refs, slice(None)).astype(jnp.float32)
    guided = (
        uncond + strength_ref[0] * (velocity_ref[...].astype(jnp.float32) - uncond)
    ).astype(jnp.bfloat16)
    guided_ref[...] = guided
    guided = guided.astype(jnp.float32)
    entry = noisy_ref[...].astype(jnp.float32) + shift_ref[...]
    inverse = inverse_rms(entry)
    inverse_dot = -(inverse * inverse * inverse) * jnp.mean(
        entry * guided, axis=-1, keepdims=True
    )
    normed_dot = (guided * inverse + entry * inverse_dot).astype(jnp.bfloat16)
    adapted(normed_dot, weights_ref, down_ref, up_ref, dots)
    primal = [primal_ref.at[i] for i in range(3)] + [refs[3]]
    time_mix(frames, primal, dots)
    done_ref[here, :] = (
        guided_ref[...].astype(jnp.float32) + dot(dots[3][...], weights_ref[3])
    ).astype(jnp.bfloat16)

    @pl.when(step == pl.num_programs(0) - 1)
    def _():
        by_frame(done_ref, going_ref, frames)
        wait_all(start_all(departures(seat_ref, going_ref, out_pieces, piece_sems)))


IN_VMEM = pl.BlockSpec(memory_space=pltpu.VMEM)
IN_SMEM = pl.BlockSpec(memory_space=pltpu.SMEM)
ANYWHERE = pl.BlockSpec(memory_space=pl.ANY)


def time_call(kernel, passes, rows, width, limit=VMEM_LIMIT, **settings):
    return pl.pallas_call(
        kernel,
        compiler_params=pltpu.CompilerParams(vmem_limit_bytes=limit),
        cost_estimate=pl.CostEstimate(
            flops=int(12 * passes * rows * width * width),
            bytes_accessed=8 * width * width + 8 * rows * width,
            transcendentals=rows * LANES * width // HEAD_DIM,
        ),
        **settings,
    )


def student_rows(seat, shift, down, up, weights, pieces, frames):
    weights, layout = weights
    width = shift.shape[-1]
    rows, chunk = frames * ROW_TILE, BLOCK * frames
    vmem = lambda *shape: pltpu.VMEM(shape, jnp.bfloat16)
    fixed = lambda value: pl.BlockSpec(value.shape, lambda i: (0,) * value.ndim)
    return time_call(
        functools.partial(student_rows_kernel, layout, (len(weights), len(pieces))),
        0.6,
        rows,
        width,
        grid=(rows // chunk,),
        out_shape=[
            jax.ShapeDtypeStruct((rows, width), jnp.bfloat16),
            jax.ShapeDtypeStruct((3, rows, width), jnp.bfloat16),
        ],
        in_specs=[IN_SMEM, fixed(shift), fixed(down), fixed(up)]
        + [ANYWHERE] * (len(weights) + len(pieces)),
        out_specs=[
            pl.BlockSpec((chunk, width), lambda i: (i, 0)),
            pl.BlockSpec((3, chunk, width), lambda i: (0, i, 0)),
        ],
        scratch_shapes=[
            vmem(4, width, width),
            vmem(frames, ROW_TILE, width),
            vmem(rows, width),
            pltpu.SemaphoreType.DMA((len(layout),)),
            pltpu.SemaphoreType.DMA((2 * len(pieces),)),
        ],
    )(seat, shift, down, up, *weights, *pieces)


def student_mix(seat, shift, rows_in, primal, weights, frames, seats):
    weights, layout = weights
    rows, width = rows_in.shape
    chunk = BLOCK * frames
    vmem = lambda *shape: pltpu.VMEM(shape, jnp.bfloat16)
    piece = jax.ShapeDtypeStruct((seats // 2, rows // seats, width), jnp.bfloat16)
    return time_call(
        functools.partial(student_mix_kernel, layout, frames),
        0.6,
        rows,
        width,
        grid=(rows // chunk,),
        out_shape=[piece] * 2,
        in_specs=[
            IN_SMEM,
            pl.BlockSpec(shift.shape, lambda i: (0, 0)),
            pl.BlockSpec((chunk, width), lambda i: (i, 0)),
            pl.BlockSpec((3, chunk, width), lambda i: (0, i, 0)),
        ]
        + [ANYWHERE] * len(weights),
        out_specs=[ANYWHERE] * 2,
        scratch_shapes=[
            vmem(4, width, width),
            vmem(2, rows, width),
            vmem(chunk, width),
            pltpu.SemaphoreType.DMA((len(layout),)),
            pltpu.SemaphoreType.DMA((seats,)),
        ],
    )(seat, shift, rows_in, primal, *weights)


def teacher_velocity(seat, weights, pieces, frames):
    weights, layout = weights
    width = pieces[0].shape[-1]
    rows = frames * ROW_TILE
    vmem = lambda *shape: pltpu.VMEM(shape, jnp.bfloat16)
    return time_call(
        functools.partial(teacher_kernel, layout, (len(weights), len(pieces))),
        1,
        rows,
        width,
        out_shape=jax.ShapeDtypeStruct((rows, width), jnp.bfloat16),
        grid=(ROW_TILE // BLOCK,),
        in_specs=[IN_SMEM] + [ANYWHERE] * (len(weights) + len(pieces)),
        out_specs=pl.BlockSpec((BLOCK * frames, width), lambda i: (i, 0)),
        scratch_shapes=[
            vmem(4, width, width),
            vmem(frames, ROW_TILE, width),
            vmem(rows, width),
        ]
        + [vmem(BLOCK * frames, width)] * 4
        + [
            pltpu.SemaphoreType.DMA((len(layout),)),
            pltpu.SemaphoreType.DMA((4 * len(pieces),)),
        ],
    )(seat, *weights, *pieces)


def student_tangent(
    seat, strength, shift, down, up, velocity, noisy, primal, weights, pieces, frames, seats
):
    weights, layout = weights
    first = len(pieces) > 1
    width = shift.shape[-1]
    rows = frames * ROW_TILE // 2
    piece = jax.ShapeDtypeStruct((rows // seats, width), jnp.bfloat16)
    vmem = lambda *shape: pltpu.VMEM(shape, jnp.bfloat16)
    chunk = BLOCK * frames
    steps = rows // chunk
    part = 0 if first else steps
    half = pl.BlockSpec((chunk, width), lambda i: (part + i, 0))
    halves = pl.BlockSpec((3, chunk, width), lambda i: (0, part + i, 0))
    fixed = lambda value: pl.BlockSpec(value.shape, lambda i: (0,) * value.ndim)
    other = jax.ShapeDtypeStruct((rows, width), jnp.bfloat16)
    return time_call(
        functools.partial(tangent_kernel, layout, (len(weights), len(pieces), seats)),
        1,
        rows,
        width,
        TANGENT_VMEM_LIMIT,
        grid=(steps,),
        out_shape=[piece] * seats + [other] * first,
        in_specs=[IN_SMEM] * 2
        + [fixed(shift), fixed(down), fixed(up), half, half, halves]
        + [ANYWHERE] * len(weights)
        + ([ANYWHERE] * len(pieces) if first else [pl.BlockSpec((chunk, width), lambda i: (i, 0))]),
        out_specs=[ANYWHERE] * seats + [fixed(other)] * first,
        scratch_shapes=[vmem(frames, ROW_TILE, width), vmem(2 * rows, width)] * first
        + [vmem(4, width, width), vmem(rows, width), vmem(rows, width)]
        + [vmem(chunk, width)] * 9
        + [
            pltpu.SemaphoreType.DMA((len(layout),)),
            pltpu.SemaphoreType.DMA((4 * max(4, seats),)),
        ],
    )(seat, strength, shift, down, up, velocity, noisy, primal, *weights, *pieces)


def place_kernel(count, seat_ref, *rest):
    result_ref = rest[-1]
    frames, _, width = result_ref.shape
    for index in range(count):
        if len(rest[0].shape) > 2:
            parts = [rest[index // 2][index % 2].astype(jnp.float32)]
        else:
            parts = [piece[...].astype(jnp.float32) for piece in rest[index:-1:count]]
        parts = [part.reshape(frames, -1, width) for part in parts]
        start = pl.multiple_of((seat_ref[1] ^ index) * ROW_TILE, ROW_TILE)
        result_ref[:, pl.ds(start, ROW_TILE), :] = jnp.concatenate(parts, axis=1).astype(
            jnp.bfloat16
        )


def placed(seat, pieces, seats, frames):
    width = pieces[0].shape[-1]
    steps = max(1, frames // 4)
    half = frames // steps

    def block(piece):
        lead, (rows, width) = piece.shape[:-2], piece.shape[-2:]
        return pl.BlockSpec((*lead, rows // steps, width), lambda f: (0,) * len(lead) + (f, 0))

    return pl.pallas_call(
        functools.partial(place_kernel, seats),
        out_shape=jax.ShapeDtypeStruct((frames, seats * ROW_TILE, width), jnp.bfloat16),
        grid=(steps,),
        in_specs=[IN_SMEM]
        + [block(piece) for piece in pieces],
        out_specs=pl.BlockSpec((half, seats * ROW_TILE, width), lambda f: (f, 0, 0)),
        compiler_params=pltpu.CompilerParams(vmem_limit_bytes=VMEM_LIMIT),
    )(seat, *pieces)


def flip(value, axis, mask):
    pairs = [(source, source ^ mask) for source in range(lax.axis_size(axis))]
    return lax.ppermute(value, axis, pairs)


def half_weights(qkv, out_weight, core):
    stacked = jnp.concatenate([jnp.swapaxes(qkv, 1, 2), out_weight[None]], axis=0)
    return lax.dynamic_slice_in_dim(stacked, core * 2, 2, axis=0)


def z_pair(value, across):
    other = flip(value, "seq", lax.axis_size("seq") // 4)
    return jnp.where(
        across % 2 == 0,
        jnp.concatenate([value, other], axis=1),
        jnp.concatenate([other, value], axis=1),
    )


def over_middle(near):
    step = lax.axis_size("seq") // 4
    pairs = [
        pair
        for low in range(step)
        for pair in ((step + low, 2 * step + low), (2 * step + low, step + low))
    ]
    return lax.ppermute(near, "seq", pairs)


def to_ends(inside, across):
    step = lax.axis_size("seq") // 4
    pairs = [
        pair
        for low in range(step)
        for pair in ((step + low, low), (2 * step + low, 3 * step + low))
    ]
    outside = lax.ppermute(inside, "seq", pairs)
    return jnp.where((across == 1) | (across == 2), inside, outside)


NEAR = ((0, 0, 0), (0, 0, 1), (1, 0, 0), (1, 0, 1))
FAR = ((0, 1, 0), (0, 1, 1), (1, 1, 0), (1, 1, 1))


def own_layout():
    return [(index, None, 0, place) for index, place in enumerate(NEAR + FAR)]


def other_core(pieces):
    swapped = []
    for piece in pieces:
        if swapped:
            piece, swapped[-1] = together(piece, swapped[-1])
        swapped.append(flip(piece, "clip", 1))
    return swapped


def send(pieces):
    return [pieces[0]] + [flip(piece, "seq", i) for i, piece in enumerate(pieces) if i > 0]


def together(*groups):
    return lax.optimization_barrier(groups)


def along_line(neighbours):
    pieces = [
        jnp.stack([given[line] for given in neighbours])
        for line in range(neighbours[0].shape[0])
    ]
    return [flip(piece, "seq", 2 * i) if i > 0 else piece for i, piece in enumerate(pieces)]


def over_both(value):
    size = lax.axis_size("cfg") * lax.axis_size("seq")
    pairs = [(d, d ^ (size // 2 + 1)) for d in range(size)]
    return lax.ppermute(value, ("cfg", "seq"), pairs)


def to_neighbours(kept, low, across, both):
    return [kept, flip(low, "seq", 1), flip(across, "cfg", 1), over_both(both)]


def on_device(
    clean,
    noise,
    timestep,
    guidance,
    condition_vector,
    empty_prompt_vector,
    timestep_direction,
    spatial_query_key_value,
    spatial_output_weight,
    temporal_query_key_value,
    temporal_output_weight,
    adapter_down_maps,
    adapter_up_maps,
):
    sides, seats = lax.axis_size("cfg"), lax.axis_size("seq")
    side, place, core = (lax.axis_index(a) for a in ("cfg", "seq", "clip"))
    frames = clean.shape[0] * seats
    width = clean.shape[2]
    seat = jnp.stack([side, place, core]).astype(jnp.int32)
    moved = timestep[0] * timestep_direction.astype(jnp.float32)
    cond_shift = (moved + condition_vector.astype(jnp.float32))[None]
    uncond_shift = (moved + empty_prompt_vector.astype(jnp.float32))[None]
    down = jnp.swapaxes(adapter_down_maps, 1, 2).reshape(-1, width)
    up = adapter_up_maps.reshape(-1, sides, 2, 2, seats // 4, HEAD_DIM)
    up = jnp.swapaxes(up, 3, 4).reshape(-1, width)

    noisy_lines = noisy_pieces(seat, timestep, clean, noise, seats)
    space_own = half_weights(spatial_query_key_value, spatial_output_weight, core)
    time_own = half_weights(temporal_query_key_value, temporal_output_weight, core)
    across = place // (seats // 4)

    space_near = z_pair(space_own, across)
    space_near, time_own = together(space_near, time_own)
    space_in = over_middle(space_near)
    space = [space_near, flip(space_near, "seq", 1), flip(space_near, "cfg", 1)]
    time_near = z_pair(time_own, across)
    space_other = other_core([space_near])
    space, space_other, space_in, time_near = together(space, space_other, space_in, time_near)

    space_far = to_ends(space_in, across)
    space_xy = flip(space[2], "seq", 1)
    time_in = over_middle(time_near)
    time_x = flip(time_near, "cfg", 1)
    space_other += other_core(space[1:])
    space += [space_xy, space_far]
    space, space_other, time_in, time_x, time_near, noisy_lines, down, up = together(
        space, space_other, time_in, time_x, time_near, noisy_lines, down, up
    )

    space_far_x = flip(space[4], "cfg", 1)
    space_far_y = flip(space[4], "seq", 1)
    time_far = to_ends(time_in, across)
    space_xy_other, time_near_other = other_core([space[3], time_near])
    space += [space_far_y, space_far_x]
    space_other += [space_xy_other]
    time_other = [time_near_other]
    middle = noisy_lines[2].shape[1] // 2
    noisy_2 = flip(noisy_lines[2][:, :middle], "seq", 4)
    space, space_other, time_other, time_far, time_near, time_x, noisy_lines, noisy_2 = together(
        space, space_other, time_other, time_far, time_near, time_x, noisy_lines, noisy_2
    )

    space_far_xy = flip(space[5], "cfg", 1)
    time_y = flip(time_near, "seq", 1)
    noisy_1 = flip(noisy_lines[1], "seq", 2)
    *space_far_other, time_x_other = other_core(space[4:] + [time_x])
    space.append(space_far_xy)
    space_other += space_far_other
    time_other += [time_x_other]
    space, space_other, time_x, time_y, time_far, time_near, time_other, noisy_came = together(
        space, space_other, time_x, time_y, time_far, time_near, time_other,
        [noisy_lines[0], noisy_1, *noisy_lines[2:]],
    )

    space_last, time_far_other, time_y_other = (
        flip(piece, "clip", 1) for piece in (space[7], time_far, time_y)
    )
    space_other += [space_last]
    time_other += [time_far_other, time_y_other]
    space, space_other, time_x, time_y, time_far, time_near, time_other, noisy_came = together(
        space, space_other, time_x, time_y, time_far, time_near, time_other, noisy_came
    )
    space_weights = (
        list(space) + list(space_other),
        [(index, None, index // 8, (NEAR + FAR)[index % 8]) for index in range(16)],
    )
    cond, uncond = [
        functools.partial(
            spatial_layer, seat, timestep, clean, noise, shift, limit,
            frames=clean.shape[0] // sides, seats=seats,
        )
        for shift, limit in (
            (cond_shift, SPACE_VMEM_LIMIT), (uncond_shift, FULL_VMEM_LIMIT)
        )
    ]
    time_xy = flip(time_y, "cfg", 1)
    time_far_x = flip(time_far, "cfg", 1)
    time_far_y = flip(time_far, "seq", 1)
    noisy_2 = [noisy_2, flip(noisy_came[2][:, middle:], "seq", 4)]
    noisy_came = list(noisy_came[:2]) + [
        jnp.concatenate(noisy_2, axis=1), flip(noisy_came[3], "seq", 6)
    ]
    cond = cond(weights=space_weights)
    cond, time_xy, time_far_x, time_far_y, noisy_came = together(
        cond, time_xy, time_far_x, time_far_y, noisy_came
    )
    time_late = [flip(piece, "clip", 1) for piece in (time_xy, time_far_y, time_far_x)]
    half = len(noisy_came) // 2
    noisy_low = jnp.stack([line[1] for line in noisy_came[:half]])
    noisy_last = jnp.stack([line[1] for line in noisy_came[half:]])
    cond, time_far_y, time_late, noisy_low, noisy_last = together(
        cond, time_far_y, time_late, noisy_low, noisy_last
    )
    uncond = uncond(weights=space_weights)
    time_far_xy = flip(time_far_y, "cfg", 1)
    noisy_low = flip(noisy_low, "seq", 1)
    cond, uncond, time_far_xy, noisy_low, noisy_last = together(
        to_neighbours(*cond), uncond, time_far_xy, noisy_low, noisy_last
    )
    noisy_last = flip(noisy_last, "seq", 1)
    lines = [jnp.stack([given[line] for given in cond]) for line in range(seats // 2)]
    far_lines = [flip(lines[i], "seq", 2 * i) for i in range(2, seats // 2)]
    time_last = flip(time_far_xy, "clip", 1)
    uncond, time_last, noisy_last = together(uncond, time_last, noisy_last)
    time_weights = (
        [time_near, time_y, time_x, time_xy, time_far, time_far_y, time_far_x, time_far_xy]
        + list(time_other) + list(time_late) + [time_last],
        [(index, None, 0, at) for index, at in enumerate(NEAR + FAR)]
        + [
            (8 + index, None, 1, at)
            for index, at in enumerate(
                [NEAR[0], NEAR[2], FAR[0], NEAR[1], NEAR[3], FAR[1], FAR[2], FAR[3]]
            )
        ],
    )
    noisy_in = list(noisy_came) + [noisy_low, noisy_last]
    kept, low, across, both = uncond
    low, across, both = flip(low, "seq", 1), flip(across, "cfg", 1), over_both(both)
    rows, primal = student_rows(seat, cond_shift, down, up, time_weights, noisy_in, frames)
    rows, primal, low, across, both, lines = together(rows, primal, low, across, both, lines)
    near_line = flip(lines[1], "seq", 2)
    uncond = [
        jnp.stack([given[line] for given in (kept, low, across, both)])
        for line in range(seats // 2)
    ]
    uncond_last = flip(uncond[-1], "seq", seats - 2)
    student_kept, student_low = student_mix(
        seat, cond_shift, rows, primal, time_weights, frames, seats
    )
    cond = [lines[0], near_line, *far_lines]
    student_kept, student_low, cond, uncond = together(student_kept, student_low, cond, uncond)
    uncond = [
        flip(line, "seq", 2 * index) if index > 0 else line
        for index, line in enumerate(uncond[:-1])
    ] + [uncond_last]
    velocity = teacher_velocity(seat, time_weights, cond, frames)
    student_low, velocity, uncond = together(flip(student_low, "seq", 1), velocity, uncond)
    student_back = along_line([student_kept, student_low])
    tangent = functools.partial(
        student_tangent, seat, guidance, cond_shift, down, up, velocity, rows, primal,
        time_weights, frames=frames, seats=seats,
    )
    *tangent_pieces, other = tangent(uncond)
    student_back, other, tangent_pieces = together(student_back, other, tangent_pieces)
    tangent_back = send(tangent_pieces)
    rest, tangent_back = together(tangent([other]), tangent_back)
    tangent_back = list(tangent_back) + send(rest)
    here = clean.shape[0]
    return placed(seat, student_back, seats, here), placed(seat, tangent_back, seats, here)


def fits(mesh, frames, positions, width):
    sides, seats = mesh.shape["cfg"], mesh.shape["seq"]
    groups = sides * seats
    return (
        sides == 2
        and mesh.shape["clip"] == 2
        and seats == 4 * sides
        and frames % (groups * ROW_TILE // 4) == 0
        and positions == groups * ROW_TILE
        and 2 * frames == LANES
        and width % LANES == 0
        and width == groups * HEAD_DIM
    )

def solution(mesh):
    specs = dict(
        mesh=mesh,
        in_specs=(
            P(("clip", "seq"), None, None),
            P(("clip", "seq"), None, None),
            P("clip"),
            P("clip"),
            P("clip"),
            P(),
            P(),
            P(None, None, ("cfg", "seq")),
            P(("cfg", "seq"), None),
            P(None, None, ("cfg", "seq")),
            P(("cfg", "seq"), None),
            P(),
            P(),
        ),
        out_specs=(P(("clip", "seq"), "cfg", None), P(("clip", "seq"), "cfg", None)),
        check_vma=False,
    )

    def whole(clean, *rest):
        frames = clean.shape[0] // mesh.shape["clip"]
        fast = fits(mesh, frames, clean.shape[1], clean.shape[2])
        return jax.shard_map(on_device if fast else plain_on_device, **specs)(clean, *rest)

    return whole
```
